32 devices in a mesh: groups: 2 (over y), space: 4 (over z), test: 4 (over x, core).
Axes of the slice: x: 2, y: 2, z: 4, core: 2. Of those that a mesh axis runs over, the one named last changes fastest.
Arguments:
- log_k: bfloat16 [384, 288, 128], P(('groups', 'space')), parts along dimension 0, may hold values from -1.5 to 1.5
- heads: bfloat16 [4, 384, 288, 128], P('test', ('groups', 'space')), parts along dimension 1, may hold values from -6 to 6
- warm_adjoint: bfloat16 [4, 384, 288, 128], P('test', ('groups', 'space')), parts along dimension 1, may hold values from -6 to 6
- obs_columns: int32 [4, 128], P('test', 'groups'), parts along dimension 1, may hold values from 0 to 55295
- obs_residuals: float32 [4, 128, 128], P('test', 'groups'), parts along dimension 1, may hold values from -18 to 18
- well_columns: int32 [8], P(('groups', 'test')), parts along dimension 0, may hold values from 0 to 55295
Outputs:
- prior_gradient: float32 [384, 288, 128], P(('groups', 'space'), 'test'), parts along dimension 0
The draws below stay inside these ranges and needn't reach their ends.
There are 2 independent parts, one for each index of `groups`. The reference program is written for one: setup_inputs(seed, part) draws one part's arguments, and reference() takes and returns one part's arrays. A program takes and returns all parts, laid end to end along the dimension named above; each array names one. Nothing has to cross between parts.
Inputs may be any that keep to these rules, and one draw needn't show every extreme that they name: `obs_columns`: x * 288 + y of the borehole's cell column. `well_columns`: x * 288 + y of the well's cell column.
All inputs are finite; a program needn't handle non-finite values.
Results may differ from the reference program's by a relative error of at most 0.0003.
Values may be sent and summed in bfloat16 or wider, within the bound.
No kernel may reach another device: no remote copies, remote signals or barrier semaphores. Data moves between devices by JAX's collectives and lax.ppermute only.
A program may use at most 128 MiB of HBM per device.

```python
import jax
import jax.numpy as jnp

NX = 192
NY = 288
NZ = 128
OBS = 64
ITERS = 2
TESTS = 4


def plant(array, key, least, largest):
    index_at = [jax.random.randint(jax.random.fold_in(key, axis), (), 0, length) for axis, length in enumerate(array.shape)]
    widest = array.shape.index(max(array.shape))
    neighbour = index_at[:widest] + [(index_at[widest] + 1) % array.shape[widest]] + index_at[widest + 1:]
    return array.at[tuple(index_at)].set(least).at[tuple(neighbour)].set(largest)


def block_scale(key, shape, pieces, least, top_value):
    def one(position, shards_of):
        steps = jax.random.uniform(jax.random.fold_in(jax.random.fold_in(key, 6), position), (shards_of,), jnp.float32, least / len(pieces), top_value / len(pieces))
        return jnp.repeat(jnp.exp(steps), shape[position] // shards_of).reshape((-1,) + (1,) * (len(shape) - position - 1))

    level = one(*pieces[0])
    for cut in pieces[1:]:
        level = level * one(*cut)
    return level


def bell_draw(rng, shape, scale, bound, shards=(), held_as=jnp.bfloat16):
    entries = jax.random.normal(rng, shape, jnp.float32) * scale
    if len(shards) > 0:
        entries = block_scale(rng, shape, shards, -0.22, 0.18) * entries
    return jnp.clip(entries, min=-bound, max=bound).astype(held_as)


def setup_inputs(seed: int = 0, part: int = 0) -> dict:
    key_of = jax.random.split(jax.random.key(seed), 7)
    part_keys = jax.random.split(jax.random.fold_in(key_of[6], part), 7)
    return {
        "log_k": jnp.clip(jax.random.uniform(part_keys[0], (NX, NY, NZ), jnp.float32, -1.5, 1.5) * block_scale(part_keys[0], (NX, NY, NZ), ((0, 4),), -0.4, 0.0), -1.5, 1.5).astype(jnp.bfloat16),
        "heads": bell_draw(part_keys[1], (TESTS, NX, NY, NZ), 1.0, 6.0, ((0, 4), (1, 4))),
        "warm_adjoint": bell_draw(part_keys[2], (TESTS, NX, NY, NZ), 1.0, 6.0, ((0, 4), (1, 4))),
        "obs_columns": plant(jax.random.randint(part_keys[3], (TESTS, OBS), 0, NX * NY), jax.random.fold_in(part_keys[3], 1), 0, (NX * NY) - 1).astype(jnp.int32),
        "obs_residuals": bell_draw(part_keys[4], (TESTS, OBS, NZ), 3.0, 18.0, ((0, 4),), jnp.float32),
        "well_columns": plant(jax.random.randint(part_keys[5], (TESTS,), 0, NX * NY), jax.random.fold_in(part_keys[5], 1), 0, (NX * NY) - 1).astype(jnp.int32),
    }


prior_gain = 5.0
range_squared = 4.0


def neighbours(padded):
    return [padded[2:, 1:-1, 1:-1], padded[:-2, 1:-1, 1:-1], padded[1:-1, 2:, 1:-1],
            padded[1:-1, :-2, 1:-1], padded[1:-1, 1:-1, 2:], padded[1:-1, 1:-1, :-2]]


def operate(values, padded, conduct):
    summed = jnp.zeros_like(values)
    for face_k, beside in zip(conduct, neighbours(padded)):
        summed = summed + face_k * (values - beside)
    return summed


def kappa_of(indices, length):
    return 4.0 * jnp.sin(jnp.pi * indices / length) ** 2


def reference(log_k, heads, warm_adjoint, obs_columns, obs_residuals, well_columns):
    logk_val = log_k.astype(jnp.float32)
    conduct = [jnp.exp(0.5 * (logk_val + beside)) for beside in neighbours(jnp.pad(logk_val, 1))]
    summed = jnp.zeros((NX, NY, NZ), jnp.float32)
    column_ids = jnp.arange(NX * NY, dtype=jnp.int32).reshape(NX, NY)
    for test_id in range(TESTS):
        source = jnp.zeros((NX * NY, NZ), jnp.float32).at[obs_columns[test_id]].add(obs_residuals[test_id])
        source = source.reshape(NX, NY, NZ)
        adjoint = warm_adjoint[test_id].astype(jnp.float32)
        residual = source - operate(adjoint, jnp.pad(adjoint, 1), conduct)
        direction = residual
        norm_now = jnp.sum(residual * residual)
        for iteration in range(ITERS):
            applied = operate(direction, jnp.pad(direction, 1), conduct)
            step_length = norm_now / jnp.sum(direction * applied)
            adjoint = adjoint + step_length * direction
            if iteration + 1 < ITERS:
                residual = residual - step_length * applied
                norm_next = jnp.sum(residual * residual)
                direction = residual + (norm_next / norm_now) * direction
                norm_now = norm_next
        head_val = heads[test_id].astype(jnp.float32)
        misfit_term = jnp.zeros_like(adjoint)
        for face_k, lam_side, head_side in zip(conduct, neighbours(jnp.pad(adjoint, 1)), neighbours(jnp.pad(head_val, 1))):
            misfit_term = misfit_term + face_k * (adjoint - lam_side) * (head_val - head_side)
        keep_mask = (column_ids != well_columns[test_id]).astype(jnp.float32)
        summed = summed + (-0.5 * misfit_term * keep_mask[:, :, None])
    kappa_x = kappa_of(jnp.arange(NX).astype(jnp.float32), NX)
    kappa_y = kappa_of(jnp.arange(NY).astype(jnp.float32), NY)
    kappa_z = kappa_of(jnp.arange(NZ).astype(jnp.float32), NZ)
    spectrum = prior_gain / (1.0 + range_squared * (kappa_x[:, None, None] + kappa_y[None, :, None] + kappa_z[None, None, :])) ** 2
    result = jnp.real(jnp.fft.ifftn(jnp.fft.fftn(summed) * spectrum))
    return result.astype(jnp.float32)
```

```python
import functools

import jax
import jax.numpy as jnp
import ml_dtypes
import numpy as np
from jax import lax
from jax.experimental import pallas as pl
from jax.experimental.pallas import tpu as pltpu
from jax.sharding import PartitionSpec as P

prior_gain = 5.0
range_squared = 4.0

HALO = 3
PAD = 8
F32 = jnp.float32
BF16 = jnp.bfloat16
VMEM_LIMIT = 60 * 1024 * 1024

SMEM_SPEC = pl.BlockSpec(memory_space=pltpu.SMEM)
VMEM_SPEC = pl.BlockSpec(memory_space=pltpu.VMEM)
ANY_SPEC = pl.BlockSpec(memory_space=pl.ANY)


def cas(length):
    index = np.arange(length)
    angle = 2.0 * np.pi * (index[:, None] * index[None, :] % length) / length
    return np.cos(angle) + np.sin(angle)


def halves(table):
    table = np.asarray(table, np.float32)
    high = table.astype(ml_dtypes.bfloat16)
    low = (table - high.astype(np.float32)).astype(ml_dtypes.bfloat16)
    return high, low


def kappa(length):
    return 4.0 * np.sin(np.pi * np.arange(length) / length) ** 2


def split(value):
    high = value.astype(BF16)
    low = (value - high.astype(F32)).astype(BF16)
    return high, low


def dot(left, right):
    return lax.dot_general(left, right, (((1,), (0,)), ((), ())), preferred_element_type=F32)


def dot3(left, right):
    return dot(left[0], right[0]) + (dot(left[0], right[1]) + dot(left[1], right[0]))


def block_rows(count):
    for rows in (48, 32, 16):
        if count % rows == 0:
            return rows
    return count


def lane_index(shape):
    return lax.broadcasted_iota(jnp.int32, shape, 1)


def window(ref, start, rows):
    return ref.at[pl.ds(pl.multiple_of(start - PAD, 8), rows + 2 * PAD)]


def neighbour_sum(ref, start, rows, plane, fill):
    near = window(ref, start, rows)
    here = near[PAD : PAD + rows]
    lanes = lane_index(here.shape)
    depth = here.shape[1]
    up = jnp.where(lanes == depth - 1, fill, pltpu.roll(here, depth - 1, 1))
    down = jnp.where(lanes == 0, fill, pltpu.roll(here, 1, 1))
    along = ref[pl.ds(pl.multiple_of(start - plane, 8), rows)] + ref[pl.ds(pl.multiple_of(start + plane, 8), rows)]
    across = near[PAD - 1 : PAD - 1 + rows] + near[PAD + 1 : PAD + 1 + rows]
    return along + across + (up + down), here


def fold(value):
    return jnp.sum(value.reshape(-1, 8, value.shape[1]), axis=0)


def moments_kernel(
    rows, ny, count_x,
    meta, columns, residuals, lk_low, lk, lk_high, w_low, w, w_high,
    v_out, q_out, mom_out,
    lk_buf, w_buf, e_ref, u_ref, v_ref, s_ref, r_ref, sems,
):
    depth = lk.shape[2]
    plane = ny + PAD
    planes = rows + 2 * HALO
    size = block_rows(ny)
    blocks = [i * size for i in range(ny // size)]
    first_row = meta[0]

    copies = []
    for index, (low, mid, high, buf) in enumerate(
        ((lk_low, lk, lk_high, lk_buf), (w_low, w, w_high, w_buf))
    ):
        copies += [
            pltpu.make_async_copy(low, buf.at[pl.ds(0, HALO)], sems.at[3 * index]),
            pltpu.make_async_copy(mid, buf.at[pl.ds(HALO, rows)], sems.at[3 * index + 1]),
            pltpu.make_async_copy(high, buf.at[pl.ds(HALO + rows, HALO)], sems.at[3 * index + 2]),
        ]
    for copy in copies:
        copy.start()

    ones = jnp.ones((PAD, depth), F32)
    zeros = jnp.zeros((PAD, depth), F32)

    def clear(p, carry):
        at = pl.ds(pl.multiple_of(p * plane, 8), PAD)
        e_ref[at] = ones
        u_ref[at] = zeros
        v_ref[at] = zeros
        return carry

    lax.fori_loop(0, planes, clear, 0)
    last = pl.ds(planes * plane, PAD)
    e_ref[last] = ones
    u_ref[last] = zeros
    v_ref[last] = zeros

    for copy in copies:
        copy.wait()

    def scale(p, carry):
        base = p * plane + PAD
        for b in blocks:
            e = jnp.exp(0.5 * lk_buf[p, b : b + size].astype(F32))
            at = pl.ds(pl.multiple_of(base + b, 8), size)
            e_ref[at] = e
            u_ref[at] = e * w_buf[p, b : b + size].astype(F32)
        return carry

    lax.fori_loop(0, planes, scale, 0)

    def inside(p):
        row = first_row + p - HALO
        return jnp.where((row >= 0) & (row < count_x), 1.0, 0.0).astype(F32)

    def residual(p, carry):
        base = p * plane + PAD
        valid = inside(p)
        for b in blocks:
            start = base + b
            at = pl.ds(pl.multiple_of(start, 8), size)
            flat = pl.ds(pl.multiple_of(p * ny + b, 8), size)
            s, e = neighbour_sum(e_ref, start, size, plane, 1.0)
            n, u = neighbour_sum(u_ref, start, size, plane, 0.0)
            r = (e * n - s * u) * valid
            s_ref[flat] = s
            r_ref[flat] = r
            v_ref[at] = e * r
        return carry

    lax.fori_loop(1, planes - 1, residual, 0)

    def plant(o, carry):
        column = columns[o]
        row = lax.div(column, ny)
        y = column - row * ny
        p = row - first_row + HALO

        @pl.when((p >= 1) & (p < planes - 1))
        def _():
            at = pl.ds(p * plane + PAD + y, 1)
            flat = pl.ds(p * ny + y, 1)
            added = residuals[pl.ds(o, 1)]
            r_ref[flat] = r_ref[flat] + added
            v_ref[at] = v_ref[at] + e_ref[at] * added

        return carry

    lax.fori_loop(0, columns.shape[0], plant, 0)
    extent = (rows + 2) * plane
    v_copy = pltpu.make_async_copy(v_ref.at[pl.ds(2 * plane, extent)], v_out, sems.at[6])
    v_copy.start()

    def image(p, sums, valid, summed):
        m0, m1, m2 = sums
        base = p * plane + PAD
        for b in blocks:
            start = base + b
            at = pl.ds(pl.multiple_of(start, 8), size)
            flat = pl.ds(pl.multiple_of(p * ny + b, 8), size)
            n, v = neighbour_sum(v_ref, start, size, plane, 0.0)
            e = e_ref[at]
            y = s_ref[flat] * v - e * n
            if valid is not None:
                y = y * valid
            u_ref[at] = e * y
            if summed:
                r = r_ref[flat]
                m0 = m0 + fold(r * r)
                m1 = m1 + fold(r * y)
                m2 = m2 + fold(y * y)
                r_ref[flat] = y
        return m0, m1, m2

    zero = jnp.zeros((8, depth), F32)
    sums = (zero, zero, zero)
    image(HALO - 1, sums, inside(HALO - 1), False)
    image(HALO + rows, sums, inside(HALO + rows), False)
    m0, m1, m2 = lax.fori_loop(HALO, HALO + rows, lambda p, c: image(p, c, None, True), sums)
    q_copy = pltpu.make_async_copy(u_ref.at[pl.ds(2 * plane, extent)], q_out, sems.at[7])
    q_copy.start()

    def second(p, m3):
        base = p * plane + PAD
        for b in blocks:
            start = base + b
            at = pl.ds(pl.multiple_of(start, 8), size)
            flat = pl.ds(pl.multiple_of(p * ny + b, 8), size)
            n, q = neighbour_sum(u_ref, start, size, plane, 0.0)
            m3 = m3 + fold(r_ref[flat] * (s_ref[flat] * q - e_ref[at] * n))
        return m3

    m3 = lax.fori_loop(HALO, HALO + rows, second, zero)
    for k, m in enumerate((m0, m1, m2, m3)):
        mom_out[k] = jnp.sum(m)
    v_copy.wait()
    q_copy.wait()


def moments(meta, columns, residuals, lk_parts, w_parts, count_x):
    rows, ny, depth = lk_parts[1].shape
    plane = ny + PAD
    planes = rows + 2 * HALO
    field = pltpu.VMEM((planes * plane + PAD, depth), F32)
    flat = pltpu.VMEM((planes * ny, depth), F32)
    out = jax.ShapeDtypeStruct(((rows + 2) * plane, depth), F32)
    cells = planes * ny * depth
    return pl.pallas_call(
        functools.partial(moments_kernel, rows, ny, count_x),
        out_shape=(out, out, jax.ShapeDtypeStruct((4,), F32)),
        in_specs=[SMEM_SPEC, SMEM_SPEC, VMEM_SPEC] + [ANY_SPEC] * 6,
        out_specs=(ANY_SPEC, ANY_SPEC, SMEM_SPEC),
        scratch_shapes=[
            pltpu.VMEM((planes, ny, depth), BF16),
            pltpu.VMEM((planes, ny, depth), BF16),
            field, field, field, flat, flat,
            pltpu.SemaphoreType.DMA((8,)),
        ],
        compiler_params=pltpu.CompilerParams(vmem_limit_bytes=VMEM_LIMIT),
        cost_estimate=pl.CostEstimate(flops=60 * cells, bytes_accessed=12 * cells, transcendentals=cells),
        name="moments",
    )(meta, columns, residuals, *lk_parts, *w_parts)


def misfit_kernel(
    rows, ny, first, size, parts, tests,
    meta, coeffs, lk_low, lk, lk_high, w_low, w, w_high, h_low, h, h_high, v, q, bd_high, bd_low,
    mine_out, other_out,
    lk_buf, w_buf, h_buf, v_buf, q_buf, e_ref, a_ref, h_ref, x_ref, t_high, t_low, f_ref, sems,
):
    depth = lk.shape[2]
    length = rows // parts
    edge = 16
    low = edge if first > 0 else 0
    high = edge if first + size < ny else 0
    wide = size + 2 * edge
    from_row, span = first - low, low + size + high
    v_low = PAD
    v_span = PAD + size + (PAD if high else 0)
    block = block_rows(size)
    blocks = [i * block for i in range(size // block)]
    first_row, well = meta[0], meta[1]

    copies = []
    sem = iter(range(5 * parts + 6 + tests))

    def start(source, target, chunk):
        copy = pltpu.make_async_copy(source, target, sems.at[next(sem)])
        copy.start()
        copies[chunk].append(copy)

    for chunk in range(parts):
        copies.append([])
        begin = chunk * length
        for lo, mid, hi, buf in (
            (lk_low, lk, lk_high, lk_buf),
            (w_low, w, w_high, w_buf),
            (h_low, h, h_high, h_buf),
        ):
            ys, yt = pl.ds(from_row, span), pl.ds(edge - low, span)
            if chunk == 0:
                start(lo.at[pl.ds(lo.shape[0] - 1, 1), ys], buf.at[pl.ds(0, 1), yt], chunk)
                start(mid.at[pl.ds(0, length + (1 if parts > 1 else 0)), ys], buf.at[pl.ds(1, length + (1 if parts > 1 else 0)), yt], chunk)
            else:
                more = 1 if chunk < parts - 1 else 0
                start(mid.at[pl.ds(begin + 1, length - 1 + more), ys], buf.at[pl.ds(begin + 2, length - 1 + more), yt], chunk)
            if chunk == parts - 1:
                start(hi.at[pl.ds(0, 1), ys], buf.at[pl.ds(rows + 1, 1), yt], chunk)
        for source, buf in ((v, v_buf), (q, q_buf)):
            zs = pl.ds(first, v_span)
            lo_p = 0 if chunk == 0 else begin + 2
            hi_p = begin + length + 2
            start(source.at[pl.ds(lo_p, hi_p - lo_p), zs], buf.at[pl.ds(lo_p, hi_p - lo_p), pl.ds(0, v_span)], chunk)

    c0, c1 = coeffs[0], coeffs[1]
    slot_rows = wide
    ones = jnp.ones((PAD, depth), F32)
    zeros = jnp.zeros((PAD, depth), F32)
    for s in range(4):
        base = s * slot_rows
        for at in (pl.ds(base + edge - PAD, PAD), pl.ds(base + edge + size, PAD)):
            e_ref[at] = ones
            a_ref[at] = zeros
            h_ref[at] = zeros

    def slot(p):
        return lax.rem(p, 4) * slot_rows

    spans = [(edge + b, block) for b in blocks]
    if low:
        spans.insert(0, (0, edge))
    if high:
        spans.append((edge + size, edge))

    def prepare(p):
        base = slot(p)
        for at, count in spans:
            e = jnp.exp(0.5 * lk_buf[p, at : at + count].astype(F32))
            a = e * w_buf[p, at : at + count].astype(F32)
            hh = h_buf[p, at : at + count].astype(F32)
            if at == 0:
                e, a, hh = e[8:], a[8:], hh[8:]
                at, count = 8, 8
            elif at == edge + size:
                e, a, hh = e[:8], a[:8], hh[:8]
                count = 8
            zat = at - edge + PAD
            a = a + c0 * v_buf[p, zat : zat + count] + c1 * q_buf[p, zat : zat + count]
            to = pl.ds(pl.multiple_of(base + at, 8), count)
            e_ref[to] = e
            a_ref[to] = a
            h_ref[to] = hh

    def along(p):
        here, there = slot(p), slot(p + 1)
        for b in blocks:
            at = pl.ds(pl.multiple_of(here + edge + b, 8), block)
            to = pl.ds(pl.multiple_of(there + edge + b, 8), block)
            x_ref[b : b + block] = (e_ref[to] * a_ref[at] - e_ref[at] * a_ref[to]) * (h_ref[at] - h_ref[to])

    def centre(p, x, part):
        here, there = slot(p), slot(p + 1)
        column = (first_row + x) * ny + first
        for b in blocks:
            begin = here + edge + b
            to = pl.ds(pl.multiple_of(there + edge + b, 8), block)
            e_near, a_near, h_near = (window(ref, begin, block) for ref in (e_ref, a_ref, h_ref))
            mid = slice(PAD, PAD + block)
            e, a, hh = e_near[mid], a_near[mid], h_near[mid]
            en, an, hn = e_ref[to], a_ref[to], h_ref[to]
            before = x_ref[b : b + block]
            after = (en * a - e * an) * (hh - hn)
            x_ref[b : b + block] = after
            total = before + after
            for shift in (-1, 1):
                at = slice(PAD + shift, PAD + shift + block)
                en, an, hn = e_near[at], a_near[at], h_near[at]
                total = total + (en * a - e * an) * (hh - hn)
            lanes = lane_index(e.shape)
            end = lanes == depth - 1
            en = jnp.where(end, 1.0, pltpu.roll(e, depth - 1, 1))
            an = jnp.where(end, 0.0, pltpu.roll(a, depth - 1, 1))
            hn = jnp.where(end, 0.0, pltpu.roll(hh, depth - 1, 1))
            up = (en * a - e * an) * (hh - hn)
            down = jnp.where(lanes == 0, a * hh, pltpu.roll(up, 1, 1))
            total = -0.5 * (total + up + down)
            row = lax.broadcasted_iota(jnp.int32, e.shape, 0) + (column + b)
            total = jnp.where(row == well, 0.0, total)
            high_part, low_part = split(total)
            to = pl.ds(pl.multiple_of((x - part * length) * size + b, 16), block)
            t_high[to, part * depth : (part + 1) * depth] = high_part
            t_low[to, part * depth : (part + 1) * depth] = low_part

    for part in range(parts):
        for copy in copies[part]:
            copy.wait()
        if part == 0:
            prepare(0)
            prepare(1)
            along(0)

        def step(x, carry):
            prepare(x + 2)
            centre(x + 1, x, part)
            return carry

        lax.fori_loop(part * length, (part + 1) * length, step, 0)

    chunk = size
    lanes_out = f_ref.shape[2]

    def transform(i, carry):
        at = pl.ds(pl.multiple_of(i * chunk, 16), chunk)
        value = dot3((t_high[at], t_low[at]), (bd_high[...], bd_low[...]))
        for t in range(tests):
            f_ref[t, at] = value[:, t * lanes_out : (t + 1) * lanes_out]
        return carry

    lax.fori_loop(0, length, transform, 0)
    chips = tests // 2
    outs = []
    for k in range(chips):
        outs.append(pltpu.make_async_copy(f_ref.at[meta[4 + k]], mine_out.at[k], sems.at[next(sem)]))
        outs.append(pltpu.make_async_copy(f_ref.at[meta[4 + chips + k]], other_out.at[k], sems.at[next(sem)]))
    for copy in outs:
        copy.start()
    for copy in outs:
        copy.wait()


def misfit(meta, coeffs, lk_parts, w_parts, h_parts, v, q, tables, first, size, parts, tests):
    rows, ny, depth = lk_parts[1].shape
    length = rows // parts
    lanes = tables[0].shape[1] // tests
    plane = ny + PAD
    v, q = (a.reshape(rows + 2, plane, depth) for a in (v, q))
    wide = size + 32
    out = jax.ShapeDtypeStruct((tests // 2, length * size, lanes), F32)
    half = pltpu.VMEM((rows + 2, wide, depth), BF16)
    full = pltpu.VMEM((rows + 2, size + 2 * PAD, depth), F32)
    ring = pltpu.VMEM((4 * wide, depth), F32)
    cells = rows * size * depth
    return pl.pallas_call(
        functools.partial(misfit_kernel, rows, ny, first, size, parts, tests),
        out_shape=(out, out),
        in_specs=[SMEM_SPEC, SMEM_SPEC] + [ANY_SPEC] * 11 + [VMEM_SPEC] * 2,
        out_specs=(ANY_SPEC, ANY_SPEC),
        scratch_shapes=[
            half, half, half, full, full, ring, ring, ring,
            pltpu.VMEM((size, depth), F32),
            pltpu.VMEM((length * size, parts * depth), BF16),
            pltpu.VMEM((length * size, parts * depth), BF16),
            pltpu.VMEM((tests, length * size, lanes), F32),
            pltpu.SemaphoreType.DMA((5 * parts + 6 + tests,)),
        ],
        compiler_params=pltpu.CompilerParams(vmem_limit_bytes=VMEM_LIMIT),
        cost_estimate=pl.CostEstimate(flops=60 * cells, bytes_accessed=18 * cells, transcendentals=cells),
        name="misfit",
    )(meta, coeffs, *lk_parts, *w_parts, *h_parts, v, q, *tables)


def power(value, exponent):
    result = None
    while exponent:
        if exponent & 1:
            result = value if result is None else result * value
        exponent >>= 1
        if exponent:
            value = value * value
    return result


def ratio_of(across, deep):
    half = (1.0 + range_squared * (across + deep) + 2.0 * range_squared) / (2.0 * range_squared)
    return 1.0 / (half + jnp.sqrt(half * half - 1.0))


def by_block(values, lanes, width):
    result = values[-1]
    for j in range(len(values) - 2, -1, -1):
        result = jnp.where(lanes < (j + 1) * width, values[j], result)
    return result


def powers(value, length, count):
    step = power(value, length)
    result = [jnp.ones_like(value)]
    for _ in range(count - 1):
        result.append(result[-1] * step)
    return result


def everywhere(value, width):
    lanes = value.shape[1]
    shift = width
    while shift < lanes:
        value = value + pltpu.roll(value, shift, 1)
        shift *= 2
    return value


def solve_kernel(length, parts, width, chunks, meta, across, deep, *refs):
    groups = refs[:chunks]
    tables = refs[chunks : 3 * chunks]
    local_out, state_out, packed_out, h_ref = refs[3 * chunks :]
    ny, lanes_count = across.shape
    size = groups[0].shape[0] // length
    pair = 2 if length % 2 == 0 else 1
    for g in range(0, length, pair):
        total = None
        for c in range(chunks):
            value = jnp.concatenate([groups[c][(g + k) * size : (g + k + 1) * size] for k in range(pair)], axis=1)
            product = dot3((tables[2 * c][...], tables[2 * c + 1][...]), split(value))
            total = product if total is None else total + product
        for k in range(pair):
            h_ref[g + k] = total[:, k * lanes_count : (k + 1) * lanes_count]

    block = block_rows(ny)
    qz = deep[pl.ds(meta[2], 1)]

    def solve(i, carry):
        at = pl.ds(pl.multiple_of(i * block, 16), block)
        rho = ratio_of(across[at], qz)
        square = rho * rho
        tilt = (1.0 + square) / (1.0 - square)
        p1 = jnp.zeros_like(rho)
        p2 = jnp.zeros_like(rho)
        for x in range(length):
            p2 = rho * (p2 + p1)
            p1 = h_ref[x, at] + rho * p1
            local_out[x, at] = p2 + tilt * p1
        n1 = jnp.zeros_like(rho)
        n2 = jnp.zeros_like(rho)
        for x in range(length - 1, -1, -1):
            local_out[x, at] = local_out[x, at] + (n2 + tilt * n1)
            n1 = rho * (n1 + h_ref[x, at])
            n2 = rho * n2 + n1
        if parts == 1:
            for k, value in enumerate((p1, p2, n1, n2)):
                state_out[k, at] = jnp.zeros_like(rho)
                packed_out[k, at] = value
            return carry
        lanes = lane_index(rho.shape)
        steps = powers(rho, length, parts)
        zero = jnp.zeros_like(rho)
        into = [zero] * 4
        for s in range(1, parts):
            weight = jnp.where(lanes >= s * width, steps[s - 1], 0.0)
            far = float(length * (s - 1))
            one, two = (pltpu.roll(value, s * width, 1) for value in (p1, p2))
            into[0] = into[0] + weight * one
            into[1] = into[1] + weight * (two + far * one)
            weight = jnp.where(lanes < (parts - s) * width, steps[s - 1], 0.0)
            one, two = (pltpu.roll(value, lanes_count - s * width, 1) for value in (n1, n2))
            into[2] = into[2] + weight * one
            into[3] = into[3] + weight * (two + far * one)
        for k in range(4):
            state_out[k, at] = into[k]
        place = lanes // width
        weight = by_block(steps[::-1], lanes, width)
        far = ((parts - 1 - place) * length).astype(F32)
        d1 = everywhere(weight * p1, width)
        d2 = everywhere(weight * (p2 + far * p1), width)
        weight = by_block(steps, lanes, width)
        far = (place * length).astype(F32)
        e1 = everywhere(weight * n1, width)
        e2 = everywhere(weight * (n2 + far * n1), width)
        packed_out[at] = by_block([d1, d2, e1, e2], lanes, width)
        return carry

    lax.fori_loop(0, ny // block, solve, 0)


def solve(meta, across, deep, groups, tables, length, parts, width):
    ny, lanes = across.shape
    chunks = len(groups)
    packed = (ny, lanes) if parts == 4 else (4, ny, lanes)
    cells = length * ny * lanes
    return pl.pallas_call(
        functools.partial(solve_kernel, length, parts, width, chunks),
        out_shape=(
            jax.ShapeDtypeStruct((length, ny, lanes), F32),
            jax.ShapeDtypeStruct((4, ny, lanes), F32),
            jax.ShapeDtypeStruct(packed, F32),
        ),
        in_specs=[SMEM_SPEC] + [VMEM_SPEC] * (2 + 3 * chunks),
        out_specs=(VMEM_SPEC,) * 3,
        scratch_shapes=[pltpu.VMEM((length, ny, lanes), F32)],
        compiler_params=pltpu.CompilerParams(vmem_limit_bytes=VMEM_LIMIT),
        cost_estimate=pl.CostEstimate(flops=6 * cells * ny, bytes_accessed=16 * cells, transcendentals=0),
        name="solve",
    )(meta, across, deep, *groups, *tables)


def finish_kernel(
    length, parts, width, spaces, tests, scale,
    meta, across, deep, local, state, packed, c_high, c_low, out, v_ref, v_high, v_low,
):
    ny, lanes_count = across.shape
    block = block_rows(ny)
    qz = deep[pl.ds(meta[2], 1)]
    rank = meta[3]
    slab = length * parts

    def correct(i, carry):
        at = pl.ds(pl.multiple_of(i * block, 16), block)
        rho = ratio_of(across[at], qz)
        square = rho * rho
        tilt = (1.0 + square) / (1.0 - square)
        gain = rho / (2.0 * range_squared * 0.5 * (1.0 - square))
        gain = (prior_gain * scale) * gain * gain
        lanes = lane_index(rho.shape)
        step = power(rho, slab)
        weight = jnp.ones_like(rho)
        if parts > 1:
            near = far = jnp.zeros_like(rho)
            for k in range(1, spaces + 1):
                left = packed[lax.rem(rank + spaces - k, spaces), at]
                right = packed[lax.rem(rank + k, spaces), at]
                value = weight * jnp.where(lanes < 2 * width, left, right)
                near = near + value
                far = far + float(slab * (k - 1)) * value
                weight = weight * step

            def pick(value, s):
                return everywhere(jnp.where((lanes >= s * width) & (lanes < (s + 1) * width), value, 0.0), width)

            one, two, far_one = pick(near, 0), pick(near, 1), pick(far, 0)
            back_one, back_two, back_far = pick(near, 2), pick(near, 3), pick(far, 2)
        else:
            one = two = far_one = back_one = back_two = back_far = jnp.zeros_like(rho)
            for k in range(1, spaces + 1):
                left = lax.rem(rank + spaces - k, spaces)
                right = lax.rem(rank + k, spaces)
                first = weight * packed[left, 0, at]
                one = one + first
                two = two + weight * packed[left, 1, at]
                far_one = far_one + float(slab * (k - 1)) * first
                first = weight * packed[right, 2, at]
                back_one = back_one + first
                back_two = back_two + weight * packed[right, 3, at]
                back_far = back_far + float(slab * (k - 1)) * first
                weight = weight * step
        around = 1.0 / (1.0 - weight)
        again = float(slab * spaces) * weight * around * around
        two = around * (two + far_one) + again * one
        one = around * one
        back_two = around * (back_two + back_far) + again * back_one
        back_one = around * back_one
        if parts > 1:
            steps = powers(rho, length, parts)
            place = lanes // width
            weight = by_block(steps, lanes, width)
            two = weight * (two + (place * length).astype(F32) * one)
            one = weight * one
            weight = by_block(steps[::-1], lanes, width)
            back_two = weight * (back_two + ((parts - 1 - place) * length).astype(F32) * back_one)
            back_one = weight * back_one
        one = one + state[0, at]
        two = two + state[1, at]
        back_one = back_one + state[2, at]
        back_two = back_two + state[3, at]
        for x in range(length):
            two = rho * (two + one)
            one = rho * one
            v_ref[x, at] = local[x, at] + (two + tilt * one)
        for x in range(length - 1, -1, -1):
            value = gain * (v_ref[x, at] + (back_two + tilt * back_one))
            v_high[x, at], v_low[x, at] = split(value)
            back_one = rho * back_one
            back_two = rho * back_two + back_one
        return carry

    lax.fori_loop(0, ny // block, correct, 0)
    pair = 2 if length % 2 == 0 else 1
    rows = ny // tests
    for g in range(0, length, pair):
        right = tuple(jnp.concatenate([ref[g + k] for k in range(pair)], axis=1) for ref in (v_high, v_low))
        total = dot3((c_high[...], c_low[...]), right)
        for k in range(pair):
            for t in range(tests):
                out[t, g + k] = total[t * rows : (t + 1) * rows, k * lanes_count : (k + 1) * lanes_count]


def finish(meta, across, deep, local, state, packed, tables, parts, width, tests, scale):
    length, ny, lanes = local.shape
    spaces = packed.shape[0]
    cells = length * ny * lanes
    return pl.pallas_call(
        functools.partial(finish_kernel, length, parts, width, spaces, tests, scale),
        out_shape=jax.ShapeDtypeStruct((tests, length, ny // tests, lanes), F32),
        in_specs=[SMEM_SPEC] + [VMEM_SPEC] * 7,
        out_specs=VMEM_SPEC,
        scratch_shapes=[
            pltpu.VMEM((length, ny, lanes), F32),
            pltpu.VMEM((length, ny, lanes), BF16),
            pltpu.VMEM((length, ny, lanes), BF16),
        ],
        compiler_params=pltpu.CompilerParams(vmem_limit_bytes=VMEM_LIMIT),
        cost_estimate=pl.CostEstimate(flops=6 * cells * ny, bytes_accessed=16 * cells, transcendentals=0),
        name="finish",
    )(meta, across, deep, local, state, packed, *tables)


def depth_kernel(tests, parts, depth, pieces, bd_high, bd_low, out):
    rows = pieces.shape[1]
    value = jnp.concatenate([pieces[t] for t in range(tests)], axis=1)
    result = dot3(split(value), (bd_high[...], bd_low[...]))
    for j in range(parts):
        out[j] = result[:, j * depth : (j + 1) * depth]


def depth_cells(pieces, tables, parts, depth):
    tests, rows, lanes = pieces.shape
    steps = 3 if rows % 24 == 0 else 1
    return pl.pallas_call(
        functools.partial(depth_kernel, tests, parts, depth),
        out_shape=jax.ShapeDtypeStruct((parts, rows, depth), F32),
        grid=(steps,),
        in_specs=[
            pl.BlockSpec((tests, rows // steps, lanes), lambda i: (0, i, 0)),
            pl.BlockSpec(tables[0].shape, lambda i: (0, 0)),
            pl.BlockSpec(tables[1].shape, lambda i: (0, 0)),
        ],
        out_specs=pl.BlockSpec((parts, rows // steps, depth), lambda i: (0, i, 0)),
        compiler_params=pltpu.CompilerParams(vmem_limit_bytes=VMEM_LIMIT),
        cost_estimate=pl.CostEstimate(
            flops=6 * tests * rows * lanes * parts * depth, bytes_accessed=8 * tests * rows * lanes, transcendentals=0
        ),
        name="depth_cells",
    )(pieces, *tables)


def on_device(log_k, heads, warm_adjoint, obs_columns, obs_residuals, well_columns):
    rows, ny, depth = log_k.shape
    spaces = lax.axis_size("space")
    tests = lax.axis_size("test")
    rank = lax.axis_index("space")
    test = lax.axis_index("test")
    chips = tests // 2
    width = depth // tests
    parts = depth // width if depth // width == 4 and rows % 4 == 0 else 1
    length = rows // parts
    lanes = depth
    count_x = rows * spaces

    forward = [(i, i + 1) for i in range(spaces - 1)]
    backward = [(i + 1, i) for i in range(spaces - 1)]

    def with_halo(field, count):
        low = lax.ppermute(field[rows - count :], "space", forward)
        high = lax.ppermute(field[:count], "space", backward)
        return low, field, high

    w_parts = with_halo(warm_adjoint[0], HALO)
    lk_parts = with_halo(log_k, HALO)
    h_parts = with_halo(heads[0], 1)

    chip, core = test // 2, test % 2
    order = [2 * ((chip + k) % chips) + core for k in range(chips)]
    order += [2 * ((chip + k) % chips) + 1 - core for k in range(chips)]
    meta = jnp.stack([rank * rows, well_columns[0], test, rank] + order).astype(jnp.int32)

    v, q, sums = moments(meta, obs_columns[0], obs_residuals[0], lk_parts, w_parts, count_x)
    m0, m1, m2, m3 = lax.psum(sums, "space")
    alpha = m0 / m1
    new = alpha * alpha * m2 - 2.0 * alpha * m1 + m0
    beta = new / m0
    bent = 1.0 + beta
    second = new / (bent * bent * m1 - 2.0 * bent * alpha * m2 + alpha * alpha * m3)
    coeffs = jnp.stack([alpha + second * bent, -second * alpha])

    cas_z = cas(depth)
    forward_z = np.zeros((parts, depth, tests, lanes))
    inverse_z = np.zeros((tests, lanes, parts, depth))
    kappa_z = np.zeros((tests, lanes))
    for t in range(tests):
        chosen = np.arange(t * width, (t + 1) * width)
        for j in range(parts):
            at = slice(j * width, (j + 1) * width)
            forward_z[j, :, t, at] = cas_z[:, chosen]
            inverse_z[t, at, j, :] = cas_z[chosen, :]
            kappa_z[t, at] = kappa(depth)[chosen]
    forward_z = halves(forward_z.reshape(parts * depth, tests * lanes))
    inverse_z = halves(inverse_z.reshape(tests * lanes, parts * depth))
    deep = kappa_z.astype(np.float32)
    across = np.repeat(kappa(ny)[:, None], lanes, axis=1).astype(np.float32)
    cas_y = cas(ny)

    chunks = 2 if (ny // 2) % 48 == 0 else 1
    size = ny // chunks
    other_core = [(i, i ^ 1) for i in range(tests)]
    groups, tables = [], []
    for c in range(chunks):
        mine, other = misfit(
            meta, coeffs, lk_parts, w_parts, h_parts, v, q, forward_z, c * size, size, parts, tests
        )
        summed = mine + lax.ppermute(other, "test", other_core)
        total = summed[0]
        for k in range(1, chips):
            total = total + lax.ppermute(
                summed[k], "test", [(i, (i + 2 * k) % tests) for i in range(tests)]
            )
        groups.append(total)
        tables += halves(cas_y[:, c * size : (c + 1) * size])

    local, state, packed = solve(meta, across, deep, groups, tables, length, parts, width)
    gathered = lax.all_gather(packed, "space")
    pieces = finish(
        meta, across, deep, local, state, gathered, halves(cas_y), parts, width, tests, 1.0 / (ny * depth)
    )
    pieces = pieces.reshape(tests, length * (ny // tests), lanes)
    pieces = lax.all_to_all(pieces, "test", split_axis=0, concat_axis=0, tiled=True)
    return depth_cells(pieces, inverse_z, parts, depth).reshape(rows, ny // tests, depth)


def solution(mesh):
    placed = (
        P(("groups", "space"), None, None),
        P("test", ("groups", "space"), None, None),
        P("test", ("groups", "space"), None, None),
        P("test", "groups"),
        P("test", "groups", None),
        P(("groups", "test")),
    )
    return jax.shard_map(
        on_device,
        mesh=mesh,
        in_specs=placed,
        out_specs=P(("groups", "space"), "test", None),
        check_vma=False,
    )
```

```python
import functools

import jax
import jax.numpy as jnp
import ml_dtypes
import numpy as np
from jax import lax
from jax.experimental import pallas as pl
from jax.experimental.pallas import tpu as pltpu
from jax.sharding import PartitionSpec as P

prior_gain = 5.0
range_squared = 4.0

HALO = 3
PAD = 8
F32 = jnp.float32
BF16 = jnp.bfloat16
VMEM_LIMIT = 32 * 1024 * 1024
SMALL_LIMIT = 20 * 1024 * 1024
MISFIT_LIMIT = 40 * 1024 * 1024

SMEM_SPEC = pl.BlockSpec(memory_space=pltpu.SMEM)
VMEM_SPEC = pl.BlockSpec(memory_space=pltpu.VMEM)
ANY_SPEC = pl.BlockSpec(memory_space=pl.ANY)


def in_vmem(array):
    return pltpu.with_memory_space_constraint(array, pltpu.VMEM)


def in_hbm(array):
    return pltpu.with_memory_space_constraint(array, pltpu.HBM)


def cas(length):
    index = np.arange(length)
    angle = 2.0 * np.pi * (index[:, None] * index[None, :] % length) / length
    return np.cos(angle) + np.sin(angle)


def halves(table):
    table = np.asarray(table, np.float32)
    high = table.astype(ml_dtypes.bfloat16)
    low = (table - high.astype(np.float32)).astype(ml_dtypes.bfloat16)
    return high, low


def kappa(length):
    return 4.0 * np.sin(np.pi * np.arange(length) / length) ** 2


def split(value):
    high = value.astype(BF16)
    low = (value - high.astype(F32)).astype(BF16)
    return high, low


def dot(left, right):
    return lax.dot_general(left, right, (((1,), (0,)), ((), ())), preferred_element_type=F32)


def dot3(left, right):
    return dot(left[0], right[0]) + (dot(left[0], right[1]) + dot(left[1], right[0]))


def block_rows(count):
    for rows in (48, 32, 16):
        if count % rows == 0:
            return rows
    return count


def unrolled(start, stop, body, carry, most=4):
    count = stop - start
    factor = next(f for f in range(most, 0, -1) if count % f == 0)
    return lax.fori_loop(start, stop, body, carry, unroll=factor)


def lane_index(shape):
    return lax.broadcasted_iota(jnp.int32, shape, 1)


def window(ref, start, rows):
    return ref.at[pl.ds(pl.multiple_of(start - PAD, 8), rows + 2 * PAD)]


def neighbour_sum(ref, start, rows, plane, fill):
    near = window(ref, start, rows)
    here = near[PAD : PAD + rows]
    lanes = lane_index(here.shape)
    depth = here.shape[1]
    up = jnp.where(lanes == depth - 1, fill, pltpu.roll(here, depth - 1, 1))
    down = jnp.where(lanes == 0, fill, pltpu.roll(here, 1, 1))
    along = ref[pl.ds(pl.multiple_of(start - plane, 8), rows)] + ref[pl.ds(pl.multiple_of(start + plane, 8), rows)]
    across = near[PAD - 1 : PAD - 1 + rows] + near[PAD + 1 : PAD + 1 + rows]
    return along + across + (up + down), here


def fold(value):
    return jnp.sum(value.reshape(-1, 8, value.shape[1]), axis=0)


def field_rows(rows, ny):
    return (rows + 2 * HALO) * (ny + PAD) + PAD


def scale_plane(e_ref, u_ref, p, ny, size, lk_of, w_of):
    base = p * (ny + PAD) + PAD
    for b in range(0, ny, size):
        e = jnp.exp(0.5 * lk_of(b).astype(F32))
        at = pl.ds(pl.multiple_of(base + b, 8), size)
        e_ref[at] = e
        u_ref[at] = e * w_of(b).astype(F32)


def residual_plane(e_ref, u_ref, s_ref, r_ref, v_ref, p, ny, size, valid):
    plane = ny + PAD
    for b in range(0, ny, size):
        start = p * plane + PAD + b
        at = pl.ds(pl.multiple_of(start, 8), size)
        flat = pl.ds(pl.multiple_of(p * ny + b, 8), size)
        s, e = neighbour_sum(e_ref, start, size, plane, 1.0)
        n, u = neighbour_sum(u_ref, start, size, plane, 0.0)
        r = e * n - s * u
        if valid is not None:
            r = r * valid
        s_ref[flat] = s
        r_ref[flat] = r
        v_ref[at] = e * r


def thirds(ref):
    count = ref.shape[0] // 3
    return tuple(ref.at[pl.ds(k * count, count)] for k in range(3))


def halved(ref):
    count = ref.shape[0] // 2
    return tuple(ref.at[pl.ds(k * count, count)] for k in range(2))


def interior_kernel(rows, ny, pieces, meta, lk_in, w_in, fields, flats, lk, w, sems):
    e_ref, u_ref, v_ref = thirds(fields)
    s_ref, r_ref = halved(flats)
    depth = lk.shape[2]
    plane = ny + PAD
    planes = rows + 2 * HALO
    size = block_rows(ny)
    count = rows // pieces
    copies = []
    for piece in range(pieces):
        at = pl.ds(piece * count, count)
        for k, (source, target) in enumerate(((lk_in, lk), (w_in, w))):
            copies.append(pltpu.make_async_copy(source.at[at], target.at[at], sems.at[2 * piece + k]))
    for copy in copies:
        copy.start()
    ones = jnp.ones((PAD, depth), F32)
    zeros = jnp.zeros((PAD, depth), F32)

    def clear(p, carry):
        at = pl.ds(pl.multiple_of(p * plane, 8), PAD)
        e_ref[at] = ones
        u_ref[at] = zeros
        v_ref[at] = zeros
        return carry

    lax.fori_loop(0, planes + 1, clear, 0)

    def scale(x, carry):
        scale_plane(
            e_ref, u_ref, x + HALO, ny, size, lambda b: lk[x, b : b + size], lambda b: w[x, b : b + size]
        )
        return carry

    for piece in range(pieces):
        copies[2 * piece].wait()
        copies[2 * piece + 1].wait()
        unrolled(piece * count, (piece + 1) * count, scale, 0)

    def residual(p, carry):
        residual_plane(e_ref, u_ref, s_ref, r_ref, v_ref, p, ny, size, None)
        return carry

    unrolled(HALO + 1, HALO + rows - 1, residual, 0)


def interior(meta, lk, w):
    rows, ny, depth = lk.shape
    fields = pltpu.VMEM((3 * field_rows(rows, ny), depth), F32)
    flats = pltpu.VMEM((2 * (rows + 2 * HALO) * ny, depth), F32)
    cells = rows * ny * depth
    pieces = next(k for k in (4, 3, 2, 1) if rows % k == 0)
    return pl.pallas_call(
        functools.partial(interior_kernel, rows, ny, pieces),
        out_shape=(fields, flats),
        in_specs=[SMEM_SPEC] + [ANY_SPEC] * 2,
        out_specs=(VMEM_SPEC,) * 2,
        scratch_shapes=[
            pltpu.VMEM((rows, ny, depth), BF16),
            pltpu.VMEM((rows, ny, depth), BF16),
            pltpu.SemaphoreType.DMA((2 * pieces,)),
        ],
        compiler_params=pltpu.CompilerParams(vmem_limit_bytes=SMALL_LIMIT),
        cost_estimate=pl.CostEstimate(flops=5000 * cells, bytes_accessed=4 * cells, transcendentals=cells),
        name="interior",
    )(meta, in_hbm(lk), in_hbm(w))


def moments_kernel(
    rows, ny, count_x,
    meta, columns, residuals, ends_low, ends_high, fields_in, flats_in,
    fields, flats, held_out, mom_out, sems,
):
    e_ref, u_ref, v_ref = thirds(fields)
    s_ref, r_ref = halved(flats)
    holds = [
        pltpu.make_async_copy(ref.at[pl.ds(0, held_out.shape[1])], held_out.at[k], sems.at[k])
        for k, ref in enumerate((e_ref, u_ref, v_ref))
    ]
    depth = residuals.shape[1]
    plane = ny + PAD
    planes = rows + 2 * HALO
    size = block_rows(ny)
    blocks = range(0, ny, size)
    first_row = meta[0]

    for ends, begin in ((ends_low, 0), (ends_high, HALO + rows)):

        def scale(p, carry):
            scale_plane(
                e_ref, u_ref, p + begin, ny, size,
                lambda b: ends[HALO + p, b : b + size], lambda b: ends[p, b : b + size],
            )
            return carry

        unrolled(0, HALO, scale, 0)

    def inside(p):
        row = first_row + p - HALO
        return jnp.where((row >= 0) & (row < count_x), 1.0, 0.0).astype(F32)

    def residual(p, carry):
        residual_plane(e_ref, u_ref, s_ref, r_ref, v_ref, p, ny, size, inside(p))
        return carry

    unrolled(1, HALO + 1, residual, 0)
    unrolled(HALO + rows - 1, planes - 1, residual, 0)

    def plant(o, carry):
        column = columns[o]
        row = lax.div(column, ny)
        y = column - row * ny
        p = row - first_row + HALO

        @pl.when((p >= 1) & (p < planes - 1))
        def _():
            at = pl.ds(p * plane + PAD + y, 1)
            flat = pl.ds(p * ny + y, 1)
            added = residuals[pl.ds(o, 1)]
            r_ref[flat] = r_ref[flat] + added
            v_ref[at] = v_ref[at] + e_ref[at] * added

        return carry

    holds[0].start()
    lax.fori_loop(0, columns.shape[0], plant, 0)
    holds[2].start()

    def image(p, sums, valid, summed):
        m0, m1, m2 = sums
        base = p * plane + PAD
        for b in blocks:
            start = base + b
            at = pl.ds(pl.multiple_of(start, 8), size)
            flat = pl.ds(pl.multiple_of(p * ny + b, 8), size)
            n, v = neighbour_sum(v_ref, start, size, plane, 0.0)
            e = e_ref[at]
            y = s_ref[flat] * v - e * n
            if valid is not None:
                y = y * valid
            u_ref[at] = e * y
            if summed:
                r = r_ref[flat]
                m0 = m0 + fold(r * r)
                m1 = m1 + fold(r * y)
                m2 = m2 + fold(y * y)
                r_ref[flat] = y
        return m0, m1, m2

    zero = jnp.zeros((8, depth), F32)
    sums = (zero, zero, zero)
    image(HALO - 1, sums, inside(HALO - 1), False)
    image(HALO + rows, sums, inside(HALO + rows), False)
    m0, m1, m2 = unrolled(HALO, HALO + rows, lambda p, c: image(p, c, None, True), sums)

    holds[1].start()

    def second(p, m3):
        base = p * plane + PAD
        for b in blocks:
            start = base + b
            flat = pl.ds(pl.multiple_of(p * ny + b, 8), size)
            near = window(u_ref, start, size)
            q = near[PAD : PAD + size]
            up = jnp.where(lane_index(q.shape) == depth - 1, 0.0, pltpu.roll(q, depth - 1, 1))
            ahead = u_ref[pl.ds(pl.multiple_of(start + plane, 8), size)] + near[PAD + 1 : PAD + 1 + size] + up
            m3 = m3 + fold(q * (s_ref[flat] * r_ref[flat] - 2.0 * ahead))
        return m3

    m3 = unrolled(HALO, HALO + rows, second, zero)
    for k, m in enumerate((m0, m1, m2, m3)):
        mom_out[k] = jnp.sum(m)
    for hold in holds:
        hold.wait()


def moments(meta, columns, residuals, ends, fields, flats, rows, ny, count_x):
    depth = residuals.shape[1]
    cells = rows * ny * depth
    return pl.pallas_call(
        functools.partial(moments_kernel, rows, ny, count_x),
        out_shape=(
            pltpu.VMEM(fields.shape, F32), pltpu.VMEM(flats.shape, F32),
            jax.ShapeDtypeStruct((3, fields.shape[0] // 3 - PAD, depth), F32), jax.ShapeDtypeStruct((4,), F32),
        ),
        in_specs=[SMEM_SPEC, SMEM_SPEC] + [VMEM_SPEC] * 5,
        out_specs=(VMEM_SPEC,) * 2 + (ANY_SPEC, SMEM_SPEC),
        input_output_aliases={5: 0, 6: 1},
        scratch_shapes=[pltpu.SemaphoreType.DMA((3,))],
        compiler_params=pltpu.CompilerParams(vmem_limit_bytes=SMALL_LIMIT),
        cost_estimate=pl.CostEstimate(flops=5000 * cells, bytes_accessed=4 * cells, transcendentals=cells),
        name="moments",
    )(meta, columns, residuals, *ends, in_vmem(fields), in_vmem(flats))


def step_lengths(sums):
    m0, m1, m2, m3 = (sum(ref[k] for ref in sums) for k in range(4))
    alpha = m0 / m1
    new = alpha * alpha * m2 - 2.0 * alpha * m1 + m0
    bent = 1.0 + new / m0
    second = new / (bent * bent * m1 - 2.0 * bent * alpha * m2 + alpha * alpha * m3)
    return alpha + second * bent, -second * alpha


def misfit_kernel(rows, ny, first, size, parts, tests, terms, meta, *refs):
    sums = refs[:terms]
    (
        fields, w, h, ends_low, ends_high, bd_high, bd_low,
        mine_out, other_out, e_ref, q_ref, v_ref, w_ref, h_bf, a_ref, h_ref, x_ref, t_high, t_low, sems,
    ) = refs[terms:]
    depth = w.shape[2]
    length = rows // parts
    plane = ny + PAD
    slot_rows = size + 2 * PAD
    edge = 16
    low = edge if first > 0 else 0
    high = edge if first + size < ny else 0
    held = PAD + size + (PAD if high else 0)
    early = min(4, length)
    sem = iter(range(sems.shape[0]))
    waits = ([], [])

    def bring(source, target, group):
        copy = pltpu.make_async_copy(source, target, sems.at[next(sem)])
        copy.start()
        waits[group].append(copy)

    def bring_rows(group, begin, end):
        count = end - begin
        for k, ref in enumerate((e_ref, q_ref, v_ref)):
            bring(
                fields.at[k, pl.ds(begin + HALO - 1, count), pl.ds(first, held)],
                ref.at[pl.ds(begin, count), pl.ds(0, held)],
                group,
            )
        ys, yt = pl.ds(first - low, low + size + high), pl.ds(edge - low, low + size + high)
        for source, below, above, ref in ((w, HALO - 1, 0, w_ref), (h, 2 * HALO, 2 * HALO, h_bf)):
            lo, hi = begin, end
            if lo == 0:
                bring(ends_low.at[pl.ds(below, 1), ys], ref.at[pl.ds(0, 1), yt], group)
                lo = 1
            if hi == rows + 2:
                bring(ends_high.at[pl.ds(above, 1), ys], ref.at[pl.ds(rows + 1, 1), yt], group)
                hi = rows + 1
            if hi > lo:
                bring(source.at[pl.ds(lo - 1, hi - lo), ys], ref.at[pl.ds(lo, hi - lo), yt], group)

    for part in range(parts):
        bring_rows(0, part * length, part * length + early)
    for part in range(parts):
        end = rows + 2 if part == parts - 1 else (part + 1) * length
        if end > part * length + early:
            bring_rows(1, part * length + early, end)
    block = block_rows(size)
    blocks = range(0, size, block)
    first_row, well = meta[0], meta[1]
    c0, c1 = step_lengths(sums)
    lanes_out = mine_out.shape[2]
    chips = tests // 2
    chip, core = meta[2] // 2, meta[2] % 2

    if first + size == ny:
        beyond = jnp.ones((PAD, depth), F32)

        def fill(p, carry):
            e_ref[p, pl.ds(PAD + size, PAD)] = beyond
            return carry

        lax.fori_loop(0, rows + 2, fill, 0)
    zeros = jnp.zeros((PAD, depth), F32)
    for s in range(4 * parts):
        for at in (pl.ds(s * slot_rows, PAD), pl.ds(s * slot_rows + PAD + size, PAD)):
            a_ref[at] = zeros
            h_ref[at] = zeros

    def slot(part, i):
        return (4 * part + lax.rem(i, 4)) * slot_rows

    spans = [(b, block, 0, block) for b in blocks]
    if low:
        spans.append((-edge, edge, PAD, PAD))
    if high:
        spans.append((size, edge, 0, PAD))

    def prepare(part, i):
        base = slot(part, i)
        p = part * length + i
        for y, count, skip, keep in spans:
            at = slice(PAD + y + skip, PAD + y + skip + keep)
            to = pl.ds(pl.multiple_of(base + PAD + y + skip, 8), keep)
            wide = w_ref[p, edge + y : edge + y + count].astype(F32)[skip : skip + keep]
            a_ref[to] = e_ref[p, at] * wide + c0 * v_ref[p, at] + c1 * q_ref[p, at]
            h_ref[to] = h_bf[p, edge + y : edge + y + count].astype(F32)[skip : skip + keep]

    def rows_at(start, count):
        return pl.ds(pl.multiple_of(start, 8), count)

    def along(part):
        for b in blocks:
            at = rows_at(slot(part, 0) + PAD + b, block)
            to = rows_at(slot(part, 1) + PAD + b, block)
            e = e_ref[part * length, PAD + b : PAD + b + block]
            en = e_ref[part * length + 1, PAD + b : PAD + b + block]
            x_ref[part, b : b + block] = (en * a_ref[at] - e * a_ref[to]) * (h_ref[at] - h_ref[to])

    def centre(part, x, buffer):
        here, there = slot(part, x + 1), slot(part, x + 2)
        p = part * length + x + 1
        column = (first_row + part * length + x) * ny + first
        for b in blocks:
            to = rows_at(there + PAD + b, block)
            e_near = e_ref.at[p, b : b + block + 2 * PAD]
            a_near, h_near = (window(ref, here + PAD + b, block) for ref in (a_ref, h_ref))
            mid = slice(PAD, PAD + block)
            e, a, hh = e_near[mid], a_near[mid], h_near[mid]
            en, an, hn = e_ref[p + 1, PAD + b : PAD + b + block], a_ref[to], h_ref[to]
            before = x_ref[part, b : b + block]
            after = (en * a - e * an) * (hh - hn)
            x_ref[part, b : b + block] = after
            total = before + after
            for shift in (-1, 1):
                at = slice(PAD + shift, PAD + shift + block)
                en, an, hn = e_near[at], a_near[at], h_near[at]
                total = total + (en * a - e * an) * (hh - hn)
            lanes = lane_index(e.shape)
            end = lanes == depth - 1
            en = jnp.where(end, 1.0, pltpu.roll(e, depth - 1, 1))
            an = jnp.where(end, 0.0, pltpu.roll(a, depth - 1, 1))
            hn = jnp.where(end, 0.0, pltpu.roll(hh, depth - 1, 1))
            up = (en * a - e * an) * (hh - hn)
            down = jnp.where(lanes == 0, a * hh, pltpu.roll(up, 1, 1))
            total = -0.5 * (total + up + down)
            row = lax.broadcasted_iota(jnp.int32, e.shape, 0) + (column + b)
            total = jnp.where(row == well, 0.0, total)
            high_part, low_part = split(total)
            t_high[buffer, b : b + block, part * depth : (part + 1) * depth] = high_part
            t_low[buffer, b : b + block, part * depth : (part + 1) * depth] = low_part

    def transform(x, buffer):
        value = dot3((t_high[buffer], t_low[buffer]), (bd_high[...], bd_low[...]))
        at = rows_at(x * size, size)
        for c in range(chips):
            even, odd = (value[:, (2 * c + k) * lanes_out : (2 * c + k + 1) * lanes_out] for k in range(2))
            k = lax.rem(c + chips - chip, chips)
            mine_out[k, at] = jnp.where(core == 0, even, odd)
            other_out[k, at] = jnp.where(core == 0, odd, even)

    def step(x):
        for part in range(parts):
            prepare(part, x + 2)
        for part in range(parts):
            centre(part, x, lax.rem(x, 2))

    def loop(x, carry):
        transform(x - 1, lax.rem(x + 1, 2))
        step(x)
        return carry

    for copy in waits[0]:
        copy.wait()
    for part in range(parts):
        prepare(part, 0)
        prepare(part, 1)
        along(part)
    if parts == 1 or length <= early:
        for copy in waits[1]:
            copy.wait()
        step(0)
        lax.fori_loop(1, length, loop, 0)
    else:
        step(0)
        lax.fori_loop(1, early - 2, loop, 0)
        for copy in waits[1]:
            copy.wait()
        lax.fori_loop(early - 2, length, loop, 0)
    transform(length - 1, (length - 1) % 2)


def misfit(meta, sums, fields, w, h, ends, tables, first, size, parts, tests):
    rows, ny, depth = w.shape
    length = rows // parts
    lanes = tables[0].shape[1] // tests
    out = jax.ShapeDtypeStruct((tests // 2, length * size, lanes), F32)
    ring = pltpu.VMEM((4 * parts * (size + 2 * PAD), depth), F32)
    full = pltpu.VMEM((rows + 2, size + 2 * PAD, depth), F32)
    half = pltpu.VMEM((rows + 2, size + 32, depth), BF16)
    cells = rows * size * depth
    return pl.pallas_call(
        functools.partial(misfit_kernel, rows, ny, first, size, parts, tests, len(sums)),
        out_shape=(out, out),
        in_specs=[SMEM_SPEC] * (1 + len(sums)) + [ANY_SPEC] * 5 + [VMEM_SPEC] * 2,
        out_specs=(VMEM_SPEC, VMEM_SPEC),
        scratch_shapes=[
            full, full, full, half, half, ring, ring,
            pltpu.VMEM((parts, size, depth), F32),
            pltpu.VMEM((2, size, parts * depth), BF16),
            pltpu.VMEM((2, size, parts * depth), BF16),
            pltpu.SemaphoreType.DMA((10 * parts + 4,)),
        ],
        compiler_params=pltpu.CompilerParams(vmem_limit_bytes=MISFIT_LIMIT),
        cost_estimate=pl.CostEstimate(flops=8000 * cells, bytes_accessed=4 * cells, transcendentals=cells),
        name="misfit",
    )(meta, *sums, in_hbm(fields), in_hbm(w), in_hbm(h), *ends, *tables)


def pack_rest(rests, width, kept):
    lanes = lane_index(rests[0].shape) % width
    result = rests[0]
    for m in range(1, len(rests)):
        moved = pltpu.roll(rests[m], m * kept, 1)
        result = jnp.where((lanes >= m * kept) & (lanes < (m + 1) * kept), moved, result)
    return result


def unpack_rest(packed, count, width, kept):
    near = lane_index(packed.shape) % width < kept
    depth = packed.shape[1]
    return [
        jnp.where(near, packed if m == 0 else pltpu.roll(packed, depth - m * kept, 1), 0.0) for m in range(count)
    ]


def join_kernel(length, width, kept, mine, other, own_out, far_out):
    far_count, rows = mine.shape[0] - 1, mine.shape[1]
    size = rows // length
    share = width // kept
    block = block_rows(size)

    def add(i, carry):
        at = pl.ds(pl.multiple_of(i * size, 16), size)
        own_out[at] = mine[0, at] + other[0, at]
        return carry

    lax.fori_loop(0, length, add, 0)
    for f in range(far_count):

        def code(i, carry):
            for b in range(0, size, block):
                rests = []
                for m in range(share):
                    at = pl.ds(pl.multiple_of((i * share + m) * size + b, 16), block)
                    value = mine[1 + f, at] + other[1 + f, at]
                    high = value.astype(BF16)
                    far_out[f, at] = high
                    rests.append(value - high.astype(F32))
                at = pl.ds(pl.multiple_of(rows + i * size + b, 16), block)
                far_out[f, at] = pack_rest(rests, width, kept).astype(BF16)
            return carry

        lax.fori_loop(0, length // share, code, 0)


def join(mine, other, length, width, kept):
    chips, rows, lanes = mine.shape
    return pl.pallas_call(
        functools.partial(join_kernel, length, width, kept),
        out_shape=(
            jax.ShapeDtypeStruct((rows, lanes), F32),
            jax.ShapeDtypeStruct((chips - 1, rows + rows * kept // width, lanes), BF16),
        ),
        in_specs=[VMEM_SPEC] * 2,
        out_specs=(VMEM_SPEC,) * 2,
        compiler_params=pltpu.CompilerParams(vmem_limit_bytes=VMEM_LIMIT),
        cost_estimate=pl.CostEstimate(flops=4 * rows * lanes, bytes_accessed=16 * rows * lanes, transcendentals=0),
        name="join",
    )(mine, other)


def power(value, exponent):
    result = None
    while exponent:
        if exponent & 1:
            result = value if result is None else result * value
        exponent >>= 1
        if exponent:
            value = value * value
    return result


def ratio_of(across, deep):
    half = (1.0 + range_squared * (across + deep) + 2.0 * range_squared) / (2.0 * range_squared)
    return 1.0 / (half + jnp.sqrt(half * half - 1.0))


def by_block(values, lanes, width):
    result = values[-1]
    for j in range(len(values) - 2, -1, -1):
        result = jnp.where(lanes < (j + 1) * width, values[j], result)
    return result


def powers(value, length, count):
    step = power(value, length)
    result = [jnp.ones_like(value)]
    for _ in range(count - 1):
        result.append(result[-1] * step)
    return result


def everywhere(value, width):
    lanes = value.shape[1]
    shift = width
    while shift < lanes:
        value = value + pltpu.roll(value, shift, 1)
        shift *= 2
    return value


def solve_kernel(length, parts, width, kept, chunks, fars, meta, across, deep, *refs):
    groups = refs[:chunks]
    far_refs = refs[chunks : chunks * (1 + fars)]
    tables = refs[chunks * (1 + fars) : chunks * (3 + fars)]
    local_out, state_out, packed_out, h_ref = refs[chunks * (3 + fars) :]
    ny, lanes_count = across.shape
    size = groups[0].shape[0] // length
    pair = 2 if length % 2 == 0 else 1
    share = width // kept
    rests = {}

    def gathered(c, x):
        at = slice(x * size, (x + 1) * size)
        value = groups[c][at]
        for f in range(fars):
            ref = far_refs[c * fars + f]
            g = x // share
            if (c, f, g) not in rests:
                start = length * size + g * size
                rests[c, f, g] = unpack_rest(ref[start : start + size].astype(F32), share, width, kept)
            value = value + (ref[at].astype(F32) + rests[c, f, g][x % share])
        return value

    for g in range(0, length, pair):
        total = None
        for c in range(chunks):
            value = jnp.concatenate([gathered(c, g + k) for k in range(pair)], axis=1)
            product = dot3((tables[2 * c][...], tables[2 * c + 1][...]), split(value))
            total = product if total is None else total + product
        for k in range(pair):
            h_ref[g + k] = total[:, k * lanes_count : (k + 1) * lanes_count]

    block = block_rows(ny)
    qz = deep[pl.ds(meta[2], 1)]

    def solve(i, carry):
        at = pl.ds(pl.multiple_of(i * block, 16), block)
        rho = ratio_of(across[at], qz)
        square = rho * rho
        tilt = (1.0 + square) / (1.0 - square)
        p1 = jnp.zeros_like(rho)
        p2 = jnp.zeros_like(rho)
        for x in range(length):
            p2 = rho * (p2 + p1)
            p1 = h_ref[x, at] + rho * p1
            local_out[x, at] = p2 + tilt * p1
        n1 = jnp.zeros_like(rho)
        n2 = jnp.zeros_like(rho)
        for x in range(length - 1, -1, -1):
            local_out[x, at] = local_out[x, at] + (n2 + tilt * n1)
            n1 = rho * (n1 + h_ref[x, at])
            n2 = rho * n2 + n1
        if parts == 1:
            for k, value in enumerate((p1, p2, n1, n2)):
                state_out[k, at] = jnp.zeros_like(rho)
                packed_out[k, at] = value
            return carry
        lanes = lane_index(rho.shape)
        steps = powers(rho, length, parts)
        zero = jnp.zeros_like(rho)
        into = [zero] * 4
        for s in range(1, parts):
            weight = jnp.where(lanes >= s * width, steps[s - 1], 0.0)
            far = float(length * (s - 1))
            one, two = (pltpu.roll(value, s * width, 1) for value in (p1, p2))
            into[0] = into[0] + weight * one
            into[1] = into[1] + weight * (two + far * one)
            weight = jnp.where(lanes < (parts - s) * width, steps[s - 1], 0.0)
            one, two = (pltpu.roll(value, lanes_count - s * width, 1) for value in (n1, n2))
            into[2] = into[2] + weight * one
            into[3] = into[3] + weight * (two + far * one)
        for k in range(4):
            state_out[k, at] = into[k]
        place = lanes // width
        weight = by_block(steps[::-1], lanes, width)
        far = ((parts - 1 - place) * length).astype(F32)
        d1 = everywhere(weight * p1, width)
        d2 = everywhere(weight * (p2 + far * p1), width)
        weight = by_block(steps, lanes, width)
        far = (place * length).astype(F32)
        e1 = everywhere(weight * n1, width)
        e2 = everywhere(weight * (n2 + far * n1), width)
        packed_out[at] = by_block([d1, d2, e1, e2], lanes, width)
        return carry

    lax.fori_loop(0, ny // block, solve, 0)


def solve(meta, across, deep, groups, fars, tables, length, parts, width, kept):
    ny, lanes = across.shape
    chunks = len(groups)
    packed = (ny, lanes) if parts == 4 else (4, ny, lanes)
    cells = length * ny * lanes
    return pl.pallas_call(
        functools.partial(solve_kernel, length, parts, width, kept, chunks, len(fars) // chunks),
        out_shape=(
            jax.ShapeDtypeStruct((length, ny, lanes), F32),
            jax.ShapeDtypeStruct((4, ny, lanes), F32),
            jax.ShapeDtypeStruct(packed, F32),
        ),
        in_specs=[SMEM_SPEC] + [VMEM_SPEC] * (2 + 3 * chunks + len(fars)),
        out_specs=(VMEM_SPEC,) * 3,
        scratch_shapes=[pltpu.VMEM((length, ny, lanes), F32)],
        compiler_params=pltpu.CompilerParams(vmem_limit_bytes=VMEM_LIMIT),
        cost_estimate=pl.CostEstimate(flops=6 * cells * ny, bytes_accessed=16 * cells, transcendentals=0),
        name="solve",
    )(meta, across, deep, *groups, *fars, *tables)


def peer(test, chips, hop, which):
    return 2 * lax.rem(test // 2 + hop, chips) + lax.rem(test % 2 + which, 2)


def finish_kernel(length, parts, width, kept, spaces, tests, scale, meta, across, deep, local, state, *refs):
    packed = refs[:spaces]
    c_high, c_low, *outs = refs[spaces : -4]
    v_ref, v_high, v_low, total_ref = refs[-4:]
    ny, lanes_count = across.shape
    block = block_rows(ny)
    qz = deep[pl.ds(meta[2], 1)]
    slab = length * parts

    def correct(i, carry):
        at = pl.ds(pl.multiple_of(i * block, 16), block)
        rho = ratio_of(across[at], qz)
        square = rho * rho
        tilt = (1.0 + square) / (1.0 - square)
        gain = rho / (2.0 * range_squared * 0.5 * (1.0 - square))
        gain = (prior_gain * scale) * gain * gain
        lanes = lane_index(rho.shape)
        step = power(rho, slab)
        weight = jnp.ones_like(rho)
        if parts > 1:
            near = far = jnp.zeros_like(rho)
            for k in range(1, spaces + 1):
                left = packed[k % spaces][at].astype(F32)
                right = packed[(spaces - k) % spaces][at].astype(F32)
                value = weight * jnp.where(lanes < 2 * width, left, right)
                near = near + value
                far = far + float(slab * (k - 1)) * value
                weight = weight * step

            def pick(value, s):
                return everywhere(jnp.where((lanes >= s * width) & (lanes < (s + 1) * width), value, 0.0), width)

            one, two, far_one = pick(near, 0), pick(near, 1), pick(far, 0)
            back_one, back_two, back_far = pick(near, 2), pick(near, 3), pick(far, 2)
        else:
            one = two = far_one = back_one = back_two = back_far = jnp.zeros_like(rho)
            for k in range(1, spaces + 1):
                left, right = packed[k % spaces], packed[(spaces - k) % spaces]
                first = weight * left[0, at]
                one = one + first
                two = two + weight * left[1, at]
                far_one = far_one + float(slab * (k - 1)) * first
                first = weight * right[2, at]
                back_one = back_one + first
                back_two = back_two + weight * right[3, at]
                back_far = back_far + float(slab * (k - 1)) * first
                weight = weight * step
        around = 1.0 / (1.0 - weight)
        again = float(slab * spaces) * weight * around * around
        two = around * (two + far_one) + again * one
        one = around * one
        back_two = around * (back_two + back_far) + again * back_one
        back_one = around * back_one
        if parts > 1:
            steps = powers(rho, length, parts)
            place = lanes // width
            weight = by_block(steps, lanes, width)
            two = weight * (two + (place * length).astype(F32) * one)
            one = weight * one
            weight = by_block(steps[::-1], lanes, width)
            back_two = weight * (back_two + ((parts - 1 - place) * length).astype(F32) * back_one)
            back_one = weight * back_one
        one = one + state[0, at]
        two = two + state[1, at]
        back_one = back_one + state[2, at]
        back_two = back_two + state[3, at]
        for x in range(length):
            two = rho * (two + one)
            one = rho * one
            v_ref[x, at] = local[x, at] + (two + tilt * one)
        for x in range(length - 1, -1, -1):
            value = gain * (v_ref[x, at] + (back_two + tilt * back_one))
            v_high[x, at], v_low[x, at] = split(value)
            back_one = rho * back_one
            back_two = rho * back_two + back_one
        return carry

    lax.fori_loop(0, ny // block, correct, 0)
    pair = 2 if length % 2 == 0 else 1
    rows = ny // tests
    four = total_ref.shape[0]
    for start in range(0, length, four):
        for g in range(0, four, pair):
            right = tuple(
                jnp.concatenate([ref[start + g + k] for k in range(pair)], axis=1) for ref in (v_high, v_low)
            )
            total = dot3((c_high[...], c_low[...]), right)
            for k in range(pair):
                total_ref[g + k] = total[:, k * lanes_count : (k + 1) * lanes_count]
        if not kept:
            for g in range(four):
                for t in range(tests):
                    outs[0][t, start + g] = total_ref[g, t * rows : (t + 1) * rows]
            continue
        chips = tests // 2
        for hop in range(chips):
            for which in range(2):
                out = outs[2 * hop + which]
                at = pl.ds(pl.multiple_of(peer(meta[2], chips, hop, which) * rows, 8), rows)
                values = [total_ref[g, at] for g in range(four)]
                if hop == 0:
                    for g in range(four):
                        out[(start + g) * rows : (start + g + 1) * rows] = values[g]
                    continue
                highs = [value.astype(BF16).astype(F32) for value in values]
                rests = [value - high for value, high in zip(values, highs)]
                for g in range(0, four, 2):
                    place = (start + g) * rows
                    out[place : place + 2 * rows] = jnp.concatenate(highs[g : g + 2], axis=0).astype(BF16)
                share = width // kept
                packs = [pack_rest(rests[g : g + share], width, kept) for g in range(0, four, share)]
                place = length * rows + start * rows // share
                out[place : place + four * rows // share] = jnp.concatenate(packs, axis=0).astype(BF16)


def finish(meta, across, deep, local, state, packed, tables, parts, width, kept, tests, scale):
    length, ny, lanes = local.shape
    spaces = len(packed)
    cells = length * ny * lanes
    rows = length * (ny // tests)
    if kept:
        out = [jax.ShapeDtypeStruct((rows, lanes), F32)] * 2
        out += [jax.ShapeDtypeStruct((rows + rows * kept // width, lanes), BF16)] * (tests - 2)
    else:
        out = [jax.ShapeDtypeStruct((tests, length, ny // tests, lanes), F32)]
    return pl.pallas_call(
        functools.partial(finish_kernel, length, parts, width, kept, spaces, tests, scale),
        out_shape=tuple(out),
        in_specs=[SMEM_SPEC] + [VMEM_SPEC] * (6 + spaces),
        out_specs=(VMEM_SPEC,) * len(out),
        scratch_shapes=[
            pltpu.VMEM((length, ny, lanes), F32),
            pltpu.VMEM((length, ny, lanes), BF16),
            pltpu.VMEM((length, ny, lanes), BF16),
            pltpu.VMEM((4 if length % 4 == 0 else length, ny, lanes), F32),
        ],
        compiler_params=pltpu.CompilerParams(vmem_limit_bytes=VMEM_LIMIT),
        cost_estimate=pl.CostEstimate(flops=6 * cells * ny, bytes_accessed=16 * cells, transcendentals=0),
        name="finish",
    )(meta, across, deep, local, state, *packed, *tables)


def depth_kernel(tests, parts, depth, pieces, bd_high, bd_low, out):
    rows = pieces.shape[1]
    value = jnp.concatenate([pieces[t] for t in range(tests)], axis=1)
    result = dot3(split(value), (bd_high[...], bd_low[...]))
    for j in range(parts):
        out[j] = result[:, j * depth : (j + 1) * depth]


def depth_cells(pieces, tables, parts, depth):
    tests, rows, lanes = pieces.shape
    steps = 3 if rows % 24 == 0 else 1
    return pl.pallas_call(
        functools.partial(depth_kernel, tests, parts, depth),
        out_shape=jax.ShapeDtypeStruct((parts, rows, depth), F32),
        grid=(steps,),
        in_specs=[
            pl.BlockSpec((tests, rows // steps, lanes), lambda i: (0, i, 0)),
            pl.BlockSpec(tables[0].shape, lambda i: (0, 0)),
            pl.BlockSpec(tables[1].shape, lambda i: (0, 0)),
        ],
        out_specs=pl.BlockSpec((parts, rows // steps, depth), lambda i: (0, i, 0)),
        compiler_params=pltpu.CompilerParams(vmem_limit_bytes=VMEM_LIMIT),
        cost_estimate=pl.CostEstimate(
            flops=6 * tests * rows * lanes * parts * depth, bytes_accessed=8 * tests * rows * lanes, transcendentals=0
        ),
        name="depth_cells",
    )(pieces, *tables)


def depth_coded_kernel(tests, parts, depth, width, kept, meta, *refs):
    out = refs[-1]
    bd_high, bd_low = refs[-3:-1]
    pieces = refs[:-3]
    chips = tests // 2
    share = width // kept
    values, places = [pieces[0][...], pieces[1][...]], [meta[2], peer(meta[2], chips, 0, 1)]
    for hop in range(1, chips):
        for which in range(2):
            k = 2 + 2 * (2 * (hop - 1) + which)
            high, rest = pieces[k], pieces[k + 1]
            rows = high.shape[0] // 4
            packed = rest[...].astype(F32)
            rests = []
            for g in range(4 // share):
                rests += unpack_rest(packed[g * rows : (g + 1) * rows], share, width, kept)
            values.append(high[...].astype(F32) + jnp.concatenate(rests, axis=0))
            places.append(peer(meta[2], chips, chips - hop, which))
    lanes = values[0].shape[1]
    high, low = (
        jnp.concatenate([ref[pl.ds(pl.multiple_of(place * lanes, lanes), lanes)] for place in places], axis=0)
        for ref in (bd_high, bd_low)
    )
    result = dot3(split(jnp.concatenate(values, axis=1)), (high, low))
    for j in range(parts):
        out[j] = result[:, j * depth : (j + 1) * depth]


def depth_coded(meta, pieces, tables, tests, parts, depth, width, kept, length):
    rows, lanes = pieces[0].shape
    steps = length // 4
    block = rows // steps
    share = width // kept
    specs = [pl.BlockSpec((block, lanes), lambda i: (i, 0))] * 2
    args = list(pieces[:2])
    for piece in pieces[2:]:
        specs.append(pl.BlockSpec((block, lanes), lambda i: (i, 0)))
        specs.append(pl.BlockSpec((block // share, lanes), lambda i: (share * steps + i, 0)))
        args += [piece, piece]
    whole = pl.BlockSpec(tables[0].shape, lambda i: (0, 0))
    return pl.pallas_call(
        functools.partial(depth_coded_kernel, tests, parts, depth, width, kept),
        out_shape=jax.ShapeDtypeStruct((parts, rows, depth), F32),
        grid=(steps,),
        in_specs=[SMEM_SPEC] + specs + [whole, whole],
        out_specs=pl.BlockSpec((parts, block, depth), lambda i: (0, i, 0)),
        compiler_params=pltpu.CompilerParams(vmem_limit_bytes=VMEM_LIMIT),
        cost_estimate=pl.CostEstimate(
            flops=6 * tests * rows * lanes * parts * depth, bytes_accessed=8 * tests * rows * lanes, transcendentals=0
        ),
        name="depth_cells",
    )(meta, *args, *tables)


def on_device(log_k, heads, warm_adjoint, obs_columns, obs_residuals, well_columns):
    rows, ny, depth = log_k.shape
    spaces = lax.axis_size("space")
    tests = lax.axis_size("test")
    rank = lax.axis_index("space")
    test = lax.axis_index("test")
    chips = tests // 2
    width = depth // tests
    parts = depth // width if depth // width == 4 and rows % 4 == 0 else 1
    length = rows // parts
    lanes = depth
    count_x = rows * spaces

    w, h = warm_adjoint[0], heads[0]
    ends = (
        lax.ppermute(
            jnp.concatenate([w[rows - HALO :], log_k[rows - HALO :], h[rows - 1 :]]),
            "space", [(i, i + 1) for i in range(spaces - 1)],
        ),
        lax.ppermute(
            jnp.concatenate([w[:HALO], log_k[:HALO], h[:1]]),
            "space", [(i + 1, i) for i in range(spaces - 1)],
        ),
    )

    meta = jnp.stack([rank * rows, well_columns[0], test, rank]).astype(jnp.int32)

    fields, flats = interior(meta, log_k, w)
    _, _, fields, sums = moments(
        meta, obs_columns[0], obs_residuals[0], ends, fields, flats, rows, ny, count_x
    )
    if spaces <= 8:
        turns = [[(i, (i + k) % spaces) for i in range(spaces)] for k in range(1, spaces)]
        sums = [sums] + [lax.ppermute(sums, "space", turn) for turn in turns]
    else:
        sums = [lax.psum(sums, "space")]

    fields = fields.reshape(3, rows + 2 * HALO, ny + PAD, depth)

    cas_z = cas(depth)
    order = np.argsort(np.minimum(np.arange(depth), depth - np.arange(depth)), kind="stable")
    forward_z = np.zeros((parts, depth, tests, lanes))
    inverse_z = np.zeros((tests, lanes, parts, depth))
    kappa_z = np.zeros((tests, lanes))
    for t in range(tests):
        chosen = order[t::tests]
        for j in range(parts):
            at = slice(j * width, (j + 1) * width)
            forward_z[j, :, t, at] = cas_z[:, chosen]
            inverse_z[t, at, j, :] = cas_z[chosen, :]
            kappa_z[t, at] = kappa(depth)[chosen]
    forward_z = halves(forward_z.reshape(parts * depth, tests * lanes))
    inverse_z = halves(inverse_z.reshape(tests * lanes, parts * depth))
    deep = kappa_z.astype(np.float32)
    across = np.repeat(kappa(ny)[:, None], lanes, axis=1).astype(np.float32)
    cas_y = cas(ny)

    chunks = 2 if (ny // 2) % 48 == 0 else 1
    size = ny // chunks
    other_core = [(i, i ^ 1) for i in range(tests)]
    coded = parts > 1 and length % 4 == 0 and size % 16 == 0
    groups, fars, tables = [], [], []
    for c in range(chunks):
        mine, other = misfit(meta, sums, fields, w, h, ends, forward_z, c * size, size, parts, tests)
        if fars:
            other, fars[-1] = lax.optimization_barrier((other, fars[-1]))
        other = lax.ppermute(other, "test", other_core)
        hops = [[(i, (i + 2 * k) % tests) for i in range(tests)] for k in range(1, chips)]
        if coded:
            total, far = join(mine, other, length, width, width // 4)
            fars += [lax.ppermute(far[k], "test", hop) for k, hop in enumerate(hops)]
            far, *sums = lax.optimization_barrier((far, *sums))
        else:
            summed = mine + other
            total = summed[0]
            for k, hop in enumerate(hops, 1):
                total = total + lax.ppermute(summed[k], "test", hop)
        groups.append(total)
        tables += halves(cas_y[:, c * size : (c + 1) * size])

    local, state, packed = solve(
        meta, across, deep, groups, fars, tables, length, parts, width, width // 4
    )
    if spaces <= 8:
        wide = 0.61**rows > 1e-4
        gathered = [packed]
        for k, turn in enumerate(turns, 1):
            near = wide or k in (1, spaces - 1)
            gathered.append(lax.ppermute(packed if near else packed.astype(BF16), "space", turn))
    else:
        gathered = jnp.take(lax.all_gather(packed, "space"), (rank - jnp.arange(spaces)) % spaces, axis=0)
        gathered = [gathered[k] for k in range(spaces)]
    kept = width // 2 if coded and (ny // tests) % 8 == 0 else 0
    pieces = finish(
        meta, across, deep, local, state, gathered, halves(cas_y), parts, width, kept, tests, 1.0 / (ny * depth)
    )
    if kept:
        arrived = [pieces[0]]
        for k in range(1, tests):
            hop, which = divmod(k, 2)
            turn = [(i, 2 * ((i // 2 + hop) % chips) + (i % 2 + which) % 2) for i in range(tests)]
            arrived.append(lax.ppermute(pieces[k], "test", turn))
        result = depth_coded(meta, arrived, inverse_z, tests, parts, depth, width, kept, length)
    else:
        pieces = pieces[0].reshape(tests, length * (ny // tests), lanes)
        pieces = lax.all_to_all(pieces, "test", split_axis=0, concat_axis=0, tiled=True)
        result = depth_cells(pieces, inverse_z, parts, depth)
    return result.reshape(rows, ny // tests, depth)


def solution(mesh):
    placed = (
        P(("groups", "space"), None, None),
        P("test", ("groups", "space"), None, None),
        P("test", ("groups", "space"), None, None),
        P("test", "groups"),
        P("test", "groups", None),
        P(("groups", "test")),
    )
    return jax.shard_map(
        on_device,
        mesh=mesh,
        in_specs=placed,
        out_specs=P(("groups", "space"), "test", None),
        check_vma=False,
    )
```

```python
import functools

import jax
import jax.numpy as jnp
import ml_dtypes
import numpy as np
from jax import lax
from jax.experimental import pallas as pl
from jax.experimental.pallas import tpu as pltpu
from jax.sharding import PartitionSpec as P

prior_gain = 5.0
range_squared = 4.0

HALO = 3
PAD = 8
F32 = jnp.float32
BF16 = jnp.bfloat16
VMEM_LIMIT = 32 * 1024 * 1024
SMALL_LIMIT = 20 * 1024 * 1024
MISFIT_LIMIT = 40 * 1024 * 1024

SMEM_SPEC = pl.BlockSpec(memory_space=pltpu.SMEM)
VMEM_SPEC = pl.BlockSpec(memory_space=pltpu.VMEM)
ANY_SPEC = pl.BlockSpec(memory_space=pl.ANY)


def in_vmem(array):
    return pltpu.with_memory_space_constraint(array, pltpu.VMEM)


def in_hbm(array):
    return pltpu.with_memory_space_constraint(array, pltpu.HBM)


def cas(length):
    index = np.arange(length)
    angle = 2.0 * np.pi * (index[:, None] * index[None, :] % length) / length
    return np.cos(angle) + np.sin(angle)


def halves(table):
    table = np.asarray(table, np.float32)
    high = table.astype(ml_dtypes.bfloat16)
    low = (table - high.astype(np.float32)).astype(ml_dtypes.bfloat16)
    return high, low


def kappa(length):
    return 4.0 * np.sin(np.pi * np.arange(length) / length) ** 2


def split(value):
    high = value.astype(BF16)
    low = (value - high.astype(F32)).astype(BF16)
    return high, low


def dot(left, right):
    return lax.dot_general(left, right, (((1,), (0,)), ((), ())), preferred_element_type=F32)


def dot3(left, right):
    return dot(left[0], right[0]) + (dot(left[0], right[1]) + dot(left[1], right[0]))


def block_rows(count):
    for rows in (48, 32, 16):
        if count % rows == 0:
            return rows
    return count


def unrolled(start, stop, body, carry, most=4):
    count = stop - start
    factor = next(f for f in range(most, 0, -1) if count % f == 0)
    return lax.fori_loop(start, stop, body, carry, unroll=factor)


def lane_index(shape):
    return lax.broadcasted_iota(jnp.int32, shape, 1)


def window(ref, start, rows):
    return ref.at[pl.ds(pl.multiple_of(start - PAD, 8), rows + 2 * PAD)]


def neighbour_sum(ref, start, rows, plane, fill):
    near = window(ref, start, rows)
    here = near[PAD : PAD + rows]
    lanes = lane_index(here.shape)
    depth = here.shape[1]
    up = jnp.where(lanes == depth - 1, fill, pltpu.roll(here, depth - 1, 1))
    down = jnp.where(lanes == 0, fill, pltpu.roll(here, 1, 1))
    along = ref[pl.ds(pl.multiple_of(start - plane, 8), rows)] + ref[pl.ds(pl.multiple_of(start + plane, 8), rows)]
    across = near[PAD - 1 : PAD - 1 + rows] + near[PAD + 1 : PAD + 1 + rows]
    return along + across + (up + down), here


def fold(value):
    return jnp.sum(value.reshape(-1, 8, value.shape[1]), axis=0)


def field_rows(rows, ny):
    return (rows + 2 * HALO) * (ny + PAD) + PAD


def scale_plane(e_ref, u_ref, p, ny, size, lk_of, w_of):
    base = p * (ny + PAD) + PAD
    for b in range(0, ny, size):
        e = jnp.exp(0.5 * lk_of(b).astype(F32))
        at = pl.ds(pl.multiple_of(base + b, 8), size)
        e_ref[at] = e
        u_ref[at] = e * w_of(b).astype(F32)


def residual_plane(e_ref, u_ref, s_ref, r_ref, v_ref, p, ny, size, valid):
    plane = ny + PAD
    for b in range(0, ny, size):
        start = p * plane + PAD + b
        at = pl.ds(pl.multiple_of(start, 8), size)
        flat = pl.ds(pl.multiple_of(p * ny + b, 8), size)
        s, e = neighbour_sum(e_ref, start, size, plane, 1.0)
        n, u = neighbour_sum(u_ref, start, size, plane, 0.0)
        r = e * n - s * u
        if valid is not None:
            r = r * valid
        s_ref[flat] = s
        r_ref[flat] = r
        v_ref[at] = e * r


def thirds(ref):
    count = ref.shape[0] // 3
    return tuple(ref.at[pl.ds(k * count, count)] for k in range(3))


def halved(ref):
    count = ref.shape[0] // 2
    return tuple(ref.at[pl.ds(k * count, count)] for k in range(2))


def interior_kernel(rows, ny, pieces, meta, lk_in, w_in, fields, flats, lk, w, sems):
    e_ref, u_ref, v_ref = thirds(fields)
    s_ref, r_ref = halved(flats)
    depth = lk.shape[2]
    plane = ny + PAD
    planes = rows + 2 * HALO
    size = block_rows(ny)
    count = rows // pieces
    copies = []
    for piece in range(pieces):
        at = pl.ds(piece * count, count)
        for k, (source, target) in enumerate(((lk_in, lk), (w_in, w))):
            copies.append(pltpu.make_async_copy(source.at[at], target.at[at], sems.at[2 * piece + k]))
    for copy in copies:
        copy.start()
    ones = jnp.ones((PAD, depth), F32)
    zeros = jnp.zeros((PAD, depth), F32)

    def clear(p, carry):
        at = pl.ds(pl.multiple_of(p * plane, 8), PAD)
        e_ref[at] = ones
        u_ref[at] = zeros
        v_ref[at] = zeros
        return carry

    lax.fori_loop(0, planes + 1, clear, 0)

    def scale(x, carry):
        scale_plane(
            e_ref, u_ref, x + HALO, ny, size, lambda b: lk[x, b : b + size], lambda b: w[x, b : b + size]
        )
        return carry

    for piece in range(pieces):
        copies[2 * piece].wait()
        copies[2 * piece + 1].wait()
        unrolled(piece * count, (piece + 1) * count, scale, 0)

    def residual(p, carry):
        residual_plane(e_ref, u_ref, s_ref, r_ref, v_ref, p, ny, size, None)
        return carry

    unrolled(HALO + 1, HALO + rows - 1, residual, 0)


def interior(meta, lk, w):
    rows, ny, depth = lk.shape
    fields = pltpu.VMEM((3 * field_rows(rows, ny), depth), F32)
    flats = pltpu.VMEM((2 * (rows + 2 * HALO) * ny, depth), F32)
    cells = rows * ny * depth
    pieces = next(k for k in (4, 3, 2, 1) if rows % k == 0)
    return pl.pallas_call(
        functools.partial(interior_kernel, rows, ny, pieces),
        out_shape=(fields, flats),
        in_specs=[SMEM_SPEC] + [ANY_SPEC] * 2,
        out_specs=(VMEM_SPEC,) * 2,
        scratch_shapes=[
            pltpu.VMEM((rows, ny, depth), BF16),
            pltpu.VMEM((rows, ny, depth), BF16),
            pltpu.SemaphoreType.DMA((2 * pieces,)),
        ],
        compiler_params=pltpu.CompilerParams(vmem_limit_bytes=SMALL_LIMIT),
        cost_estimate=pl.CostEstimate(flops=5000 * cells, bytes_accessed=4 * cells, transcendentals=cells),
        name="interior",
    )(meta, in_hbm(lk), in_hbm(w))


def moments_kernel(
    rows, ny, count_x,
    meta, columns, residuals, ends_low, ends_high, fields_in, flats_in,
    fields, flats, held_out, mom_out, sems,
):
    e_ref, u_ref, v_ref = thirds(fields)
    s_ref, r_ref = halved(flats)
    holds = [
        pltpu.make_async_copy(ref.at[pl.ds(0, held_out.shape[1])], held_out.at[k], sems.at[k])
        for k, ref in enumerate((e_ref, u_ref, v_ref))
    ]
    depth = residuals.shape[1]
    plane = ny + PAD
    planes = rows + 2 * HALO
    size = block_rows(ny)
    blocks = range(0, ny, size)
    first_row = meta[0]

    for ends, begin in ((ends_low, 0), (ends_high, HALO + rows)):

        def scale(p, carry):
            scale_plane(
                e_ref, u_ref, p + begin, ny, size,
                lambda b: ends[HALO + p, b : b + size], lambda b: ends[p, b : b + size],
            )
            return carry

        unrolled(0, HALO, scale, 0)

    def inside(p):
        row = first_row + p - HALO
        return jnp.where((row >= 0) & (row < count_x), 1.0, 0.0).astype(F32)

    def residual(p, carry):
        residual_plane(e_ref, u_ref, s_ref, r_ref, v_ref, p, ny, size, inside(p))
        return carry

    unrolled(1, HALO + 1, residual, 0)
    unrolled(HALO + rows - 1, planes - 1, residual, 0)

    def plant(o, carry):
        column = columns[o] - (first_row - HALO) * ny

        @pl.when((column >= ny) & (column < (planes - 1) * ny))
        def _():
            p = lax.div(column, ny)
            y = column - p * ny
            at = pl.ds(p * plane + PAD + y, 1)
            flat = pl.ds(p * ny + y, 1)
            added = residuals[pl.ds(o, 1)]
            r_ref[flat] = r_ref[flat] + added
            v_ref[at] = v_ref[at] + e_ref[at] * added

        return carry

    holds[0].start()
    lax.fori_loop(0, columns.shape[0], plant, 0)
    holds[2].start()

    def image(p, sums, valid, summed):
        m0, m1, m2 = sums
        base = p * plane + PAD
        for b in blocks:
            start = base + b
            at = pl.ds(pl.multiple_of(start, 8), size)
            flat = pl.ds(pl.multiple_of(p * ny + b, 8), size)
            n, v = neighbour_sum(v_ref, start, size, plane, 0.0)
            e = e_ref[at]
            y = s_ref[flat] * v - e * n
            if valid is not None:
                y = y * valid
            u_ref[at] = e * y
            if summed:
                r = r_ref[flat]
                m0 = m0 + fold(r * r)
                m1 = m1 + fold(r * y)
                m2 = m2 + fold(y * y)
                r_ref[flat] = y
        return m0, m1, m2

    zero = jnp.zeros((8, depth), F32)
    sums = (zero, zero, zero)
    image(HALO - 1, sums, inside(HALO - 1), False)
    image(HALO + rows, sums, inside(HALO + rows), False)
    m0, m1, m2 = unrolled(HALO, HALO + rows, lambda p, c: image(p, c, None, True), sums)

    holds[1].start()

    def second(p, m3):
        base = p * plane + PAD
        for b in blocks:
            start = base + b
            flat = pl.ds(pl.multiple_of(p * ny + b, 8), size)
            near = window(u_ref, start, size)
            q = near[PAD : PAD + size]
            up = jnp.where(lane_index(q.shape) == depth - 1, 0.0, pltpu.roll(q, depth - 1, 1))
            ahead = u_ref[pl.ds(pl.multiple_of(start + plane, 8), size)] + near[PAD + 1 : PAD + 1 + size] + up
            m3 = m3 + fold(q * (s_ref[flat] * r_ref[flat] - 2.0 * ahead))
        return m3

    m3 = unrolled(HALO, HALO + rows, second, zero)
    for k, m in enumerate((m0, m1, m2, m3)):
        mom_out[k] = jnp.sum(m)
    for hold in holds:
        hold.wait()


def moments(meta, columns, residuals, ends, fields, flats, rows, ny, count_x):
    depth = residuals.shape[1]
    cells = rows * ny * depth
    return pl.pallas_call(
        functools.partial(moments_kernel, rows, ny, count_x),
        out_shape=(
            pltpu.VMEM(fields.shape, F32), pltpu.VMEM(flats.shape, F32),
            jax.ShapeDtypeStruct((3, fields.shape[0] // 3 - PAD, depth), F32), jax.ShapeDtypeStruct((4,), F32),
        ),
        in_specs=[SMEM_SPEC, SMEM_SPEC] + [VMEM_SPEC] * 5,
        out_specs=(VMEM_SPEC,) * 2 + (ANY_SPEC, SMEM_SPEC),
        input_output_aliases={5: 0, 6: 1},
        scratch_shapes=[pltpu.SemaphoreType.DMA((3,))],
        compiler_params=pltpu.CompilerParams(vmem_limit_bytes=SMALL_LIMIT),
        cost_estimate=pl.CostEstimate(flops=5000 * cells, bytes_accessed=4 * cells, transcendentals=cells),
        name="moments",
    )(meta, columns, residuals, *ends, in_vmem(fields), in_vmem(flats))


def step_lengths(sums):
    m0, m1, m2, m3 = (sum(ref[k] for ref in sums) for k in range(4))
    alpha = m0 / m1
    new = alpha * alpha * m2 - 2.0 * alpha * m1 + m0
    bent = 1.0 + new / m0
    second = new / (bent * bent * m1 - 2.0 * bent * alpha * m2 + alpha * alpha * m3)
    return alpha + second * bent, -second * alpha


def misfit_kernel(rows, ny, first, size, parts, tests, terms, meta, *refs):
    sums = refs[:terms]
    (
        fields, w, h, ends_low, ends_high, bd_high, bd_low,
        mine_out, other_out, e_ref, q_ref, v_ref, w_ref, h_bf, a_ref, h_ref, x_ref, t_high, t_low, sems,
    ) = refs[terms:]
    depth = w.shape[2]
    length = rows // parts
    plane = ny + PAD
    slot_rows = size + 2 * PAD
    edge = 16
    low = edge if first > 0 else 0
    high = edge if first + size < ny else 0
    held = PAD + size + (PAD if high else 0)
    cuts = misfit_cuts(length, parts)
    sem = iter(range(sems.shape[0]))
    waits = [[] for _ in cuts[1:]]

    def bring(source, target, group):
        copy = pltpu.make_async_copy(source, target, sems.at[next(sem)])
        copy.start()
        waits[group].append(copy)

    def bring_rows(group, begin, end):
        count = end - begin
        for k, ref in enumerate((e_ref, q_ref, v_ref)):
            bring(
                fields.at[k, pl.ds(begin + HALO - 1, count), pl.ds(first, held)],
                ref.at[pl.ds(begin, count), pl.ds(0, held)],
                group,
            )
        ys, yt = pl.ds(first - low, low + size + high), pl.ds(edge - low, low + size + high)
        for source, below, above, ref in ((w, HALO - 1, 0, w_ref), (h, 2 * HALO, 2 * HALO, h_bf)):
            lo, hi = begin, end
            if lo == 0:
                bring(ends_low.at[pl.ds(below, 1), ys], ref.at[pl.ds(0, 1), yt], group)
                lo = 1
            if hi == rows + 2:
                bring(ends_high.at[pl.ds(above, 1), ys], ref.at[pl.ds(rows + 1, 1), yt], group)
                hi = rows + 1
            if hi > lo:
                bring(source.at[pl.ds(lo - 1, hi - lo), ys], ref.at[pl.ds(lo, hi - lo), yt], group)

    def bring_group(group):
        for part in range(parts):
            end = cuts[group + 1]
            if part == parts - 1 and end == length:
                end = length + 2
            bring_rows(group, part * length + cuts[group], part * length + end)

    for group in range(min(2, len(waits))):
        bring_group(group)
    block = size if size % 16 == 0 else block_rows(size)
    blocks = range(0, size, block)
    first_row, well = meta[0], meta[1]
    c0, c1 = step_lengths(sums)
    lanes_out = mine_out.shape[2]
    chips = tests // 2
    chip, core = meta[2] // 2, meta[2] % 2

    if first + size == ny:
        beyond = jnp.ones((PAD, depth), F32)

        def fill(p, carry):
            e_ref[p, pl.ds(PAD + size, PAD)] = beyond
            return carry

        lax.fori_loop(0, rows + 2, fill, 0)
    zeros = jnp.zeros((PAD, depth), F32)
    for s in range(4 * parts):
        for at in (pl.ds(s * slot_rows, PAD), pl.ds(s * slot_rows + PAD + size, PAD)):
            a_ref[at] = zeros
            h_ref[at] = zeros

    def slot(part, i):
        return (4 * part + lax.rem(i, 4)) * slot_rows

    spans = [(b, block, 0, block) for b in blocks]
    if low:
        spans.append((-edge, edge, PAD, PAD))
    if high:
        spans.append((size, edge, 0, PAD))

    def prepare(part, i):
        base = slot(part, i)
        p = part * length + i
        for y, count, skip, keep in spans:
            at = slice(PAD + y + skip, PAD + y + skip + keep)
            to = pl.ds(pl.multiple_of(base + PAD + y + skip, 8), keep)
            wide = w_ref[p, edge + y : edge + y + count].astype(F32)[skip : skip + keep]
            a_ref[to] = e_ref[p, at] * wide + c0 * v_ref[p, at] + c1 * q_ref[p, at]
            h_ref[to] = h_bf[p, edge + y : edge + y + count].astype(F32)[skip : skip + keep]

    def rows_at(start, count):
        return pl.ds(pl.multiple_of(start, 8), count)

    def along(part):
        for b in blocks:
            at = rows_at(slot(part, 0) + PAD + b, block)
            to = rows_at(slot(part, 1) + PAD + b, block)
            e = e_ref[part * length, PAD + b : PAD + b + block]
            en = e_ref[part * length + 1, PAD + b : PAD + b + block]
            x_ref[part, b : b + block] = (en * a_ref[at] - e * a_ref[to]) * (h_ref[at] - h_ref[to])

    def centre(part, x, buffer):
        here, there = slot(part, x + 1), slot(part, x + 2)
        p = part * length + x + 1
        column = (first_row + part * length + x) * ny + first
        for b in blocks:
            to = rows_at(there + PAD + b, block)
            e_near = e_ref.at[p, b : b + block + 2 * PAD]
            a_near, h_near = (window(ref, here + PAD + b, block) for ref in (a_ref, h_ref))
            mid = slice(PAD, PAD + block)
            e, a, hh = e_near[mid], a_near[mid], h_near[mid]
            en, an, hn = e_ref[p + 1, PAD + b : PAD + b + block], a_ref[to], h_ref[to]
            before = x_ref[part, b : b + block]
            after = (en * a - e * an) * (hh - hn)
            x_ref[part, b : b + block] = after
            total = before + after
            for shift in (-1, 1):
                at = slice(PAD + shift, PAD + shift + block)
                en, an, hn = e_near[at], a_near[at], h_near[at]
                total = total + (en * a - e * an) * (hh - hn)
            lanes = lane_index(e.shape)
            end = lanes == depth - 1
            en = jnp.where(end, 1.0, pltpu.roll(e, depth - 1, 1))
            an = jnp.where(end, 0.0, pltpu.roll(a, depth - 1, 1))
            hn = jnp.where(end, 0.0, pltpu.roll(hh, depth - 1, 1))
            up = (en * a - e * an) * (hh - hn)
            down = jnp.where(lanes == 0, a * hh, pltpu.roll(up, 1, 1))
            total = -0.5 * (total + up + down)
            row = lax.broadcasted_iota(jnp.int32, e.shape, 0) + (column + b)
            total = jnp.where(row == well, 0.0, total)
            high_part, low_part = split(total)
            t_high[buffer, b : b + block, part * depth : (part + 1) * depth] = high_part
            t_low[buffer, b : b + block, part * depth : (part + 1) * depth] = low_part

    def transform(x, buffer):
        value = dot3((t_high[buffer], t_low[buffer]), (bd_high[...], bd_low[...]))
        at = rows_at(x * size, size)
        for c in range(chips):
            even, odd = (value[:, (2 * c + k) * lanes_out : (2 * c + k + 1) * lanes_out] for k in range(2))
            k = lax.rem(c + chips - chip, chips)
            mine_out[k, at] = jnp.where(core == 0, even, odd)
            other_out[k, at] = jnp.where(core == 0, odd, even)

    def step(x):
        for part in range(parts):
            prepare(part, x + 2)
        for part in range(parts):
            centre(part, x, lax.rem(x, 2))

    def loop(x, carry):
        transform(x - 1, lax.rem(x + 1, 2))
        step(x)
        return carry

    done = 0
    for group in range(len(waits)):
        for copy in waits[group]:
            copy.wait()
        if group + 2 < len(waits):
            bring_group(group + 2)
        if group == 0:
            for part in range(parts):
                prepare(part, 0)
                prepare(part, 1)
                along(part)
            step(0)
            done = 1
        ready = length if group == len(waits) - 1 else cuts[group + 1] - 2
        if ready > done:
            lax.fori_loop(done, ready, loop, 0)
            done = ready
    transform(length - 1, (length - 1) % 2)


def misfit_cuts(length, parts):
    if parts == 1 or length <= 4:
        return [0, length]
    return list(range(0, length - 2, 3)) + [length]


def misfit(meta, sums, fields, w, h, ends, tables, first, size, parts, tests):
    rows, ny, depth = w.shape
    length = rows // parts
    lanes = tables[0].shape[1] // tests
    out = jax.ShapeDtypeStruct((tests // 2, length * size, lanes), F32)
    ring = pltpu.VMEM((4 * parts * (size + 2 * PAD), depth), F32)
    full = pltpu.VMEM((rows + 2, size + 2 * PAD, depth), F32)
    half = pltpu.VMEM((rows + 2, size + 32, depth), BF16)
    cells = rows * size * depth
    return pl.pallas_call(
        functools.partial(misfit_kernel, rows, ny, first, size, parts, tests, len(sums)),
        out_shape=(out, out),
        in_specs=[SMEM_SPEC] * (1 + len(sums)) + [ANY_SPEC] * 5 + [VMEM_SPEC] * 2,
        out_specs=(VMEM_SPEC, VMEM_SPEC),
        scratch_shapes=[
            full, full, full, half, half, ring, ring,
            pltpu.VMEM((parts, size, depth), F32),
            pltpu.VMEM((2, size, parts * depth), BF16),
            pltpu.VMEM((2, size, parts * depth), BF16),
            pltpu.SemaphoreType.DMA((5 * parts * (len(misfit_cuts(length, parts)) - 1) + 4,)),
        ],
        compiler_params=pltpu.CompilerParams(vmem_limit_bytes=MISFIT_LIMIT),
        cost_estimate=pl.CostEstimate(flops=8000 * cells, bytes_accessed=4 * cells, transcendentals=cells),
        name="misfit",
    )(meta, *sums, in_hbm(fields), in_hbm(w), in_hbm(h), *ends, *tables)


def pack_rest(rests, width, kept):
    lanes = lane_index(rests[0].shape) % width
    result = rests[0]
    for m in range(1, len(rests)):
        moved = pltpu.roll(rests[m], m * kept, 1)
        result = jnp.where((lanes >= m * kept) & (lanes < (m + 1) * kept), moved, result)
    return result


def unpack_rest(packed, count, width, kept):
    near = lane_index(packed.shape) % width < kept
    depth = packed.shape[1]
    return [
        jnp.where(near, packed if m == 0 else pltpu.roll(packed, depth - m * kept, 1), 0.0) for m in range(count)
    ]


def join_kernel(length, width, kept, mine, other, own_out, far_out):
    far_count, rows = mine.shape[0] - 1, mine.shape[1]
    size = rows // length
    share = width // kept
    block = block_rows(size)

    def add(i, carry):
        at = pl.ds(pl.multiple_of(i * size, 16), size)
        own_out[at] = mine[0, at] + other[0, at]
        return carry

    lax.fori_loop(0, length, add, 0)
    for f in range(far_count):

        def code(i, carry):
            for b in range(0, size, block):
                rests = []
                for m in range(share):
                    at = pl.ds(pl.multiple_of((i * share + m) * size + b, 16), block)
                    value = mine[1 + f, at] + other[1 + f, at]
                    high = value.astype(BF16)
                    far_out[f, at] = high
                    rests.append(value - high.astype(F32))
                at = pl.ds(pl.multiple_of(rows + i * size + b, 16), block)
                far_out[f, at] = pack_rest(rests, width, kept).astype(BF16)
            return carry

        lax.fori_loop(0, length // share, code, 0)


def join(mine, other, length, width, kept):
    chips, rows, lanes = mine.shape
    return pl.pallas_call(
        functools.partial(join_kernel, length, width, kept),
        out_shape=(
            jax.ShapeDtypeStruct((rows, lanes), F32),
            jax.ShapeDtypeStruct((chips - 1, rows + rows * kept // width, lanes), BF16),
        ),
        in_specs=[VMEM_SPEC] * 2,
        out_specs=(VMEM_SPEC,) * 2,
        compiler_params=pltpu.CompilerParams(vmem_limit_bytes=VMEM_LIMIT),
        cost_estimate=pl.CostEstimate(flops=4 * rows * lanes, bytes_accessed=16 * rows * lanes, transcendentals=0),
        name="join",
    )(mine, other)


def power(value, exponent):
    result = None
    while exponent:
        if exponent & 1:
            result = value if result is None else result * value
        exponent >>= 1
        if exponent:
            value = value * value
    return result


def ratio_of(across, deep):
    half = (1.0 + range_squared * (across + deep) + 2.0 * range_squared) / (2.0 * range_squared)
    return 1.0 / (half + jnp.sqrt(half * half - 1.0))


def by_block(values, lanes, width):
    result = values[-1]
    for j in range(len(values) - 2, -1, -1):
        result = jnp.where(lanes < (j + 1) * width, values[j], result)
    return result


def powers(value, length, count):
    step = power(value, length)
    result = [jnp.ones_like(value)]
    for _ in range(count - 1):
        result.append(result[-1] * step)
    return result


def everywhere(value, width):
    lanes = value.shape[1]
    shift = width
    while shift < lanes:
        value = value + pltpu.roll(value, shift, 1)
        shift *= 2
    return value


def solve_kernel(length, parts, width, kept, chunks, fars, meta, across, deep, *refs):
    groups = refs[:chunks]
    far_refs = refs[chunks : chunks * (1 + fars)]
    tables = refs[chunks * (1 + fars) : chunks * (3 + fars)]
    local_out, state_out, packed_out, h_ref = refs[chunks * (3 + fars) :]
    ny, lanes_count = across.shape
    size = groups[0].shape[0] // length
    pair = 2 if length % 2 == 0 else 1
    share = width // kept
    rests = {}

    def gathered(c, x):
        at = slice(x * size, (x + 1) * size)
        value = groups[c][at]
        for f in range(fars):
            ref = far_refs[c * fars + f]
            g = x // share
            if (c, f, g) not in rests:
                start = length * size + g * size
                rests[c, f, g] = unpack_rest(ref[start : start + size].astype(F32), share, width, kept)
            value = value + (ref[at].astype(F32) + rests[c, f, g][x % share])
        return value

    for g in range(0, length, pair):
        total = None
        for c in range(chunks):
            value = jnp.concatenate([gathered(c, g + k) for k in range(pair)], axis=1)
            product = dot3((tables[2 * c][...], tables[2 * c + 1][...]), split(value))
            total = product if total is None else total + product
        for k in range(pair):
            h_ref[g + k] = total[:, k * lanes_count : (k + 1) * lanes_count]

    block = block_rows(ny)
    qz = deep[pl.ds(meta[2], 1)]

    def solve(i, carry):
        at = pl.ds(pl.multiple_of(i * block, 16), block)
        rho = ratio_of(across[at], qz)
        square = rho * rho
        tilt = (1.0 + square) / (1.0 - square)
        p1 = jnp.zeros_like(rho)
        p2 = jnp.zeros_like(rho)
        for x in range(length):
            p2 = rho * (p2 + p1)
            p1 = h_ref[x, at] + rho * p1
            local_out[x, at] = p2 + tilt * p1
        n1 = jnp.zeros_like(rho)
        n2 = jnp.zeros_like(rho)
        for x in range(length - 1, -1, -1):
            local_out[x, at] = local_out[x, at] + (n2 + tilt * n1)
            n1 = rho * (n1 + h_ref[x, at])
            n2 = rho * n2 + n1
        if parts == 1:
            for k, value in enumerate((p1, p2, n1, n2)):
                state_out[k, at] = jnp.zeros_like(rho)
                packed_out[k, at] = value
            return carry
        lanes = lane_index(rho.shape)
        steps = powers(rho, length, parts)
        zero = jnp.zeros_like(rho)
        into = [zero] * 4
        for s in range(1, parts):
            weight = jnp.where(lanes >= s * width, steps[s - 1], 0.0)
            far = float(length * (s - 1))
            one, two = (pltpu.roll(value, s * width, 1) for value in (p1, p2))
            into[0] = into[0] + weight * one
            into[1] = into[1] + weight * (two + far * one)
            weight = jnp.where(lanes < (parts - s) * width, steps[s - 1], 0.0)
            one, two = (pltpu.roll(value, lanes_count - s * width, 1) for value in (n1, n2))
            into[2] = into[2] + weight * one
            into[3] = into[3] + weight * (two + far * one)
        for k in range(4):
            state_out[k, at] = into[k]
        place = lanes // width
        weight = by_block(steps[::-1], lanes, width)
        far = ((parts - 1 - place) * length).astype(F32)
        d1 = everywhere(weight * p1, width)
        d2 = everywhere(weight * (p2 + far * p1), width)
        weight = by_block(steps, lanes, width)
        far = (place * length).astype(F32)
        e1 = everywhere(weight * n1, width)
        e2 = everywhere(weight * (n2 + far * n1), width)
        packed_out[at] = by_block([d1, d2, e1, e2], lanes, width)
        return carry

    lax.fori_loop(0, ny // block, solve, 0)


def solve(meta, across, deep, groups, fars, tables, length, parts, width, kept):
    ny, lanes = across.shape
    chunks = len(groups)
    packed = (ny, lanes) if parts == 4 else (4, ny, lanes)
    cells = length * ny * lanes
    return pl.pallas_call(
        functools.partial(solve_kernel, length, parts, width, kept, chunks, len(fars) // chunks),
        out_shape=(
            jax.ShapeDtypeStruct((length, ny, lanes), F32),
            jax.ShapeDtypeStruct((4, ny, lanes), F32),
            jax.ShapeDtypeStruct(packed, F32),
        ),
        in_specs=[SMEM_SPEC] + [VMEM_SPEC] * (2 + 3 * chunks + len(fars)),
        out_specs=(VMEM_SPEC,) * 3,
        scratch_shapes=[pltpu.VMEM((length, ny, lanes), F32)],
        compiler_params=pltpu.CompilerParams(vmem_limit_bytes=VMEM_LIMIT),
        cost_estimate=pl.CostEstimate(flops=6 * cells * ny, bytes_accessed=16 * cells, transcendentals=0),
        name="solve",
    )(meta, across, deep, *groups, *fars, *tables)


def peer(test, chips, hop, which):
    return 2 * lax.rem(test // 2 + hop, chips) + lax.rem(test % 2 + which, 2)


def finish_kernel(length, parts, width, kept, spaces, tests, scale, meta, across, deep, local, state, *refs):
    packed = refs[:spaces]
    c_high, c_low, *outs = refs[spaces : -4]
    v_ref, v_high, v_low, total_ref = refs[-4:]
    ny, lanes_count = across.shape
    block = block_rows(ny)
    qz = deep[pl.ds(meta[2], 1)]
    slab = length * parts

    def correct(i, carry):
        at = pl.ds(pl.multiple_of(i * block, 16), block)
        rho = ratio_of(across[at], qz)
        square = rho * rho
        tilt = (1.0 + square) / (1.0 - square)
        gain = rho / (2.0 * range_squared * 0.5 * (1.0 - square))
        gain = (prior_gain * scale) * gain * gain
        lanes = lane_index(rho.shape)
        step = power(rho, slab)
        weight = jnp.ones_like(rho)
        if parts > 1:
            near = far = jnp.zeros_like(rho)
            for k in range(1, spaces + 1):
                left = packed[k % spaces][at].astype(F32)
                right = packed[(spaces - k) % spaces][at].astype(F32)
                value = weight * jnp.where(lanes < 2 * width, left, right)
                near = near + value
                far = far + float(slab * (k - 1)) * value
                weight = weight * step

            def pick(value, s):
                return everywhere(jnp.where((lanes >= s * width) & (lanes < (s + 1) * width), value, 0.0), width)

            one, two, far_one = pick(near, 0), pick(near, 1), pick(far, 0)
            back_one, back_two, back_far = pick(near, 2), pick(near, 3), pick(far, 2)
        else:
            one = two = far_one = back_one = back_two = back_far = jnp.zeros_like(rho)
            for k in range(1, spaces + 1):
                left, right = packed[k % spaces], packed[(spaces - k) % spaces]
                first = weight * left[0, at]
                one = one + first
                two = two + weight * left[1, at]
                far_one = far_one + float(slab * (k - 1)) * first
                first = weight * right[2, at]
                back_one = back_one + first
                back_two = back_two + weight * right[3, at]
                back_far = back_far + float(slab * (k - 1)) * first
                weight = weight * step
        around = 1.0 / (1.0 - weight)
        again = float(slab * spaces) * weight * around * around
        two = around * (two + far_one) + again * one
        one = around * one
        back_two = around * (back_two + back_far) + again * back_one
        back_one = around * back_one
        if parts > 1:
            steps = powers(rho, length, parts)
            place = lanes // width
            weight = by_block(steps, lanes, width)
            two = weight * (two + (place * length).astype(F32) * one)
            one = weight * one
            weight = by_block(steps[::-1], lanes, width)
            back_two = weight * (back_two + ((parts - 1 - place) * length).astype(F32) * back_one)
            back_one = weight * back_one
        one = one + state[0, at]
        two = two + state[1, at]
        back_one = back_one + state[2, at]
        back_two = back_two + state[3, at]
        for x in range(length):
            two = rho * (two + one)
            one = rho * one
            v_ref[x, at] = local[x, at] + (two + tilt * one)
        for x in range(length - 1, -1, -1):
            value = gain * (v_ref[x, at] + (back_two + tilt * back_one))
            v_high[x, at], v_low[x, at] = split(value)
            back_one = rho * back_one
            back_two = rho * back_two + back_one
        return carry

    lax.fori_loop(0, ny // block, correct, 0)
    pair = 2 if length % 2 == 0 else 1
    rows = ny // tests
    four = total_ref.shape[0]
    for start in range(0, length, four):
        for g in range(0, four, pair):
            right = tuple(
                jnp.concatenate([ref[start + g + k] for k in range(pair)], axis=1) for ref in (v_high, v_low)
            )
            total = dot3((c_high[...], c_low[...]), right)
            for k in range(pair):
                total_ref[g + k] = total[:, k * lanes_count : (k + 1) * lanes_count]
        if not kept:
            for g in range(four):
                for t in range(tests):
                    outs[0][t, start + g] = total_ref[g, t * rows : (t + 1) * rows]
            continue
        chips = tests // 2
        for hop in range(chips):
            for which in range(2):
                out = outs[2 * hop + which]
                at = pl.ds(pl.multiple_of(peer(meta[2], chips, hop, which) * rows, 8), rows)
                values = [total_ref[g, at] for g in range(four)]
                if hop == 0:
                    for g in range(four):
                        out[(start + g) * rows : (start + g + 1) * rows] = values[g]
                    continue
                highs = [value.astype(BF16).astype(F32) for value in values]
                rests = [value - high for value, high in zip(values, highs)]
                for g in range(0, four, 2):
                    place = (start + g) * rows
                    out[place : place + 2 * rows] = jnp.concatenate(highs[g : g + 2], axis=0).astype(BF16)
                share = width // kept
                packs = [pack_rest(rests[g : g + share], width, kept) for g in range(0, four, share)]
                place = length * rows + start * rows // share
                out[place : place + four * rows // share] = jnp.concatenate(packs, axis=0).astype(BF16)


def finish(meta, across, deep, local, state, packed, tables, parts, width, kept, tests, scale):
    length, ny, lanes = local.shape
    spaces = len(packed)
    cells = length * ny * lanes
    rows = length * (ny // tests)
    if kept:
        out = [jax.ShapeDtypeStruct((rows, lanes), F32)] * 2
        out += [jax.ShapeDtypeStruct((rows + rows * kept // width, lanes), BF16)] * (tests - 2)
    else:
        out = [jax.ShapeDtypeStruct((tests, length, ny // tests, lanes), F32)]
    return pl.pallas_call(
        functools.partial(finish_kernel, length, parts, width, kept, spaces, tests, scale),
        out_shape=tuple(out),
        in_specs=[SMEM_SPEC] + [VMEM_SPEC] * (6 + spaces),
        out_specs=(VMEM_SPEC,) * len(out),
        scratch_shapes=[
            pltpu.VMEM((length, ny, lanes), F32),
            pltpu.VMEM((length, ny, lanes), BF16),
            pltpu.VMEM((length, ny, lanes), BF16),
            pltpu.VMEM((4 if length % 4 == 0 else length, ny, lanes), F32),
        ],
        compiler_params=pltpu.CompilerParams(vmem_limit_bytes=VMEM_LIMIT),
        cost_estimate=pl.CostEstimate(flops=6 * cells * ny, bytes_accessed=16 * cells, transcendentals=0),
        name="finish",
    )(meta, across, deep, local, state, *packed, *tables)


def depth_kernel(tests, parts, depth, pieces, bd_high, bd_low, out):
    rows = pieces.shape[1]
    value = jnp.concatenate([pieces[t] for t in range(tests)], axis=1)
    result = dot3(split(value), (bd_high[...], bd_low[...]))
    for j in range(parts):
        out[j] = result[:, j * depth : (j + 1) * depth]


def depth_cells(pieces, tables, parts, depth):
    tests, rows, lanes = pieces.shape
    steps = 3 if rows % 24 == 0 else 1
    return pl.pallas_call(
        functools.partial(depth_kernel, tests, parts, depth),
        out_shape=jax.ShapeDtypeStruct((parts, rows, depth), F32),
        grid=(steps,),
        in_specs=[
            pl.BlockSpec((tests, rows // steps, lanes), lambda i: (0, i, 0)),
            pl.BlockSpec(tables[0].shape, lambda i: (0, 0)),
            pl.BlockSpec(tables[1].shape, lambda i: (0, 0)),
        ],
        out_specs=pl.BlockSpec((parts, rows // steps, depth), lambda i: (0, i, 0)),
        compiler_params=pltpu.CompilerParams(vmem_limit_bytes=VMEM_LIMIT),
        cost_estimate=pl.CostEstimate(
            flops=6 * tests * rows * lanes * parts * depth, bytes_accessed=8 * tests * rows * lanes, transcendentals=0
        ),
        name="depth_cells",
    )(pieces, *tables)


def depth_coded_kernel(tests, parts, depth, width, kept, meta, *refs):
    out = refs[-1]
    bd_high, bd_low = refs[-3:-1]
    pieces = refs[:-3]
    chips = tests // 2
    share = width // kept
    values, places = [pieces[0][...], pieces[1][...]], [meta[2], peer(meta[2], chips, 0, 1)]
    for hop in range(1, chips):
        for which in range(2):
            k = 2 + 2 * (2 * (hop - 1) + which)
            high, rest = pieces[k], pieces[k + 1]
            rows = high.shape[0] // 4
            packed = rest[...].astype(F32)
            rests = []
            for g in range(4 // share):
                rests += unpack_rest(packed[g * rows : (g + 1) * rows], share, width, kept)
            values.append(high[...].astype(F32) + jnp.concatenate(rests, axis=0))
            places.append(peer(meta[2], chips, chips - hop, which))
    lanes = values[0].shape[1]
    high, low = (
        jnp.concatenate([ref[pl.ds(pl.multiple_of(place * lanes, lanes), lanes)] for place in places], axis=0)
        for ref in (bd_high, bd_low)
    )
    result = dot3(split(jnp.concatenate(values, axis=1)), (high, low))
    for j in range(parts):
        out[j] = result[:, j * depth : (j + 1) * depth]


def depth_coded(meta, pieces, tables, tests, parts, depth, width, kept, length):
    rows, lanes = pieces[0].shape
    steps = length // 4
    block = rows // steps
    share = width // kept
    specs = [pl.BlockSpec((block, lanes), lambda i: (i, 0))] * 2
    args = list(pieces[:2])
    for piece in pieces[2:]:
        specs.append(pl.BlockSpec((block, lanes), lambda i: (i, 0)))
        specs.append(pl.BlockSpec((block // share, lanes), lambda i: (share * steps + i, 0)))
        args += [piece, piece]
    whole = pl.BlockSpec(tables[0].shape, lambda i: (0, 0))
    return pl.pallas_call(
        functools.partial(depth_coded_kernel, tests, parts, depth, width, kept),
        out_shape=jax.ShapeDtypeStruct((parts, rows, depth), F32),
        grid=(steps,),
        in_specs=[SMEM_SPEC] + specs + [whole, whole],
        out_specs=pl.BlockSpec((parts, block, depth), lambda i: (0, i, 0)),
        compiler_params=pltpu.CompilerParams(vmem_limit_bytes=VMEM_LIMIT),
        cost_estimate=pl.CostEstimate(
            flops=6 * tests * rows * lanes * parts * depth, bytes_accessed=8 * tests * rows * lanes, transcendentals=0
        ),
        name="depth_cells",
    )(meta, *args, *tables)


def on_device(log_k, heads, warm_adjoint, obs_columns, obs_residuals, well_columns):
    rows, ny, depth = log_k.shape
    spaces = lax.axis_size("space")
    tests = lax.axis_size("test")
    rank = lax.axis_index("space")
    test = lax.axis_index("test")
    chips = tests // 2
    width = depth // tests
    parts = depth // width if depth // width == 4 and rows % 4 == 0 else 1
    length = rows // parts
    lanes = depth
    count_x = rows * spaces

    w, h = warm_adjoint[0], heads[0]
    ends = (
        lax.ppermute(
            jnp.concatenate([w[rows - HALO :], log_k[rows - HALO :], h[rows - 1 :]]),
            "space", [(i, i + 1) for i in range(spaces - 1)],
        ),
        lax.ppermute(
            jnp.concatenate([w[:HALO], log_k[:HALO], h[:1]]),
            "space", [(i + 1, i) for i in range(spaces - 1)],
        ),
    )

    meta = jnp.stack([rank * rows, well_columns[0], test, rank]).astype(jnp.int32)

    fields, flats = interior(meta, log_k, w)
    _, _, fields, sums = moments(
        meta, obs_columns[0], obs_residuals[0], ends, fields, flats, rows, ny, count_x
    )
    if spaces <= 8:
        turns = [[(i, (i + k) % spaces) for i in range(spaces)] for k in range(1, spaces)]
        sums = [sums] + [lax.ppermute(sums, "space", turn) for turn in turns]
    else:
        sums = [lax.psum(sums, "space")]

    fields = fields.reshape(3, rows + 2 * HALO, ny + PAD, depth)

    cas_z = cas(depth)
    order = np.argsort(np.minimum(np.arange(depth), depth - np.arange(depth)), kind="stable")
    forward_z = np.zeros((parts, depth, tests, lanes))
    inverse_z = np.zeros((tests, lanes, parts, depth))
    kappa_z = np.zeros((tests, lanes))
    for t in range(tests):
        chosen = order[t::tests]
        for j in range(parts):
            at = slice(j * width, (j + 1) * width)
            forward_z[j, :, t, at] = cas_z[:, chosen]
            inverse_z[t, at, j, :] = cas_z[chosen, :]
            kappa_z[t, at] = kappa(depth)[chosen]
    forward_z = halves(forward_z.reshape(parts * depth, tests * lanes))
    inverse_z = halves(inverse_z.reshape(tests * lanes, parts * depth))
    deep = kappa_z.astype(np.float32)
    across = np.repeat(kappa(ny)[:, None], lanes, axis=1).astype(np.float32)
    cas_y = cas(ny)

    chunks = 2 if (ny // 2) % 48 == 0 else 1
    size = ny // chunks
    other_core = [(i, i ^ 1) for i in range(tests)]
    coded = parts > 1 and length % 4 == 0 and size % 16 == 0
    groups, fars, tables = [], [], []
    for c in range(chunks):
        mine, other = misfit(meta, sums, fields, w, h, ends, forward_z, c * size, size, parts, tests)
        if fars:
            other, fars[-1] = lax.optimization_barrier((other, fars[-1]))
        other = lax.ppermute(other, "test", other_core)
        hops = [[(i, (i + 2 * k) % tests) for i in range(tests)] for k in range(1, chips)]
        if coded:
            total, far = join(mine, other, length, width, width // 4)
            fars += [lax.ppermute(far[k], "test", hop) for k, hop in enumerate(hops)]
            far, *sums = lax.optimization_barrier((far, *sums))
        else:
            summed = mine + other
            total = summed[0]
            for k, hop in enumerate(hops, 1):
                total = total + lax.ppermute(summed[k], "test", hop)
        groups.append(total)
        tables += halves(cas_y[:, c * size : (c + 1) * size])

    local, state, packed = solve(
        meta, across, deep, groups, fars, tables, length, parts, width, width // 4
    )
    if spaces <= 8:
        wide = 0.61**rows > 1e-4
        gathered = [packed]
        for k, turn in enumerate(turns, 1):
            near = wide or k in (1, spaces - 1)
            gathered.append(lax.ppermute(packed if near else packed.astype(BF16), "space", turn))
    else:
        gathered = jnp.take(lax.all_gather(packed, "space"), (rank - jnp.arange(spaces)) % spaces, axis=0)
        gathered = [gathered[k] for k in range(spaces)]
    kept = width // 2 if coded and (ny // tests) % 8 == 0 else 0
    pieces = finish(
        meta, across, deep, local, state, gathered, halves(cas_y), parts, width, kept, tests, 1.0 / (ny * depth)
    )
    if kept:
        arrived = [pieces[0]]
        for k in range(1, tests):
            hop, which = divmod(k, 2)
            turn = [(i, 2 * ((i // 2 + hop) % chips) + (i % 2 + which) % 2) for i in range(tests)]
            arrived.append(lax.ppermute(pieces[k], "test", turn))
        result = depth_coded(meta, arrived, inverse_z, tests, parts, depth, width, kept, length)
    else:
        pieces = pieces[0].reshape(tests, length * (ny // tests), lanes)
        pieces = lax.all_to_all(pieces, "test", split_axis=0, concat_axis=0, tiled=True)
        result = depth_cells(pieces, inverse_z, parts, depth)
    return result.reshape(rows, ny // tests, depth)


def solution(mesh):
    placed = (
        P(("groups", "space"), None, None),
        P("test", ("groups", "space"), None, None),
        P("test", ("groups", "space"), None, None),
        P("test", "groups"),
        P("test", "groups", None),
        P(("groups", "test")),
    )
    return jax.shard_map(
        on_device,
        mesh=mesh,
        in_specs=placed,
        out_specs=P(("groups", "space"), "test", None),
        check_vma=False,
    )
```

```python
import functools

import jax
import jax.numpy as jnp
import ml_dtypes
import numpy as np
from jax import lax
from jax.experimental import pallas as pl
from jax.experimental.pallas import tpu as pltpu
from jax.sharding import PartitionSpec as P

prior_gain = 5.0
range_squared = 4.0

HALO = 3
PAD = 8
F32 = jnp.float32
BF16 = jnp.bfloat16
VMEM_LIMIT = 32 * 1024 * 1024
SMALL_LIMIT = 20 * 1024 * 1024
MISFIT_LIMIT = 40 * 1024 * 1024

SMEM_SPEC = pl.BlockSpec(memory_space=pltpu.SMEM)
VMEM_SPEC = pl.BlockSpec(memory_space=pltpu.VMEM)
ANY_SPEC = pl.BlockSpec(memory_space=pl.ANY)


def in_vmem(array):
    return pltpu.with_memory_space_constraint(array, pltpu.VMEM)


def in_hbm(array):
    return pltpu.with_memory_space_constraint(array, pltpu.HBM)


def cas(length):
    index = np.arange(length)
    angle = 2.0 * np.pi * (index[:, None] * index[None, :] % length) / length
    return np.cos(angle) + np.sin(angle)


def halves(table):
    table = np.asarray(table, np.float32)
    high = table.astype(ml_dtypes.bfloat16)
    low = (table - high.astype(np.float32)).astype(ml_dtypes.bfloat16)
    return high, low


def kappa(length):
    return 4.0 * np.sin(np.pi * np.arange(length) / length) ** 2


def split(value):
    high = value.astype(BF16)
    low = (value - high.astype(F32)).astype(BF16)
    return high, low


def dot(left, right):
    return lax.dot_general(left, right, (((1,), (0,)), ((), ())), preferred_element_type=F32)


def dot3(left, right):
    return dot(left[0], right[0]) + (dot(left[0], right[1]) + dot(left[1], right[0]))


def block_rows(count):
    for rows in (48, 32, 16):
        if count % rows == 0:
            return rows
    return count


def unrolled(start, stop, body, carry, most=4):
    count = stop - start
    factor = next(f for f in range(most, 0, -1) if count % f == 0)
    return lax.fori_loop(start, stop, body, carry, unroll=factor)


def lane_index(shape):
    return lax.broadcasted_iota(jnp.int32, shape, 1)


def window(ref, start, rows):
    return ref.at[pl.ds(pl.multiple_of(start - PAD, 8), rows + 2 * PAD)]


def neighbour_sum(ref, start, rows, plane, fill):
    near = window(ref, start, rows)
    here = near[PAD : PAD + rows]
    lanes = lane_index(here.shape)
    depth = here.shape[1]
    up = jnp.where(lanes == depth - 1, fill, pltpu.roll(here, depth - 1, 1))
    down = jnp.where(lanes == 0, fill, pltpu.roll(here, 1, 1))
    along = ref[pl.ds(pl.multiple_of(start - plane, 8), rows)] + ref[pl.ds(pl.multiple_of(start + plane, 8), rows)]
    across = near[PAD - 1 : PAD - 1 + rows] + near[PAD + 1 : PAD + 1 + rows]
    return along + across + (up + down), here


def fold(value):
    return jnp.sum(value.reshape(-1, 8, value.shape[1]), axis=0)


def field_rows(rows, ny):
    return (rows + 2 * HALO) * (ny + PAD) + PAD


def scale_plane(e_ref, u_ref, p, ny, size, lk_of, w_of):
    base = p * (ny + PAD) + PAD
    for b in range(0, ny, size):
        e = jnp.exp(0.5 * lk_of(b).astype(F32))
        at = pl.ds(pl.multiple_of(base + b, 8), size)
        e_ref[at] = e
        u_ref[at] = e * w_of(b).astype(F32)


def residual_plane(e_ref, u_ref, s_ref, r_ref, v_ref, p, ny, size, valid):
    plane = ny + PAD
    for b in range(0, ny, size):
        start = p * plane + PAD + b
        at = pl.ds(pl.multiple_of(start, 8), size)
        flat = pl.ds(pl.multiple_of(p * ny + b, 8), size)
        s, e = neighbour_sum(e_ref, start, size, plane, 1.0)
        n, u = neighbour_sum(u_ref, start, size, plane, 0.0)
        r = e * n - s * u
        if valid is not None:
            r = r * valid
        s_ref[flat] = s
        r_ref[flat] = r
        v_ref[at] = e * r


def thirds(ref):
    count = ref.shape[0] // 3
    return tuple(ref.at[pl.ds(k * count, count)] for k in range(3))


def halved(ref):
    count = ref.shape[0] // 2
    return tuple(ref.at[pl.ds(k * count, count)] for k in range(2))


def interior_kernel(rows, ny, pieces, meta, lk_in, w_in, fields, flats, lk, w, sems):
    e_ref, u_ref, v_ref = thirds(fields)
    s_ref, r_ref = halved(flats)
    depth = lk.shape[2]
    plane = ny + PAD
    planes = rows + 2 * HALO
    size = block_rows(ny)
    count = rows // pieces
    copies = []
    for piece in range(pieces):
        at = pl.ds(piece * count, count)
        for k, (source, target) in enumerate(((lk_in, lk), (w_in, w))):
            copies.append(pltpu.make_async_copy(source.at[at], target.at[at], sems.at[2 * piece + k]))
    for copy in copies:
        copy.start()
    ones = jnp.ones((PAD, depth), F32)
    zeros = jnp.zeros((PAD, depth), F32)

    def clear(p, carry):
        at = pl.ds(pl.multiple_of(p * plane, 8), PAD)
        e_ref[at] = ones
        u_ref[at] = zeros
        v_ref[at] = zeros
        return carry

    lax.fori_loop(0, planes + 1, clear, 0)

    def scale(x, carry):
        scale_plane(
            e_ref, u_ref, x + HALO, ny, size, lambda b: lk[x, b : b + size], lambda b: w[x, b : b + size]
        )
        return carry

    for piece in range(pieces):
        copies[2 * piece].wait()
        copies[2 * piece + 1].wait()
        unrolled(piece * count, (piece + 1) * count, scale, 0)

    def residual(p, carry):
        residual_plane(e_ref, u_ref, s_ref, r_ref, v_ref, p, ny, size, None)
        return carry

    unrolled(HALO + 1, HALO + rows - 1, residual, 0)


def interior(meta, lk, w):
    rows, ny, depth = lk.shape
    fields = pltpu.VMEM((3 * field_rows(rows, ny), depth), F32)
    flats = pltpu.VMEM((2 * (rows + 2 * HALO) * ny, depth), F32)
    cells = rows * ny * depth
    pieces = next(k for k in (4, 3, 2, 1) if rows % k == 0)
    return pl.pallas_call(
        functools.partial(interior_kernel, rows, ny, pieces),
        out_shape=(fields, flats),
        in_specs=[SMEM_SPEC] + [ANY_SPEC] * 2,
        out_specs=(VMEM_SPEC,) * 2,
        scratch_shapes=[
            pltpu.VMEM((rows, ny, depth), BF16),
            pltpu.VMEM((rows, ny, depth), BF16),
            pltpu.SemaphoreType.DMA((2 * pieces,)),
        ],
        compiler_params=pltpu.CompilerParams(vmem_limit_bytes=SMALL_LIMIT),
        cost_estimate=pl.CostEstimate(flops=5000 * cells, bytes_accessed=4 * cells, transcendentals=cells),
        name="interior",
    )(meta, in_hbm(lk), in_hbm(w))


def moments_kernel(
    rows, ny, count_x,
    meta, columns, residuals, ends_low, ends_high, fields_in, flats_in,
    fields, flats, held_out, mom_out, sems,
):
    e_ref, u_ref, v_ref = thirds(fields)
    s_ref, r_ref = halved(flats)
    holds = [
        pltpu.make_async_copy(ref.at[pl.ds(0, held_out.shape[1])], held_out.at[k], sems.at[k])
        for k, ref in enumerate((e_ref, u_ref, v_ref))
    ]
    depth = residuals.shape[1]
    plane = ny + PAD
    planes = rows + 2 * HALO
    size = block_rows(ny)
    blocks = range(0, ny, size)
    first_row = meta[0]

    for ends, begin in ((ends_low, 0), (ends_high, HALO + rows)):

        def scale(p, carry):
            scale_plane(
                e_ref, u_ref, p + begin, ny, size,
                lambda b: ends[HALO + p, b : b + size], lambda b: ends[p, b : b + size],
            )
            return carry

        unrolled(0, HALO, scale, 0)

    def inside(p):
        row = first_row + p - HALO
        return jnp.where((row >= 0) & (row < count_x), 1.0, 0.0).astype(F32)

    def residual(p, carry):
        residual_plane(e_ref, u_ref, s_ref, r_ref, v_ref, p, ny, size, inside(p))
        return carry

    unrolled(1, HALO + 1, residual, 0)
    unrolled(HALO + rows - 1, planes - 1, residual, 0)

    def plant(o, carry):
        column = columns[o] - (first_row - HALO) * ny

        @pl.when((column >= ny) & (column < (planes - 1) * ny))
        def _():
            p = lax.div(column, ny)
            y = column - p * ny
            at = pl.ds(p * plane + PAD + y, 1)
            flat = pl.ds(p * ny + y, 1)
            added = residuals[pl.ds(o, 1)]
            r_ref[flat] = r_ref[flat] + added
            v_ref[at] = v_ref[at] + e_ref[at] * added

        return carry

    holds[0].start()
    lax.fori_loop(0, columns.shape[0], plant, 0)
    holds[2].start()

    def image(p, sums, valid, summed):
        m0, m1, m2 = sums
        base = p * plane + PAD
        for b in blocks:
            start = base + b
            at = pl.ds(pl.multiple_of(start, 8), size)
            flat = pl.ds(pl.multiple_of(p * ny + b, 8), size)
            n, v = neighbour_sum(v_ref, start, size, plane, 0.0)
            e = e_ref[at]
            y = s_ref[flat] * v - e * n
            if valid is not None:
                y = y * valid
            u_ref[at] = e * y
            if summed:
                r = r_ref[flat]
                m0 = m0 + fold(r * r)
                m1 = m1 + fold(r * y)
                m2 = m2 + fold(y * y)
                r_ref[flat] = y
        return m0, m1, m2

    zero = jnp.zeros((8, depth), F32)
    sums = (zero, zero, zero)
    image(HALO - 1, sums, inside(HALO - 1), False)
    image(HALO + rows, sums, inside(HALO + rows), False)
    m0, m1, m2 = unrolled(HALO, HALO + rows, lambda p, c: image(p, c, None, True), sums)

    holds[1].start()

    def second(p, m3):
        base = p * plane + PAD
        for b in blocks:
            start = base + b
            flat = pl.ds(pl.multiple_of(p * ny + b, 8), size)
            near = window(u_ref, start, size)
            q = near[PAD : PAD + size]
            up = jnp.where(lane_index(q.shape) == depth - 1, 0.0, pltpu.roll(q, depth - 1, 1))
            ahead = u_ref[pl.ds(pl.multiple_of(start + plane, 8), size)] + near[PAD + 1 : PAD + 1 + size] + up
            m3 = m3 + fold(q * (s_ref[flat] * r_ref[flat] - 2.0 * ahead))
        return m3

    m3 = unrolled(HALO, HALO + rows, second, zero)
    for k, m in enumerate((m0, m1, m2, m3)):
        mom_out[k] = jnp.sum(m)
    for hold in holds:
        hold.wait()


def moments(meta, columns, residuals, ends, fields, flats, rows, ny, count_x):
    depth = residuals.shape[1]
    cells = rows * ny * depth
    return pl.pallas_call(
        functools.partial(moments_kernel, rows, ny, count_x),
        out_shape=(
            pltpu.VMEM(fields.shape, F32), pltpu.VMEM(flats.shape, F32),
            jax.ShapeDtypeStruct((3, fields.shape[0] // 3 - PAD, depth), F32), jax.ShapeDtypeStruct((4,), F32),
        ),
        in_specs=[SMEM_SPEC, SMEM_SPEC] + [VMEM_SPEC] * 5,
        out_specs=(VMEM_SPEC,) * 2 + (ANY_SPEC, SMEM_SPEC),
        input_output_aliases={5: 0, 6: 1},
        scratch_shapes=[pltpu.SemaphoreType.DMA((3,))],
        compiler_params=pltpu.CompilerParams(vmem_limit_bytes=SMALL_LIMIT),
        cost_estimate=pl.CostEstimate(flops=5000 * cells, bytes_accessed=4 * cells, transcendentals=cells),
        name="moments",
    )(meta, columns, residuals, *ends, in_vmem(fields), in_vmem(flats))


def step_lengths(sums):
    m0, m1, m2, m3 = (sum(ref[k] for ref in sums) for k in range(4))
    alpha = m0 / m1
    new = alpha * alpha * m2 - 2.0 * alpha * m1 + m0
    bent = 1.0 + new / m0
    second = new / (bent * bent * m1 - 2.0 * bent * alpha * m2 + alpha * alpha * m3)
    return alpha + second * bent, -second * alpha


def misfit_kernel(rows, ny, first, size, parts, tests, terms, meta, *refs):
    sums = refs[:terms]
    (
        fields, w, h, ends_low, ends_high, bd_high, bd_low,
        mine_out, other_out, e_ref, q_ref, v_ref, w_ref, h_bf, a_ref, h_ref, x_ref, t_high, t_low, sems,
    ) = refs[terms:]
    depth = w.shape[2]
    length = rows // parts
    plane = ny + PAD
    slot_rows = size + 2 * PAD
    edge = 16
    low = edge if first > 0 else 0
    high = edge if first + size < ny else 0
    held = PAD + size + (PAD if high else 0)
    cuts = misfit_cuts(length, parts)
    sem = iter(range(sems.shape[0]))
    waits = [[] for _ in cuts[1:]]

    def bring(source, target, group):
        copy = pltpu.make_async_copy(source, target, sems.at[next(sem)])
        copy.start()
        waits[group].append(copy)

    def bring_rows(group, begin, end):
        count = end - begin
        for k, ref in enumerate((e_ref, q_ref, v_ref)):
            bring(
                fields.at[k, pl.ds(begin + HALO - 1, count), pl.ds(first, held)],
                ref.at[pl.ds(begin, count), pl.ds(0, held)],
                group,
            )
        ys, yt = pl.ds(first - low, low + size + high), pl.ds(edge - low, low + size + high)
        for source, below, above, ref in ((w, HALO - 1, 0, w_ref), (h, 2 * HALO, 2 * HALO, h_bf)):
            lo, hi = begin, end
            if lo == 0:
                bring(ends_low.at[pl.ds(below, 1), ys], ref.at[pl.ds(0, 1), yt], group)
                lo = 1
            if hi == rows + 2:
                bring(ends_high.at[pl.ds(above, 1), ys], ref.at[pl.ds(rows + 1, 1), yt], group)
                hi = rows + 1
            if hi > lo:
                bring(source.at[pl.ds(lo - 1, hi - lo), ys], ref.at[pl.ds(lo, hi - lo), yt], group)

    def bring_group(group):
        for part in range(parts):
            end = cuts[group + 1]
            if part == parts - 1 and end == length:
                end = length + 2
            bring_rows(group, part * length + cuts[group], part * length + end)

    for group in range(min(2, len(waits))):
        bring_group(group)
    block = size if size % 16 == 0 else block_rows(size)
    blocks = range(0, size, block)
    first_row, well = meta[0], meta[1]
    c0, c1 = step_lengths(sums)
    lanes_out = mine_out.shape[2]
    chips = tests // 2
    chip, core = meta[2] // 2, meta[2] % 2

    if first + size == ny:
        beyond = jnp.ones((PAD, depth), F32)

        def fill(p, carry):
            e_ref[p, pl.ds(PAD + size, PAD)] = beyond
            return carry

        lax.fori_loop(0, rows + 2, fill, 0)
    zeros = jnp.zeros((PAD, depth), F32)
    for s in range(4 * parts):
        for at in (pl.ds(s * slot_rows, PAD), pl.ds(s * slot_rows + PAD + size, PAD)):
            a_ref[at] = zeros
            h_ref[at] = zeros

    def slot(part, i):
        return (4 * part + lax.rem(i, 4)) * slot_rows

    spans = [(b, block, 0, block) for b in blocks]
    if low:
        spans.append((-edge, edge, PAD, PAD))
    if high:
        spans.append((size, edge, 0, PAD))

    def prepare(part, i):
        base = slot(part, i)
        p = part * length + i
        for y, count, skip, keep in spans:
            at = slice(PAD + y + skip, PAD + y + skip + keep)
            to = pl.ds(pl.multiple_of(base + PAD + y + skip, 8), keep)
            wide = w_ref[p, edge + y : edge + y + count].astype(F32)[skip : skip + keep]
            a_ref[to] = e_ref[p, at] * wide + c0 * v_ref[p, at] + c1 * q_ref[p, at]
            h_ref[to] = h_bf[p, edge + y : edge + y + count].astype(F32)[skip : skip + keep]

    def rows_at(start, count):
        return pl.ds(pl.multiple_of(start, 8), count)

    def along(part):
        for b in blocks:
            at = rows_at(slot(part, 0) + PAD + b, block)
            to = rows_at(slot(part, 1) + PAD + b, block)
            e = e_ref[part * length, PAD + b : PAD + b + block]
            en = e_ref[part * length + 1, PAD + b : PAD + b + block]
            x_ref[part, b : b + block] = (en * a_ref[at] - e * a_ref[to]) * (h_ref[at] - h_ref[to])

    def centre(part, x, buffer):
        here, there = slot(part, x + 1), slot(part, x + 2)
        p = part * length + x + 1
        column = (first_row + part * length + x) * ny + first
        for b in blocks:
            to = rows_at(there + PAD + b, block)
            e_near = e_ref.at[p, b : b + block + 2 * PAD]
            a_near, h_near = (window(ref, here + PAD + b, block) for ref in (a_ref, h_ref))
            mid = slice(PAD, PAD + block)
            e, a, hh = e_near[mid], a_near[mid], h_near[mid]
            en, an, hn = e_ref[p + 1, PAD + b : PAD + b + block], a_ref[to], h_ref[to]
            before = x_ref[part, b : b + block]
            after = (en * a - e * an) * (hh - hn)
            x_ref[part, b : b + block] = after
            total = before + after
            for shift in (-1, 1):
                at = slice(PAD + shift, PAD + shift + block)
                en, an, hn = e_near[at], a_near[at], h_near[at]
                total = total + (en * a - e * an) * (hh - hn)
            lanes = lane_index(e.shape)
            end = lanes == depth - 1
            en = jnp.where(end, 1.0, pltpu.roll(e, depth - 1, 1))
            an = jnp.where(end, 0.0, pltpu.roll(a, depth - 1, 1))
            hn = jnp.where(end, 0.0, pltpu.roll(hh, depth - 1, 1))
            up = (en * a - e * an) * (hh - hn)
            down = jnp.where(lanes == 0, a * hh, pltpu.roll(up, 1, 1))
            total = -0.5 * (total + up + down)
            row = lax.broadcasted_iota(jnp.int32, e.shape, 0) + (column + b)
            total = jnp.where(row == well, 0.0, total)
            high_part, low_part = split(total)
            t_high[buffer, b : b + block, part * depth : (part + 1) * depth] = high_part
            t_low[buffer, b : b + block, part * depth : (part + 1) * depth] = low_part

    def transform(x, buffer):
        value = dot3((t_high[buffer], t_low[buffer]), (bd_high[...], bd_low[...]))
        at = rows_at(x * size, size)
        for c in range(chips):
            even, odd = (value[:, (2 * c + k) * lanes_out : (2 * c + k + 1) * lanes_out] for k in range(2))
            k = lax.rem(c + chips - chip, chips)
            mine_out[k, at] = jnp.where(core == 0, even, odd)
            other_out[k, at] = jnp.where(core == 0, odd, even)

    def step(x):
        for part in range(parts):
            prepare(part, x + 2)
        for part in range(parts):
            centre(part, x, lax.rem(x, 2))

    def loop(x, carry):
        transform(x - 1, lax.rem(x + 1, 2))
        step(x)
        return carry

    done = 0
    for group in range(len(waits)):
        for copy in waits[group]:
            copy.wait()
        if group + 2 < len(waits):
            bring_group(group + 2)
        if group == 0:
            for part in range(parts):
                prepare(part, 0)
                prepare(part, 1)
                along(part)
            step(0)
            done = 1
        ready = length if group == len(waits) - 1 else cuts[group + 1] - 2
        if ready > done:
            lax.fori_loop(done, ready, loop, 0)
            done = ready
    transform(length - 1, (length - 1) % 2)


def misfit_cuts(length, parts):
    if parts == 1 or length <= 4:
        return [0, length]
    return list(range(0, length - 2, 3)) + [length]


def misfit(meta, sums, fields, w, h, ends, tables, first, size, parts, tests):
    rows, ny, depth = w.shape
    length = rows // parts
    lanes = tables[0].shape[1] // tests
    out = jax.ShapeDtypeStruct((tests // 2, length * size, lanes), F32)
    ring = pltpu.VMEM((4 * parts * (size + 2 * PAD), depth), F32)
    full = pltpu.VMEM((rows + 2, size + 2 * PAD, depth), F32)
    half = pltpu.VMEM((rows + 2, size + 32, depth), BF16)
    cells = rows * size * depth
    return pl.pallas_call(
        functools.partial(misfit_kernel, rows, ny, first, size, parts, tests, len(sums)),
        out_shape=(out, out),
        in_specs=[SMEM_SPEC] * (1 + len(sums)) + [ANY_SPEC] * 5 + [VMEM_SPEC] * 2,
        out_specs=(VMEM_SPEC, VMEM_SPEC),
        scratch_shapes=[
            full, full, full, half, half, ring, ring,
            pltpu.VMEM((parts, size, depth), F32),
            pltpu.VMEM((2, size, parts * depth), BF16),
            pltpu.VMEM((2, size, parts * depth), BF16),
            pltpu.SemaphoreType.DMA((5 * parts * (len(misfit_cuts(length, parts)) - 1) + 4,)),
        ],
        compiler_params=pltpu.CompilerParams(vmem_limit_bytes=MISFIT_LIMIT),
        cost_estimate=pl.CostEstimate(flops=8000 * cells, bytes_accessed=4 * cells, transcendentals=cells),
        name="misfit",
    )(meta, *sums, in_hbm(fields), in_hbm(w), in_hbm(h), *(in_hbm(end) for end in ends), *tables)


def pack_rest(rests, width, kept):
    lanes = lane_index(rests[0].shape) % width
    result = rests[0]
    for m in range(1, len(rests)):
        moved = pltpu.roll(rests[m], m * kept, 1)
        result = jnp.where((lanes >= m * kept) & (lanes < (m + 1) * kept), moved, result)
    return result


def unpack_rest(packed, count, width, kept):
    near = lane_index(packed.shape) % width < kept
    depth = packed.shape[1]
    return [
        jnp.where(near, packed if m == 0 else pltpu.roll(packed, depth - m * kept, 1), 0.0) for m in range(count)
    ]


def join_kernel(length, width, kept, mine, other, own_out, far_out):
    far_count, rows = mine.shape[0] - 1, mine.shape[1]
    size = rows // length
    share = width // kept
    block = block_rows(size)

    def add(i, carry):
        at = pl.ds(pl.multiple_of(i * size, 16), size)
        own_out[at] = mine[0, at] + other[0, at]
        return carry

    lax.fori_loop(0, length, add, 0)
    for f in range(far_count):

        def code(i, carry):
            for b in range(0, size, block):
                rests = []
                for m in range(share):
                    at = pl.ds(pl.multiple_of((i * share + m) * size + b, 16), block)
                    value = mine[1 + f, at] + other[1 + f, at]
                    high = value.astype(BF16)
                    far_out[f, at] = high
                    rests.append(value - high.astype(F32))
                at = pl.ds(pl.multiple_of(rows + i * size + b, 16), block)
                far_out[f, at] = pack_rest(rests, width, kept).astype(BF16)
            return carry

        lax.fori_loop(0, length // share, code, 0)


def join(mine, other, length, width, kept):
    chips, rows, lanes = mine.shape
    return pl.pallas_call(
        functools.partial(join_kernel, length, width, kept),
        out_shape=(
            jax.ShapeDtypeStruct((rows, lanes), F32),
            jax.ShapeDtypeStruct((chips - 1, rows + rows * kept // width, lanes), BF16),
        ),
        in_specs=[VMEM_SPEC] * 2,
        out_specs=(VMEM_SPEC,) * 2,
        compiler_params=pltpu.CompilerParams(vmem_limit_bytes=VMEM_LIMIT),
        cost_estimate=pl.CostEstimate(flops=4 * rows * lanes, bytes_accessed=16 * rows * lanes, transcendentals=0),
        name="join",
    )(mine, other)


def power(value, exponent):
    result = None
    while exponent:
        if exponent & 1:
            result = value if result is None else result * value
        exponent >>= 1
        if exponent:
            value = value * value
    return result


def ratio_of(across, deep):
    half = (1.0 + range_squared * (across + deep) + 2.0 * range_squared) / (2.0 * range_squared)
    return 1.0 / (half + jnp.sqrt(half * half - 1.0))


def by_block(values, lanes, width):
    result = values[-1]
    for j in range(len(values) - 2, -1, -1):
        result = jnp.where(lanes < (j + 1) * width, values[j], result)
    return result


def powers(value, length, count):
    step = power(value, length)
    result = [jnp.ones_like(value)]
    for _ in range(count - 1):
        result.append(result[-1] * step)
    return result


def everywhere(value, width):
    lanes = value.shape[1]
    shift = width
    while shift < lanes:
        value = value + pltpu.roll(value, shift, 1)
        shift *= 2
    return value


def solve_kernel(length, parts, width, kept, chunks, fars, meta, across, deep, *refs):
    groups = refs[:chunks]
    far_refs = refs[chunks : chunks * (1 + fars)]
    tables = refs[chunks * (1 + fars) : chunks * (3 + fars)]
    local_out, state_out, packed_out, h_ref = refs[chunks * (3 + fars) :]
    ny, lanes_count = across.shape
    size = groups[0].shape[0] // length
    pair = 2 if length % 2 == 0 else 1
    share = width // kept
    rests = {}

    def gathered(c, x):
        at = slice(x * size, (x + 1) * size)
        value = groups[c][at]
        for f in range(fars):
            ref = far_refs[c * fars + f]
            g = x // share
            if (c, f, g) not in rests:
                start = length * size + g * size
                rests[c, f, g] = unpack_rest(ref[start : start + size].astype(F32), share, width, kept)
            value = value + (ref[at].astype(F32) + rests[c, f, g][x % share])
        return value

    for g in range(0, length, pair):
        total = None
        for c in range(chunks):
            value = jnp.concatenate([gathered(c, g + k) for k in range(pair)], axis=1)
            product = dot3((tables[2 * c][...], tables[2 * c + 1][...]), split(value))
            total = product if total is None else total + product
        for k in range(pair):
            h_ref[g + k] = total[:, k * lanes_count : (k + 1) * lanes_count]

    block = block_rows(ny)
    qz = deep[pl.ds(meta[2], 1)]

    def solve(i, carry):
        at = pl.ds(pl.multiple_of(i * block, 16), block)
        rho = ratio_of(across[at], qz)
        square = rho * rho
        tilt = (1.0 + square) / (1.0 - square)
        p1 = jnp.zeros_like(rho)
        p2 = jnp.zeros_like(rho)
        for x in range(length):
            p2 = rho * (p2 + p1)
            p1 = h_ref[x, at] + rho * p1
            local_out[x, at] = p2 + tilt * p1
        n1 = jnp.zeros_like(rho)
        n2 = jnp.zeros_like(rho)
        for x in range(length - 1, -1, -1):
            local_out[x, at] = local_out[x, at] + (n2 + tilt * n1)
            n1 = rho * (n1 + h_ref[x, at])
            n2 = rho * n2 + n1
        if parts == 1:
            for k, value in enumerate((p1, p2, n1, n2)):
                state_out[k, at] = jnp.zeros_like(rho)
                packed_out[k, at] = value
            return carry
        lanes = lane_index(rho.shape)
        steps = powers(rho, length, parts)
        zero = jnp.zeros_like(rho)
        into = [zero] * 4
        for s in range(1, parts):
            weight = jnp.where(lanes >= s * width, steps[s - 1], 0.0)
            far = float(length * (s - 1))
            one, two = (pltpu.roll(value, s * width, 1) for value in (p1, p2))
            into[0] = into[0] + weight * one
            into[1] = into[1] + weight * (two + far * one)
            weight = jnp.where(lanes < (parts - s) * width, steps[s - 1], 0.0)
            one, two = (pltpu.roll(value, lanes_count - s * width, 1) for value in (n1, n2))
            into[2] = into[2] + weight * one
            into[3] = into[3] + weight * (two + far * one)
        for k in range(4):
            state_out[k, at] = into[k]
        place = lanes // width
        weight = by_block(steps[::-1], lanes, width)
        far = ((parts - 1 - place) * length).astype(F32)
        d1 = everywhere(weight * p1, width)
        d2 = everywhere(weight * (p2 + far * p1), width)
        weight = by_block(steps, lanes, width)
        far = (place * length).astype(F32)
        e1 = everywhere(weight * n1, width)
        e2 = everywhere(weight * (n2 + far * n1), width)
        packed_out[at] = by_block([d1, d2, e1, e2], lanes, width)
        return carry

    lax.fori_loop(0, ny // block, solve, 0)


def solve(meta, across, deep, groups, fars, tables, length, parts, width, kept):
    ny, lanes = across.shape
    chunks = len(groups)
    packed = (ny, lanes) if parts == 4 else (4, ny, lanes)
    cells = length * ny * lanes
    return pl.pallas_call(
        functools.partial(solve_kernel, length, parts, width, kept, chunks, len(fars) // chunks),
        out_shape=(
            jax.ShapeDtypeStruct((length, ny, lanes), F32),
            jax.ShapeDtypeStruct((4, ny, lanes), F32),
            jax.ShapeDtypeStruct(packed, F32),
        ),
        in_specs=[SMEM_SPEC] + [VMEM_SPEC] * (2 + 3 * chunks + len(fars)),
        out_specs=(VMEM_SPEC,) * 3,
        scratch_shapes=[pltpu.VMEM((length, ny, lanes), F32)],
        compiler_params=pltpu.CompilerParams(vmem_limit_bytes=VMEM_LIMIT),
        cost_estimate=pl.CostEstimate(flops=6 * cells * ny, bytes_accessed=16 * cells, transcendentals=0),
        name="solve",
    )(meta, across, deep, *groups, *fars, *tables)


def peer(test, chips, hop, which):
    return 2 * lax.rem(test // 2 + hop, chips) + lax.rem(test % 2 + which, 2)


def finish_kernel(length, parts, width, kept, spaces, tests, scale, meta, across, deep, local, state, *refs):
    packed = refs[:spaces]
    c_high, c_low, *outs = refs[spaces : -4]
    v_ref, v_high, v_low, total_ref = refs[-4:]
    ny, lanes_count = across.shape
    block = block_rows(ny)
    qz = deep[pl.ds(meta[2], 1)]
    slab = length * parts

    def correct(i, carry):
        at = pl.ds(pl.multiple_of(i * block, 16), block)
        rho = ratio_of(across[at], qz)
        square = rho * rho
        tilt = (1.0 + square) / (1.0 - square)
        gain = rho / (2.0 * range_squared * 0.5 * (1.0 - square))
        gain = (prior_gain * scale) * gain * gain
        lanes = lane_index(rho.shape)
        step = power(rho, slab)
        weight = jnp.ones_like(rho)
        if parts > 1:
            near = far = jnp.zeros_like(rho)
            for k in range(1, spaces + 1):
                left = packed[k % spaces][at].astype(F32)
                right = packed[(spaces - k) % spaces][at].astype(F32)
                value = weight * jnp.where(lanes < 2 * width, left, right)
                near = near + value
                far = far + float(slab * (k - 1)) * value
                weight = weight * step

            def pick(value, s):
                return everywhere(jnp.where((lanes >= s * width) & (lanes < (s + 1) * width), value, 0.0), width)

            one, two, far_one = pick(near, 0), pick(near, 1), pick(far, 0)
            back_one, back_two, back_far = pick(near, 2), pick(near, 3), pick(far, 2)
        else:
            one = two = far_one = back_one = back_two = back_far = jnp.zeros_like(rho)
            for k in range(1, spaces + 1):
                left, right = packed[k % spaces], packed[(spaces - k) % spaces]
                first = weight * left[0, at]
                one = one + first
                two = two + weight * left[1, at]
                far_one = far_one + float(slab * (k - 1)) * first
                first = weight * right[2, at]
                back_one = back_one + first
                back_two = back_two + weight * right[3, at]
                back_far = back_far + float(slab * (k - 1)) * first
                weight = weight * step
        around = 1.0 / (1.0 - weight)
        again = float(slab * spaces) * weight * around * around
        two = around * (two + far_one) + again * one
        one = around * one
        back_two = around * (back_two + back_far) + again * back_one
        back_one = around * back_one
        if parts > 1:
            steps = powers(rho, length, parts)
            place = lanes // width
            weight = by_block(steps, lanes, width)
            two = weight * (two + (place * length).astype(F32) * one)
            one = weight * one
            weight = by_block(steps[::-1], lanes, width)
            back_two = weight * (back_two + ((parts - 1 - place) * length).astype(F32) * back_one)
            back_one = weight * back_one
        one = one + state[0, at]
        two = two + state[1, at]
        back_one = back_one + state[2, at]
        back_two = back_two + state[3, at]
        for x in range(length):
            two = rho * (two + one)
            one = rho * one
            v_ref[x, at] = local[x, at] + (two + tilt * one)
        for x in range(length - 1, -1, -1):
            value = gain * (v_ref[x, at] + (back_two + tilt * back_one))
            v_high[x, at], v_low[x, at] = split(value)
            back_one = rho * back_one
            back_two = rho * back_two + back_one
        return carry

    lax.fori_loop(0, ny // block, correct, 0)
    pair = 2 if length % 2 == 0 else 1
    rows = ny // tests
    four = total_ref.shape[0]
    for start in range(0, length, four):
        for g in range(0, four, pair):
            right = tuple(
                jnp.concatenate([ref[start + g + k] for k in range(pair)], axis=1) for ref in (v_high, v_low)
            )
            total = dot3((c_high[...], c_low[...]), right)
            for k in range(pair):
                total_ref[g + k] = total[:, k * lanes_count : (k + 1) * lanes_count]
        if not kept:
            for g in range(four):
                for t in range(tests):
                    outs[0][t, start + g] = total_ref[g, t * rows : (t + 1) * rows]
            continue
        chips = tests // 2
        for hop in range(chips):
            for which in range(2):
                out = outs[2 * hop + which]
                at = pl.ds(pl.multiple_of(peer(meta[2], chips, hop, which) * rows, 8), rows)
                values = [total_ref[g, at] for g in range(four)]
                if hop == 0:
                    for g in range(four):
                        out[(start + g) * rows : (start + g + 1) * rows] = values[g]
                    continue
                highs = [value.astype(BF16).astype(F32) for value in values]
                rests = [value - high for value, high in zip(values, highs)]
                for g in range(0, four, 2):
                    place = (start + g) * rows
                    out[place : place + 2 * rows] = jnp.concatenate(highs[g : g + 2], axis=0).astype(BF16)
                share = width // kept
                packs = [pack_rest(rests[g : g + share], width, kept) for g in range(0, four, share)]
                place = length * rows + start * rows // share
                out[place : place + four * rows // share] = jnp.concatenate(packs, axis=0).astype(BF16)


def finish(meta, across, deep, local, state, packed, tables, parts, width, kept, tests, scale):
    length, ny, lanes = local.shape
    spaces = len(packed)
    cells = length * ny * lanes
    rows = length * (ny // tests)
    if kept:
        out = [jax.ShapeDtypeStruct((rows, lanes), F32)] * 2
        out += [jax.ShapeDtypeStruct((rows + rows * kept // width, lanes), BF16)] * (tests - 2)
    else:
        out = [jax.ShapeDtypeStruct((tests, length, ny // tests, lanes), F32)]
    return pl.pallas_call(
        functools.partial(finish_kernel, length, parts, width, kept, spaces, tests, scale),
        out_shape=tuple(out),
        in_specs=[SMEM_SPEC] + [VMEM_SPEC] * (6 + spaces),
        out_specs=(VMEM_SPEC,) * len(out),
        scratch_shapes=[
            pltpu.VMEM((length, ny, lanes), F32),
            pltpu.VMEM((length, ny, lanes), BF16),
            pltpu.VMEM((length, ny, lanes), BF16),
            pltpu.VMEM((4 if length % 4 == 0 else length, ny, lanes), F32),
        ],
        compiler_params=pltpu.CompilerParams(vmem_limit_bytes=VMEM_LIMIT),
        cost_estimate=pl.CostEstimate(flops=6 * cells * ny, bytes_accessed=16 * cells, transcendentals=0),
        name="finish",
    )(meta, across, deep, local, state, *packed, *tables)


def depth_kernel(tests, parts, depth, pieces, bd_high, bd_low, out):
    rows = pieces.shape[1]
    value = jnp.concatenate([pieces[t] for t in range(tests)], axis=1)
    result = dot3(split(value), (bd_high[...], bd_low[...]))
    for j in range(parts):
        out[j] = result[:, j * depth : (j + 1) * depth]


def depth_cells(pieces, tables, parts, depth):
    tests, rows, lanes = pieces.shape
    steps = 3 if rows % 24 == 0 else 1
    return pl.pallas_call(
        functools.partial(depth_kernel, tests, parts, depth),
        out_shape=jax.ShapeDtypeStruct((parts, rows, depth), F32),
        grid=(steps,),
        in_specs=[
            pl.BlockSpec((tests, rows // steps, lanes), lambda i: (0, i, 0)),
            pl.BlockSpec(tables[0].shape, lambda i: (0, 0)),
            pl.BlockSpec(tables[1].shape, lambda i: (0, 0)),
        ],
        out_specs=pl.BlockSpec((parts, rows // steps, depth), lambda i: (0, i, 0)),
        compiler_params=pltpu.CompilerParams(vmem_limit_bytes=VMEM_LIMIT),
        cost_estimate=pl.CostEstimate(
            flops=6 * tests * rows * lanes * parts * depth, bytes_accessed=8 * tests * rows * lanes, transcendentals=0
        ),
        name="depth_cells",
    )(pieces, *tables)


def depth_coded_kernel(tests, parts, depth, width, kept, meta, *refs):
    out = refs[-1]
    bd_high, bd_low = refs[-3:-1]
    pieces = refs[:-3]
    chips = tests // 2
    share = width // kept
    values, places = [pieces[0][...], pieces[1][...]], [meta[2], peer(meta[2], chips, 0, 1)]
    for hop in range(1, chips):
        for which in range(2):
            k = 2 + 2 * (2 * (hop - 1) + which)
            high, rest = pieces[k], pieces[k + 1]
            rows = high.shape[0] // 4
            packed = rest[...].astype(F32)
            rests = []
            for g in range(4 // share):
                rests += unpack_rest(packed[g * rows : (g + 1) * rows], share, width, kept)
            values.append(high[...].astype(F32) + jnp.concatenate(rests, axis=0))
            places.append(peer(meta[2], chips, chips - hop, which))
    lanes = values[0].shape[1]
    high, low = (
        jnp.concatenate([ref[pl.ds(pl.multiple_of(place * lanes, lanes), lanes)] for place in places], axis=0)
        for ref in (bd_high, bd_low)
    )
    result = dot3(split(jnp.concatenate(values, axis=1)), (high, low))
    for j in range(parts):
        out[j] = result[:, j * depth : (j + 1) * depth]


def depth_coded(meta, pieces, tables, tests, parts, depth, width, kept, length):
    rows, lanes = pieces[0].shape
    steps = length // 4
    block = rows // steps
    share = width // kept
    specs = [pl.BlockSpec((block, lanes), lambda i: (i, 0))] * 2
    args = list(pieces[:2])
    for piece in pieces[2:]:
        specs.append(pl.BlockSpec((block, lanes), lambda i: (i, 0)))
        specs.append(pl.BlockSpec((block // share, lanes), lambda i: (share * steps + i, 0)))
        args += [piece, piece]
    whole = pl.BlockSpec(tables[0].shape, lambda i: (0, 0))
    return pl.pallas_call(
        functools.partial(depth_coded_kernel, tests, parts, depth, width, kept),
        out_shape=jax.ShapeDtypeStruct((parts, rows, depth), F32),
        grid=(steps,),
        in_specs=[SMEM_SPEC] + specs + [whole, whole],
        out_specs=pl.BlockSpec((parts, block, depth), lambda i: (0, i, 0)),
        compiler_params=pltpu.CompilerParams(vmem_limit_bytes=VMEM_LIMIT),
        cost_estimate=pl.CostEstimate(
            flops=6 * tests * rows * lanes * parts * depth, bytes_accessed=8 * tests * rows * lanes, transcendentals=0
        ),
        name="depth_cells",
    )(meta, *args, *tables)


def on_device(log_k, heads, warm_adjoint, obs_columns, obs_residuals, well_columns):
    rows, ny, depth = log_k.shape
    spaces = lax.axis_size("space")
    tests = lax.axis_size("test")
    rank = lax.axis_index("space")
    test = lax.axis_index("test")
    chips = tests // 2
    width = depth // tests
    parts = depth // width if depth // width == 4 and rows % 4 == 0 else 1
    length = rows // parts
    lanes = depth
    count_x = rows * spaces

    w, h = warm_adjoint[0], heads[0]
    ends = (
        lax.ppermute(
            jnp.concatenate([w[rows - HALO :], log_k[rows - HALO :], h[rows - 1 :]]),
            "space", [(i, i + 1) for i in range(spaces - 1)],
        ),
        lax.ppermute(
            jnp.concatenate([w[:HALO], log_k[:HALO], h[:1]]),
            "space", [(i + 1, i) for i in range(spaces - 1)],
        ),
    )

    meta = jnp.stack([rank * rows, well_columns[0], test, rank]).astype(jnp.int32)

    fields, flats = interior(meta, log_k, w)
    _, _, fields, sums = moments(
        meta, obs_columns[0], obs_residuals[0], ends, fields, flats, rows, ny, count_x
    )
    if spaces <= 8:
        turns = [[(i, (i + k) % spaces) for i in range(spaces)] for k in range(1, spaces)]
        sums = [sums] + [lax.ppermute(sums, "space", turn) for turn in turns]
    else:
        sums = [lax.psum(sums, "space")]

    fields = fields.reshape(3, rows + 2 * HALO, ny + PAD, depth)

    cas_z = cas(depth)
    order = np.argsort(np.minimum(np.arange(depth), depth - np.arange(depth)), kind="stable")
    forward_z = np.zeros((parts, depth, tests, lanes))
    inverse_z = np.zeros((tests, lanes, parts, depth))
    kappa_z = np.zeros((tests, lanes))
    for t in range(tests):
        chosen = order[t::tests]
        for j in range(parts):
            at = slice(j * width, (j + 1) * width)
            forward_z[j, :, t, at] = cas_z[:, chosen]
            inverse_z[t, at, j, :] = cas_z[chosen, :]
            kappa_z[t, at] = kappa(depth)[chosen]
    forward_z = halves(forward_z.reshape(parts * depth, tests * lanes))
    inverse_z = halves(inverse_z.reshape(tests * lanes, parts * depth))
    deep = kappa_z.astype(np.float32)
    across = np.repeat(kappa(ny)[:, None], lanes, axis=1).astype(np.float32)
    cas_y = cas(ny)

    chunks = 2 if (ny // 2) % 48 == 0 else 1
    size = ny // chunks
    other_core = [(i, i ^ 1) for i in range(tests)]
    coded = parts > 1 and length % 4 == 0 and size % 16 == 0
    groups, fars, tables = [], [], []
    for c in range(chunks):
        mine, other = misfit(meta, sums, fields, w, h, ends, forward_z, c * size, size, parts, tests)
        if fars:
            other, fars[-1] = lax.optimization_barrier((other, fars[-1]))
        other = lax.ppermute(other, "test", other_core)
        hops = [[(i, (i + 2 * k) % tests) for i in range(tests)] for k in range(1, chips)]
        if coded:
            total, far = join(mine, other, length, width, width // 4)
            fars += [lax.ppermute(far[k], "test", hop) for k, hop in enumerate(hops)]
            far, *sums = lax.optimization_barrier((far, *sums))
        else:
            summed = mine + other
            total = summed[0]
            for k, hop in enumerate(hops, 1):
                total = total + lax.ppermute(summed[k], "test", hop)
        groups.append(total)
        tables += halves(cas_y[:, c * size : (c + 1) * size])

    local, state, packed = solve(
        meta, across, deep, groups, fars, tables, length, parts, width, width // 4
    )
    if spaces <= 8:
        wide = 0.61**rows > 1e-4
        gathered = [packed]
        for k, turn in enumerate(turns, 1):
            near = wide or k in (1, spaces - 1)
            gathered.append(lax.ppermute(packed if near else packed.astype(BF16), "space", turn))
    else:
        gathered = jnp.take(lax.all_gather(packed, "space"), (rank - jnp.arange(spaces)) % spaces, axis=0)
        gathered = [gathered[k] for k in range(spaces)]
    kept = width // 2 if coded and (ny // tests) % 8 == 0 else 0
    pieces = finish(
        meta, across, deep, local, state, gathered, halves(cas_y), parts, width, kept, tests, 1.0 / (ny * depth)
    )
    if kept:
        arrived = [pieces[0]]
        for k in range(1, tests):
            hop, which = divmod(k, 2)
            turn = [(i, 2 * ((i // 2 + hop) % chips) + (i % 2 + which) % 2) for i in range(tests)]
            arrived.append(lax.ppermute(pieces[k], "test", turn))
        result = depth_coded(meta, arrived, inverse_z, tests, parts, depth, width, kept, length)
    else:
        pieces = pieces[0].reshape(tests, length * (ny // tests), lanes)
        pieces = lax.all_to_all(pieces, "test", split_axis=0, concat_axis=0, tiled=True)
        result = depth_cells(pieces, inverse_z, parts, depth)
    return result.reshape(rows, ny // tests, depth)


def solution(mesh):
    placed = (
        P(("groups", "space"), None, None),
        P("test", ("groups", "space"), None, None),
        P("test", ("groups", "space"), None, None),
        P("test", "groups"),
        P("test", "groups", None),
        P(("groups", "test")),
    )
    return jax.shard_map(
        on_device,
        mesh=mesh,
        in_specs=placed,
        out_specs=P(("groups", "space"), "test", None),
        check_vma=False,
    )
```

```python
import functools

import jax
import jax.numpy as jnp
import ml_dtypes
import numpy as np
from jax import lax
from jax.experimental import pallas as pl
from jax.experimental.pallas import tpu as pltpu
from jax.sharding import PartitionSpec as P

prior_gain = 5.0
range_squared = 4.0

HALO = 3
PAD = 8
F32 = jnp.float32
BF16 = jnp.bfloat16
VMEM_LIMIT = 32 * 1024 * 1024
SMALL_LIMIT = 20 * 1024 * 1024
MISFIT_LIMIT = 40 * 1024 * 1024

SMEM_SPEC = pl.BlockSpec(memory_space=pltpu.SMEM)
VMEM_SPEC = pl.BlockSpec(memory_space=pltpu.VMEM)
ANY_SPEC = pl.BlockSpec(memory_space=pl.ANY)


def in_vmem(array):
    return pltpu.with_memory_space_constraint(array, pltpu.VMEM)


def in_hbm(array):
    return pltpu.with_memory_space_constraint(array, pltpu.HBM)


def cas(length):
    index = np.arange(length)
    angle = 2.0 * np.pi * (index[:, None] * index[None, :] % length) / length
    return np.cos(angle) + np.sin(angle)


def halves(table):
    table = np.asarray(table, np.float32)
    high = table.astype(ml_dtypes.bfloat16)
    low = (table - high.astype(np.float32)).astype(ml_dtypes.bfloat16)
    return high, low


def kappa(length):
    return 4.0 * np.sin(np.pi * np.arange(length) / length) ** 2


def split(value):
    high = value.astype(BF16)
    low = (value - high.astype(F32)).astype(BF16)
    return high, low


def dot(left, right):
    return lax.dot_general(left, right, (((1,), (0,)), ((), ())), preferred_element_type=F32)


def dot3(left, right):
    return dot(left[0], right[0]) + (dot(left[0], right[1]) + dot(left[1], right[0]))


def block_rows(count):
    for rows in (48, 32, 16):
        if count % rows == 0:
            return rows
    return count


def unrolled(start, stop, body, carry, most=6):
    factor = min(most, stop - start)
    middle = start + (stop - start) // factor * factor
    carry = lax.fori_loop(start, middle, body, carry, unroll=factor)
    if middle < stop:
        carry = lax.fori_loop(middle, stop, body, carry, unroll=stop - middle)
    return carry


def lane_index(shape):
    return lax.broadcasted_iota(jnp.int32, shape, 1)


def window(ref, start, rows):
    return ref.at[pl.ds(pl.multiple_of(start - PAD, 8), rows + 2 * PAD)]


def neighbour_sum(ref, start, rows, plane, fill):
    near = window(ref, start, rows)
    here = near[PAD : PAD + rows]
    lanes = lane_index(here.shape)
    depth = here.shape[1]
    up = jnp.where(lanes == depth - 1, fill, pltpu.roll(here, depth - 1, 1))
    down = jnp.where(lanes == 0, fill, pltpu.roll(here, 1, 1))
    along = ref[pl.ds(pl.multiple_of(start - plane, 8), rows)] + ref[pl.ds(pl.multiple_of(start + plane, 8), rows)]
    across = near[PAD - 1 : PAD - 1 + rows] + near[PAD + 1 : PAD + 1 + rows]
    return along + across + (up + down), here


def fold(value):
    return jnp.sum(value.reshape(-1, 8, value.shape[1]), axis=0)


def field_rows(rows, ny):
    return (rows + 2 * HALO) * (ny + PAD) + PAD


def scale_plane(e_ref, u_ref, p, ny, size, lk_of, w_of):
    base = p * (ny + PAD) + PAD
    for b in range(0, ny, size):
        e = jnp.exp(0.5 * lk_of(b).astype(F32))
        at = pl.ds(pl.multiple_of(base + b, 8), size)
        e_ref[at] = e
        u_ref[at] = e * w_of(b).astype(F32)


def residual_plane(e_ref, u_ref, s_ref, r_ref, v_ref, p, ny, size, valid):
    plane = ny + PAD
    for b in range(0, ny, size):
        start = p * plane + PAD + b
        at = pl.ds(pl.multiple_of(start, 8), size)
        flat = pl.ds(pl.multiple_of(p * ny + b, 8), size)
        s, e = neighbour_sum(e_ref, start, size, plane, 1.0)
        n, u = neighbour_sum(u_ref, start, size, plane, 0.0)
        r = e * n - s * u
        if valid is not None:
            r = r * valid
        s_ref[flat] = s
        r_ref[flat] = r
        v_ref[at] = e * r


def thirds(ref):
    count = ref.shape[0] // 3
    return tuple(ref.at[pl.ds(k * count, count)] for k in range(3))


def halved(ref):
    count = ref.shape[0] // 2
    return tuple(ref.at[pl.ds(k * count, count)] for k in range(2))


def interior_kernel(rows, ny, pieces, meta, lk_in, w_in, fields, flats, lk, w, sems):
    e_ref, u_ref, v_ref = thirds(fields)
    s_ref, r_ref = halved(flats)
    depth = lk.shape[2]
    plane = ny + PAD
    planes = rows + 2 * HALO
    size = block_rows(ny)
    count = rows // pieces
    copies = []
    for piece in range(pieces):
        at = pl.ds(piece * count, count)
        for k, (source, target) in enumerate(((lk_in, lk), (w_in, w))):
            copies.append(pltpu.make_async_copy(source.at[at], target.at[at], sems.at[2 * piece + k]))
    for copy in copies:
        copy.start()
    ones = jnp.ones((PAD, depth), F32)
    zeros = jnp.zeros((PAD, depth), F32)

    def clear(p, carry):
        at = pl.ds(pl.multiple_of(p * plane, 8), PAD)
        e_ref[at] = ones
        u_ref[at] = zeros
        v_ref[at] = zeros
        return carry

    lax.fori_loop(0, planes + 1, clear, 0)

    def scale(x, carry):
        scale_plane(
            e_ref, u_ref, x + HALO, ny, size, lambda b: lk[x, b : b + size], lambda b: w[x, b : b + size]
        )
        return carry

    for piece in range(pieces):
        copies[2 * piece].wait()
        copies[2 * piece + 1].wait()
        unrolled(piece * count, (piece + 1) * count, scale, 0)

    def residual(p, carry):
        residual_plane(e_ref, u_ref, s_ref, r_ref, v_ref, p, ny, size, None)
        return carry

    unrolled(HALO + 1, HALO + rows - 1, residual, 0)


def interior(meta, lk, w):
    rows, ny, depth = lk.shape
    fields = pltpu.VMEM((3 * field_rows(rows, ny), depth), F32)
    flats = pltpu.VMEM((2 * (rows + 2 * HALO) * ny, depth), F32)
    cells = rows * ny * depth
    pieces = next(k for k in (4, 3, 2, 1) if rows % k == 0)
    return pl.pallas_call(
        functools.partial(interior_kernel, rows, ny, pieces),
        out_shape=(fields, flats),
        in_specs=[SMEM_SPEC] + [ANY_SPEC] * 2,
        out_specs=(VMEM_SPEC,) * 2,
        scratch_shapes=[
            pltpu.VMEM((rows, ny, depth), BF16),
            pltpu.VMEM((rows, ny, depth), BF16),
            pltpu.SemaphoreType.DMA((2 * pieces,)),
        ],
        compiler_params=pltpu.CompilerParams(vmem_limit_bytes=SMALL_LIMIT),
        cost_estimate=pl.CostEstimate(flops=5000 * cells, bytes_accessed=4 * cells, transcendentals=cells),
        name="interior",
    )(meta, in_hbm(lk), in_hbm(w))


def moments_kernel(
    rows, ny, count_x,
    meta, columns, residuals, ends_low, ends_high, fields_in, flats_in,
    fields, flats, held_out, mom_out, sems,
):
    e_ref, u_ref, v_ref = thirds(fields)
    s_ref, r_ref = halved(flats)
    holds = [
        pltpu.make_async_copy(ref.at[pl.ds(0, held_out.shape[1])], held_out.at[k], sems.at[k])
        for k, ref in enumerate((e_ref, u_ref, v_ref))
    ]
    depth = residuals.shape[1]
    plane = ny + PAD
    planes = rows + 2 * HALO
    size = block_rows(ny)
    blocks = range(0, ny, size)
    first_row = meta[0]

    for ends, begin in ((ends_low, 0), (ends_high, HALO + rows)):

        def scale(p, carry):
            scale_plane(
                e_ref, u_ref, p + begin, ny, size,
                lambda b: ends[HALO + p, b : b + size], lambda b: ends[p, b : b + size],
            )
            return carry

        unrolled(0, HALO, scale, 0)

    def inside(p):
        row = first_row + p - HALO
        return jnp.where((row >= 0) & (row < count_x), 1.0, 0.0).astype(F32)

    def residual(p, carry):
        residual_plane(e_ref, u_ref, s_ref, r_ref, v_ref, p, ny, size, inside(p))
        return carry

    unrolled(1, HALO + 1, residual, 0)
    unrolled(HALO + rows - 1, planes - 1, residual, 0)

    def plant(o, carry):
        column = columns[o] - (first_row - HALO) * ny

        @pl.when((column >= ny) & (column < (planes - 1) * ny))
        def _():
            p = lax.div(column, ny)
            y = column - p * ny
            at = pl.ds(p * plane + PAD + y, 1)
            flat = pl.ds(p * ny + y, 1)
            added = residuals[pl.ds(o, 1)]
            r_ref[flat] = r_ref[flat] + added
            v_ref[at] = v_ref[at] + e_ref[at] * added

        return carry

    holds[0].start()
    lax.fori_loop(0, columns.shape[0], plant, 0)
    holds[2].start()

    def image(p, sums, valid, summed):
        m0, m1, m2 = sums
        base = p * plane + PAD
        for b in blocks:
            start = base + b
            at = pl.ds(pl.multiple_of(start, 8), size)
            flat = pl.ds(pl.multiple_of(p * ny + b, 8), size)
            n, v = neighbour_sum(v_ref, start, size, plane, 0.0)
            e = e_ref[at]
            y = s_ref[flat] * v - e * n
            if valid is not None:
                y = y * valid
            u_ref[at] = e * y
            if summed:
                r = r_ref[flat]
                m0 = m0 + fold(r * r)
                m1 = m1 + fold(r * y)
                m2 = m2 + fold(y * y)
                r_ref[flat] = y
        return m0, m1, m2

    zero = jnp.zeros((8, depth), F32)
    sums = (zero, zero, zero)
    image(HALO - 1, sums, inside(HALO - 1), False)
    image(HALO + rows, sums, inside(HALO + rows), False)
    m0, m1, m2 = unrolled(HALO, HALO + rows, lambda p, c: image(p, c, None, True), sums)

    holds[1].start()

    def second(p, m3):
        base = p * plane + PAD
        for b in blocks:
            start = base + b
            flat = pl.ds(pl.multiple_of(p * ny + b, 8), size)
            near = window(u_ref, start, size)
            q = near[PAD : PAD + size]
            up = jnp.where(lane_index(q.shape) == depth - 1, 0.0, pltpu.roll(q, depth - 1, 1))
            ahead = u_ref[pl.ds(pl.multiple_of(start + plane, 8), size)] + near[PAD + 1 : PAD + 1 + size] + up
            m3 = m3 + fold(q * (s_ref[flat] * r_ref[flat] - 2.0 * ahead))
        return m3

    m3 = unrolled(HALO, HALO + rows, second, zero)
    for k, m in enumerate((m0, m1, m2, m3)):
        mom_out[k] = jnp.sum(m)
    for hold in holds:
        hold.wait()


def moments(meta, columns, residuals, ends, fields, flats, rows, ny, count_x):
    depth = residuals.shape[1]
    cells = rows * ny * depth
    return pl.pallas_call(
        functools.partial(moments_kernel, rows, ny, count_x),
        out_shape=(
            pltpu.VMEM(fields.shape, F32), pltpu.VMEM(flats.shape, F32),
            jax.ShapeDtypeStruct((3, fields.shape[0] // 3 - PAD, depth), F32), jax.ShapeDtypeStruct((4,), F32),
        ),
        in_specs=[SMEM_SPEC, SMEM_SPEC] + [VMEM_SPEC] * 5,
        out_specs=(VMEM_SPEC,) * 2 + (ANY_SPEC, SMEM_SPEC),
        input_output_aliases={5: 0, 6: 1},
        scratch_shapes=[pltpu.SemaphoreType.DMA((3,))],
        compiler_params=pltpu.CompilerParams(vmem_limit_bytes=SMALL_LIMIT),
        cost_estimate=pl.CostEstimate(flops=5000 * cells, bytes_accessed=4 * cells, transcendentals=cells),
        name="moments",
    )(meta, columns, residuals, *ends, in_vmem(fields), in_vmem(flats))


def step_lengths(sums):
    m0, m1, m2, m3 = (sum(ref[k] for ref in sums) for k in range(4))
    alpha = m0 / m1
    new = alpha * alpha * m2 - 2.0 * alpha * m1 + m0
    bent = 1.0 + new / m0
    second = new / (bent * bent * m1 - 2.0 * bent * alpha * m2 + alpha * alpha * m3)
    return alpha + second * bent, -second * alpha


def misfit_kernel(rows, ny, first, size, parts, tests, terms, meta, *refs):
    sums = refs[:terms]
    (
        fields, w, h, ends_low, ends_high, bd_high, bd_low,
        mine_out, other_out, e_ref, q_ref, v_ref, w_ref, h_bf, a_ref, h_ref, x_ref, t_high, t_low, sems,
    ) = refs[terms:]
    depth = w.shape[2]
    length = rows // parts
    plane = ny + PAD
    slot_rows = size + 2 * PAD
    edge = 16
    low = edge if first > 0 else 0
    high = edge if first + size < ny else 0
    held = PAD + size + (PAD if high else 0)
    cuts = misfit_cuts(length, parts)
    sem = iter(range(sems.shape[0]))
    waits = [[] for _ in cuts[1:]]

    def bring(source, target, group):
        copy = pltpu.make_async_copy(source, target, sems.at[next(sem)])
        copy.start()
        waits[group].append(copy)

    def bring_rows(group, begin, end):
        count = end - begin
        for k, ref in enumerate((e_ref, q_ref, v_ref)):
            bring(
                fields.at[k, pl.ds(begin + HALO - 1, count), pl.ds(first, held)],
                ref.at[pl.ds(begin, count), pl.ds(0, held)],
                group,
            )
        ys, yt = pl.ds(first - low, low + size + high), pl.ds(edge - low, low + size + high)
        for source, below, above, ref in ((w, HALO - 1, 0, w_ref), (h, 2 * HALO, 2 * HALO, h_bf)):
            lo, hi = begin, end
            if lo == 0:
                bring(ends_low.at[pl.ds(below, 1), ys], ref.at[pl.ds(0, 1), yt], group)
                lo = 1
            if hi == rows + 2:
                bring(ends_high.at[pl.ds(above, 1), ys], ref.at[pl.ds(rows + 1, 1), yt], group)
                hi = rows + 1
            if hi > lo:
                bring(source.at[pl.ds(lo - 1, hi - lo), ys], ref.at[pl.ds(lo, hi - lo), yt], group)

    def bring_group(group):
        for part in range(parts):
            end = cuts[group + 1]
            if part == parts - 1 and end == length:
                end = length + 2
            bring_rows(group, part * length + cuts[group], part * length + end)

    for group in range(min(2, len(waits))):
        bring_group(group)
    block = size if size % 16 == 0 else block_rows(size)
    blocks = range(0, size, block)
    first_row, well = meta[0], meta[1]
    c0, c1 = step_lengths(sums)
    lanes_out = mine_out.shape[2]
    chips = tests // 2
    chip, core = meta[2] // 2, meta[2] % 2

    if first + size == ny:
        beyond = jnp.ones((PAD, depth), F32)

        def fill(p, carry):
            e_ref[p, pl.ds(PAD + size, PAD)] = beyond
            return carry

        lax.fori_loop(0, rows + 2, fill, 0)
    zeros = jnp.zeros((PAD, depth), F32)
    for s in range(4 * parts):
        for at in (pl.ds(s * slot_rows, PAD), pl.ds(s * slot_rows + PAD + size, PAD)):
            a_ref[at] = zeros
            h_ref[at] = zeros

    def slot(part, i):
        return (4 * part + lax.rem(i, 4)) * slot_rows

    spans = [(b, block, 0, block) for b in blocks]
    if low:
        spans.append((-edge, edge, PAD, PAD))
    if high:
        spans.append((size, edge, 0, PAD))

    def prepare(part, i):
        base = slot(part, i)
        p = part * length + i
        for y, count, skip, keep in spans:
            at = slice(PAD + y + skip, PAD + y + skip + keep)
            to = pl.ds(pl.multiple_of(base + PAD + y + skip, 8), keep)
            wide = w_ref[p, edge + y : edge + y + count].astype(F32)[skip : skip + keep]
            a_ref[to] = e_ref[p, at] * wide + c0 * v_ref[p, at] + c1 * q_ref[p, at]
            h_ref[to] = h_bf[p, edge + y : edge + y + count].astype(F32)[skip : skip + keep]

    def rows_at(start, count):
        return pl.ds(pl.multiple_of(start, 8), count)

    def along(part):
        for b in blocks:
            at = rows_at(slot(part, 0) + PAD + b, block)
            to = rows_at(slot(part, 1) + PAD + b, block)
            e = e_ref[part * length, PAD + b : PAD + b + block]
            en = e_ref[part * length + 1, PAD + b : PAD + b + block]
            x_ref[part, b : b + block] = (en * a_ref[at] - e * a_ref[to]) * (h_ref[at] - h_ref[to])

    def centre(part, x, buffer):
        here, there = slot(part, x + 1), slot(part, x + 2)
        p = part * length + x + 1
        column = (first_row + part * length + x) * ny + first
        for b in blocks:
            to = rows_at(there + PAD + b, block)
            e_near = e_ref.at[p, b : b + block + 2 * PAD]
            a_near, h_near = (window(ref, here + PAD + b, block) for ref in (a_ref, h_ref))
            mid = slice(PAD, PAD + block)
            e, a, hh = e_near[mid], a_near[mid], h_near[mid]
            en, an, hn = e_ref[p + 1, PAD + b : PAD + b + block], a_ref[to], h_ref[to]
            before = x_ref[part, b : b + block]
            after = (en * a - e * an) * (hh - hn)
            x_ref[part, b : b + block] = after
            total = before + after
            for shift in (-1, 1):
                at = slice(PAD + shift, PAD + shift + block)
                en, an, hn = e_near[at], a_near[at], h_near[at]
                total = total + (en * a - e * an) * (hh - hn)
            lanes = lane_index(e.shape)
            end = lanes == depth - 1
            en = jnp.where(end, 1.0, pltpu.roll(e, depth - 1, 1))
            an = jnp.where(end, 0.0, pltpu.roll(a, depth - 1, 1))
            hn = jnp.where(end, 0.0, pltpu.roll(hh, depth - 1, 1))
            up = (en * a - e * an) * (hh - hn)
            down = jnp.where(lanes == 0, a * hh, pltpu.roll(up, 1, 1))
            total = -0.5 * (total + up + down)
            row = lax.broadcasted_iota(jnp.int32, e.shape, 0) + (column + b)
            total = jnp.where(row == well, 0.0, total)
            high_part, low_part = split(total)
            t_high[buffer, b : b + block, part * depth : (part + 1) * depth] = high_part
            t_low[buffer, b : b + block, part * depth : (part + 1) * depth] = low_part

    def transform(x, buffer):
        value = dot3((t_high[buffer], t_low[buffer]), (bd_high[...], bd_low[...]))
        at = rows_at(x * size, size)
        for c in range(chips):
            even, odd = (value[:, (2 * c + k) * lanes_out : (2 * c + k + 1) * lanes_out] for k in range(2))
            k = lax.rem(c + chips - chip, chips)
            mine_out[k, at] = jnp.where(core == 0, even, odd)
            other_out[k, at] = jnp.where(core == 0, odd, even)

    def step(x):
        for part in range(parts):
            prepare(part, x + 2)
        for part in range(parts):
            centre(part, x, lax.rem(x, 2))

    def loop(x, carry):
        transform(x - 1, lax.rem(x + 1, 2))
        step(x)
        return carry

    done = 0
    for group in range(len(waits)):
        for copy in waits[group]:
            copy.wait()
        if group + 2 < len(waits):
            bring_group(group + 2)
        if group == 0:
            for part in range(parts):
                prepare(part, 0)
                prepare(part, 1)
                along(part)
            step(0)
            done = 1
        ready = length if group == len(waits) - 1 else cuts[group + 1] - 2
        if ready > done:
            lax.fori_loop(done, ready, loop, 0)
            done = ready
    transform(length - 1, (length - 1) % 2)


def misfit_cuts(length, parts):
    if parts == 1 or length <= 4:
        return [0, length]
    return list(range(0, length - 2, 3)) + [length]


def misfit(meta, sums, fields, w, h, ends, tables, first, size, parts, tests):
    rows, ny, depth = w.shape
    length = rows // parts
    lanes = tables[0].shape[1] // tests
    out = jax.ShapeDtypeStruct((tests // 2, length * size, lanes), F32)
    ring = pltpu.VMEM((4 * parts * (size + 2 * PAD), depth), F32)
    full = pltpu.VMEM((rows + 2, size + 2 * PAD, depth), F32)
    half = pltpu.VMEM((rows + 2, size + 32, depth), BF16)
    cells = rows * size * depth
    return pl.pallas_call(
        functools.partial(misfit_kernel, rows, ny, first, size, parts, tests, len(sums)),
        out_shape=(out, out),
        in_specs=[SMEM_SPEC] * (1 + len(sums)) + [ANY_SPEC] * 5 + [VMEM_SPEC] * 2,
        out_specs=(VMEM_SPEC, VMEM_SPEC),
        scratch_shapes=[
            full, full, full, half, half, ring, ring,
            pltpu.VMEM((parts, size, depth), F32),
            pltpu.VMEM((2, size, parts * depth), BF16),
            pltpu.VMEM((2, size, parts * depth), BF16),
            pltpu.SemaphoreType.DMA((5 * parts * (len(misfit_cuts(length, parts)) - 1) + 4,)),
        ],
        compiler_params=pltpu.CompilerParams(vmem_limit_bytes=MISFIT_LIMIT),
        cost_estimate=pl.CostEstimate(flops=8000 * cells, bytes_accessed=4 * cells, transcendentals=cells),
        name="misfit",
    )(meta, *sums, in_hbm(fields), in_hbm(w), in_hbm(h), *(in_hbm(end) for end in ends), *tables)


def pack_rest(rests, width, kept):
    lanes = lane_index(rests[0].shape) % width
    result = rests[0]
    for m in range(1, len(rests)):
        moved = pltpu.roll(rests[m], m * kept, 1)
        result = jnp.where((lanes >= m * kept) & (lanes < (m + 1) * kept), moved, result)
    return result


def unpack_rest(packed, count, width, kept):
    near = lane_index(packed.shape) % width < kept
    depth = packed.shape[1]
    return [
        jnp.where(near, packed if m == 0 else pltpu.roll(packed, depth - m * kept, 1), 0.0) for m in range(count)
    ]


def join_kernel(length, width, kept, mine, other, own_out, far_out):
    far_count, rows = mine.shape[0] - 1, mine.shape[1]
    size = rows // length
    share = width // kept
    block = block_rows(size)

    def add(i, carry):
        at = pl.ds(pl.multiple_of(i * size, 16), size)
        own_out[at] = mine[0, at] + other[0, at]
        return carry

    lax.fori_loop(0, length, add, 0)
    for f in range(far_count):

        def code(i, carry):
            for b in range(0, size, block):
                rests = []
                for m in range(share):
                    at = pl.ds(pl.multiple_of((i * share + m) * size + b, 16), block)
                    value = mine[1 + f, at] + other[1 + f, at]
                    high = value.astype(BF16)
                    far_out[f, at] = high
                    rests.append(value - high.astype(F32))
                at = pl.ds(pl.multiple_of(rows + i * size + b, 16), block)
                far_out[f, at] = pack_rest(rests, width, kept).astype(BF16)
            return carry

        lax.fori_loop(0, length // share, code, 0)


def join(mine, other, length, width, kept):
    chips, rows, lanes = mine.shape
    return pl.pallas_call(
        functools.partial(join_kernel, length, width, kept),
        out_shape=(
            jax.ShapeDtypeStruct((rows, lanes), F32),
            jax.ShapeDtypeStruct((chips - 1, rows + rows * kept // width, lanes), BF16),
        ),
        in_specs=[VMEM_SPEC] * 2,
        out_specs=(VMEM_SPEC,) * 2,
        compiler_params=pltpu.CompilerParams(vmem_limit_bytes=VMEM_LIMIT),
        cost_estimate=pl.CostEstimate(flops=4 * rows * lanes, bytes_accessed=16 * rows * lanes, transcendentals=0),
        name="join",
    )(mine, other)


def power(value, exponent):
    result = None
    while exponent:
        if exponent & 1:
            result = value if result is None else result * value
        exponent >>= 1
        if exponent:
            value = value * value
    return result


def ratio_of(across, deep):
    half = (1.0 + range_squared * (across + deep) + 2.0 * range_squared) / (2.0 * range_squared)
    return 1.0 / (half + jnp.sqrt(half * half - 1.0))


def by_block(values, lanes, width):
    result = values[-1]
    for j in range(len(values) - 2, -1, -1):
        result = jnp.where(lanes < (j + 1) * width, values[j], result)
    return result


def powers(value, length, count):
    step = power(value, length)
    result = [jnp.ones_like(value)]
    for _ in range(count - 1):
        result.append(result[-1] * step)
    return result


def everywhere(value, width):
    lanes = value.shape[1]
    shift = width
    while shift < lanes:
        value = value + pltpu.roll(value, shift, 1)
        shift *= 2
    return value


def solve_kernel(length, parts, width, kept, chunks, fars, meta, across, deep, *refs):
    groups = refs[:chunks]
    far_refs = refs[chunks : chunks * (1 + fars)]
    tables = refs[chunks * (1 + fars) : chunks * (3 + fars)]
    local_out, state_out, packed_out, h_ref = refs[chunks * (3 + fars) :]
    ny, lanes_count = across.shape
    size = groups[0].shape[0] // length
    pair = 2 if length % 2 == 0 else 1
    share = width // kept
    rests = {}

    def gathered(c, x):
        at = slice(x * size, (x + 1) * size)
        value = groups[c][at]
        for f in range(fars):
            ref = far_refs[c * fars + f]
            g = x // share
            if (c, f, g) not in rests:
                start = length * size + g * size
                rests[c, f, g] = unpack_rest(ref[start : start + size].astype(F32), share, width, kept)
            value = value + (ref[at].astype(F32) + rests[c, f, g][x % share])
        return value

    for g in range(0, length, pair):
        total = None
        for c in range(chunks):
            value = jnp.concatenate([gathered(c, g + k) for k in range(pair)], axis=1)
            product = dot3((tables[2 * c][...], tables[2 * c + 1][...]), split(value))
            total = product if total is None else total + product
        for k in range(pair):
            h_ref[g + k] = total[:, k * lanes_count : (k + 1) * lanes_count]

    block = block_rows(ny)
    qz = deep[pl.ds(meta[2], 1)]

    def solve(i, carry):
        at = pl.ds(pl.multiple_of(i * block, 16), block)
        rho = ratio_of(across[at], qz)
        square = rho * rho
        tilt = (1.0 + square) / (1.0 - square)
        p1 = jnp.zeros_like(rho)
        p2 = jnp.zeros_like(rho)
        for x in range(length):
            p2 = rho * (p2 + p1)
            p1 = h_ref[x, at] + rho * p1
            local_out[x, at] = p2 + tilt * p1
        n1 = jnp.zeros_like(rho)
        n2 = jnp.zeros_like(rho)
        for x in range(length - 1, -1, -1):
            local_out[x, at] = local_out[x, at] + (n2 + tilt * n1)
            n1 = rho * (n1 + h_ref[x, at])
            n2 = rho * n2 + n1
        if parts == 1:
            for k, value in enumerate((p1, p2, n1, n2)):
                state_out[k, at] = jnp.zeros_like(rho)
                packed_out[k, at] = value
            return carry
        lanes = lane_index(rho.shape)
        steps = powers(rho, length, parts)
        zero = jnp.zeros_like(rho)
        into = [zero] * 4
        for s in range(1, parts):
            weight = jnp.where(lanes >= s * width, steps[s - 1], 0.0)
            far = float(length * (s - 1))
            one, two = (pltpu.roll(value, s * width, 1) for value in (p1, p2))
            into[0] = into[0] + weight * one
            into[1] = into[1] + weight * (two + far * one)
            weight = jnp.where(lanes < (parts - s) * width, steps[s - 1], 0.0)
            one, two = (pltpu.roll(value, lanes_count - s * width, 1) for value in (n1, n2))
            into[2] = into[2] + weight * one
            into[3] = into[3] + weight * (two + far * one)
        for k in range(4):
            state_out[k, at] = into[k]
        place = lanes // width
        weight = by_block(steps[::-1], lanes, width)
        far = ((parts - 1 - place) * length).astype(F32)
        d1 = everywhere(weight * p1, width)
        d2 = everywhere(weight * (p2 + far * p1), width)
        weight = by_block(steps, lanes, width)
        far = (place * length).astype(F32)
        e1 = everywhere(weight * n1, width)
        e2 = everywhere(weight * (n2 + far * n1), width)
        packed_out[at] = by_block([d1, d2, e1, e2], lanes, width)
        return carry

    lax.fori_loop(0, ny // block, solve, 0)


def solve(meta, across, deep, groups, fars, tables, length, parts, width, kept):
    ny, lanes = across.shape
    chunks = len(groups)
    packed = (ny, lanes) if parts == 4 else (4, ny, lanes)
    cells = length * ny * lanes
    return pl.pallas_call(
        functools.partial(solve_kernel, length, parts, width, kept, chunks, len(fars) // chunks),
        out_shape=(
            jax.ShapeDtypeStruct((length, ny, lanes), F32),
            jax.ShapeDtypeStruct((4, ny, lanes), F32),
            jax.ShapeDtypeStruct(packed, F32),
        ),
        in_specs=[SMEM_SPEC] + [VMEM_SPEC] * (2 + 3 * chunks + len(fars)),
        out_specs=(VMEM_SPEC,) * 3,
        scratch_shapes=[pltpu.VMEM((length, ny, lanes), F32)],
        compiler_params=pltpu.CompilerParams(vmem_limit_bytes=VMEM_LIMIT),
        cost_estimate=pl.CostEstimate(flops=6 * cells * ny, bytes_accessed=16 * cells, transcendentals=0),
        name="solve",
    )(meta, across, deep, *groups, *fars, *tables)


def peer(test, chips, hop, which):
    return 2 * lax.rem(test // 2 + hop, chips) + lax.rem(test % 2 + which, 2)


def finish_kernel(length, parts, width, kept, spaces, tests, scale, meta, across, deep, local, state, *refs):
    packed = refs[:spaces]
    c_high, c_low, *outs = refs[spaces : -4]
    v_ref, v_high, v_low, total_ref = refs[-4:]
    ny, lanes_count = across.shape
    block = block_rows(ny)
    qz = deep[pl.ds(meta[2], 1)]
    slab = length * parts

    def correct(i, carry):
        at = pl.ds(pl.multiple_of(i * block, 16), block)
        rho = ratio_of(across[at], qz)
        square = rho * rho
        tilt = (1.0 + square) / (1.0 - square)
        gain = rho / (2.0 * range_squared * 0.5 * (1.0 - square))
        gain = (prior_gain * scale) * gain * gain
        lanes = lane_index(rho.shape)
        step = power(rho, slab)
        weight = jnp.ones_like(rho)
        if parts > 1:
            near = far = jnp.zeros_like(rho)
            for k in range(1, spaces + 1):
                left = packed[k % spaces][at].astype(F32)
                right = packed[(spaces - k) % spaces][at].astype(F32)
                value = weight * jnp.where(lanes < 2 * width, left, right)
                near = near + value
                far = far + float(slab * (k - 1)) * value
                weight = weight * step

            def pick(value, s):
                return everywhere(jnp.where((lanes >= s * width) & (lanes < (s + 1) * width), value, 0.0), width)

            one, two, far_one = pick(near, 0), pick(near, 1), pick(far, 0)
            back_one, back_two, back_far = pick(near, 2), pick(near, 3), pick(far, 2)
        else:
            one = two = far_one = back_one = back_two = back_far = jnp.zeros_like(rho)
            for k in range(1, spaces + 1):
                left, right = packed[k % spaces], packed[(spaces - k) % spaces]
                first = weight * left[0, at]
                one = one + first
                two = two + weight * left[1, at]
                far_one = far_one + float(slab * (k - 1)) * first
                first = weight * right[2, at]
                back_one = back_one + first
                back_two = back_two + weight * right[3, at]
                back_far = back_far + float(slab * (k - 1)) * first
                weight = weight * step
        around = 1.0 / (1.0 - weight)
        again = float(slab * spaces) * weight * around * around
        two = around * (two + far_one) + again * one
        one = around * one
        back_two = around * (back_two + back_far) + again * back_one
        back_one = around * back_one
        if parts > 1:
            steps = powers(rho, length, parts)
            place = lanes // width
            weight = by_block(steps, lanes, width)
            two = weight * (two + (place * length).astype(F32) * one)
            one = weight * one
            weight = by_block(steps[::-1], lanes, width)
            back_two = weight * (back_two + ((parts - 1 - place) * length).astype(F32) * back_one)
            back_one = weight * back_one
        one = one + state[0, at]
        two = two + state[1, at]
        back_one = back_one + state[2, at]
        back_two = back_two + state[3, at]
        for x in range(length):
            two = rho * (two + one)
            one = rho * one
            v_ref[x, at] = local[x, at] + (two + tilt * one)
        for x in range(length - 1, -1, -1):
            value = gain * (v_ref[x, at] + (back_two + tilt * back_one))
            v_high[x, at], v_low[x, at] = split(value)
            back_one = rho * back_one
            back_two = rho * back_two + back_one
        return carry

    lax.fori_loop(0, ny // block, correct, 0)
    pair = 2 if length % 2 == 0 else 1
    rows = ny // tests
    four = total_ref.shape[0]
    for start in range(0, length, four):
        for g in range(0, four, pair):
            right = tuple(
                jnp.concatenate([ref[start + g + k] for k in range(pair)], axis=1) for ref in (v_high, v_low)
            )
            total = dot3((c_high[...], c_low[...]), right)
            for k in range(pair):
                total_ref[g + k] = total[:, k * lanes_count : (k + 1) * lanes_count]
        if not kept:
            for g in range(four):
                for t in range(tests):
                    outs[0][t, start + g] = total_ref[g, t * rows : (t + 1) * rows]
            continue
        chips = tests // 2
        for hop in range(chips):
            for which in range(2):
                out = outs[2 * hop + which]
                at = pl.ds(pl.multiple_of(peer(meta[2], chips, hop, which) * rows, 8), rows)
                values = [total_ref[g, at] for g in range(four)]
                if hop == 0:
                    for g in range(four):
                        out[(start + g) * rows : (start + g + 1) * rows] = values[g]
                    continue
                highs = [value.astype(BF16).astype(F32) for value in values]
                rests = [value - high for value, high in zip(values, highs)]
                for g in range(0, four, 2):
                    place = (start + g) * rows
                    out[place : place + 2 * rows] = jnp.concatenate(highs[g : g + 2], axis=0).astype(BF16)
                share = width // kept
                packs = [pack_rest(rests[g : g + share], width, kept) for g in range(0, four, share)]
                place = length * rows + start * rows // share
                out[place : place + four * rows // share] = jnp.concatenate(packs, axis=0).astype(BF16)


def finish(meta, across, deep, local, state, packed, tables, parts, width, kept, tests, scale):
    length, ny, lanes = local.shape
    spaces = len(packed)
    cells = length * ny * lanes
    rows = length * (ny // tests)
    if kept:
        out = [jax.ShapeDtypeStruct((rows, lanes), F32)] * 2
        out += [jax.ShapeDtypeStruct((rows + rows * kept // width, lanes), BF16)] * (tests - 2)
    else:
        out = [jax.ShapeDtypeStruct((tests, length, ny // tests, lanes), F32)]
    return pl.pallas_call(
        functools.partial(finish_kernel, length, parts, width, kept, spaces, tests, scale),
        out_shape=tuple(out),
        in_specs=[SMEM_SPEC] + [VMEM_SPEC] * (6 + spaces),
        out_specs=(VMEM_SPEC,) * len(out),
        scratch_shapes=[
            pltpu.VMEM((length, ny, lanes), F32),
            pltpu.VMEM((length, ny, lanes), BF16),
            pltpu.VMEM((length, ny, lanes), BF16),
            pltpu.VMEM((4 if length % 4 == 0 else length, ny, lanes), F32),
        ],
        compiler_params=pltpu.CompilerParams(vmem_limit_bytes=VMEM_LIMIT),
        cost_estimate=pl.CostEstimate(flops=6 * cells * ny, bytes_accessed=16 * cells, transcendentals=0),
        name="finish",
    )(meta, across, deep, local, state, *packed, *tables)


def depth_kernel(tests, parts, depth, pieces, bd_high, bd_low, out):
    rows = pieces.shape[1]
    value = jnp.concatenate([pieces[t] for t in range(tests)], axis=1)
    result = dot3(split(value), (bd_high[...], bd_low[...]))
    for j in range(parts):
        out[j] = result[:, j * depth : (j + 1) * depth]


def depth_cells(pieces, tables, parts, depth):
    tests, rows, lanes = pieces.shape
    steps = 3 if rows % 24 == 0 else 1
    return pl.pallas_call(
        functools.partial(depth_kernel, tests, parts, depth),
        out_shape=jax.ShapeDtypeStruct((parts, rows, depth), F32),
        grid=(steps,),
        in_specs=[
            pl.BlockSpec((tests, rows // steps, lanes), lambda i: (0, i, 0)),
            pl.BlockSpec(tables[0].shape, lambda i: (0, 0)),
            pl.BlockSpec(tables[1].shape, lambda i: (0, 0)),
        ],
        out_specs=pl.BlockSpec((parts, rows // steps, depth), lambda i: (0, i, 0)),
        compiler_params=pltpu.CompilerParams(vmem_limit_bytes=VMEM_LIMIT),
        cost_estimate=pl.CostEstimate(
            flops=6 * tests * rows * lanes * parts * depth, bytes_accessed=8 * tests * rows * lanes, transcendentals=0
        ),
        name="depth_cells",
    )(pieces, *tables)


def depth_coded_kernel(tests, parts, depth, width, kept, meta, *refs):
    out = refs[-1]
    bd_high, bd_low = refs[-3:-1]
    pieces = refs[:-3]
    chips = tests // 2
    share = width // kept
    values, places = [pieces[0][...], pieces[1][...]], [meta[2], peer(meta[2], chips, 0, 1)]
    for hop in range(1, chips):
        for which in range(2):
            k = 2 + 2 * (2 * (hop - 1) + which)
            high, rest = pieces[k], pieces[k + 1]
            rows = high.shape[0] // 4
            packed = rest[...].astype(F32)
            rests = []
            for g in range(4 // share):
                rests += unpack_rest(packed[g * rows : (g + 1) * rows], share, width, kept)
            values.append(high[...].astype(F32) + jnp.concatenate(rests, axis=0))
            places.append(peer(meta[2], chips, chips - hop, which))
    lanes = values[0].shape[1]
    high, low = (
        jnp.concatenate([ref[pl.ds(pl.multiple_of(place * lanes, lanes), lanes)] for place in places], axis=0)
        for ref in (bd_high, bd_low)
    )
    result = dot3(split(jnp.concatenate(values, axis=1)), (high, low))
    for j in range(parts):
        out[j] = result[:, j * depth : (j + 1) * depth]


def depth_coded(meta, pieces, tables, tests, parts, depth, width, kept, length):
    rows, lanes = pieces[0].shape
    steps = length // 4
    block = rows // steps
    share = width // kept
    specs = [pl.BlockSpec((block, lanes), lambda i: (i, 0))] * 2
    args = list(pieces[:2])
    for piece in pieces[2:]:
        specs.append(pl.BlockSpec((block, lanes), lambda i: (i, 0)))
        specs.append(pl.BlockSpec((block // share, lanes), lambda i: (share * steps + i, 0)))
        args += [piece, piece]
    whole = pl.BlockSpec(tables[0].shape, lambda i: (0, 0))
    return pl.pallas_call(
        functools.partial(depth_coded_kernel, tests, parts, depth, width, kept),
        out_shape=jax.ShapeDtypeStruct((parts, rows, depth), F32),
        grid=(steps,),
        in_specs=[SMEM_SPEC] + specs + [whole, whole],
        out_specs=pl.BlockSpec((parts, block, depth), lambda i: (0, i, 0)),
        compiler_params=pltpu.CompilerParams(vmem_limit_bytes=VMEM_LIMIT),
        cost_estimate=pl.CostEstimate(
            flops=6 * tests * rows * lanes * parts * depth, bytes_accessed=8 * tests * rows * lanes, transcendentals=0
        ),
        name="depth_cells",
    )(meta, *args, *tables)


def on_device(log_k, heads, warm_adjoint, obs_columns, obs_residuals, well_columns):
    rows, ny, depth = log_k.shape
    spaces = lax.axis_size("space")
    tests = lax.axis_size("test")
    rank = lax.axis_index("space")
    test = lax.axis_index("test")
    chips = tests // 2
    width = depth // tests
    parts = depth // width if depth // width == 4 and rows % 4 == 0 else 1
    length = rows // parts
    lanes = depth
    count_x = rows * spaces

    w, h = warm_adjoint[0], heads[0]
    ends = (
        lax.ppermute(
            jnp.concatenate([w[rows - HALO :], log_k[rows - HALO :], h[rows - 1 :]]),
            "space", [(i, i + 1) for i in range(spaces - 1)],
        ),
        lax.ppermute(
            jnp.concatenate([w[:HALO], log_k[:HALO], h[:1]]),
            "space", [(i + 1, i) for i in range(spaces - 1)],
        ),
    )

    meta = jnp.stack([rank * rows, well_columns[0], test, rank]).astype(jnp.int32)

    fields, flats = interior(meta, log_k, w)
    _, _, fields, sums = moments(
        meta, obs_columns[0], obs_residuals[0], ends, fields, flats, rows, ny, count_x
    )
    if spaces <= 8:
        turns = [[(i, (i + k) % spaces) for i in range(spaces)] for k in range(1, spaces)]
        sums = [sums] + [lax.ppermute(sums, "space", turn) for turn in turns]
    else:
        sums = [lax.psum(sums, "space")]

    fields = fields.reshape(3, rows + 2 * HALO, ny + PAD, depth)

    cas_z = cas(depth)
    order = np.argsort(np.minimum(np.arange(depth), depth - np.arange(depth)), kind="stable")
    forward_z = np.zeros((parts, depth, tests, lanes))
    inverse_z = np.zeros((tests, lanes, parts, depth))
    kappa_z = np.zeros((tests, lanes))
    for t in range(tests):
        chosen = order[t::tests]
        for j in range(parts):
            at = slice(j * width, (j + 1) * width)
            forward_z[j, :, t, at] = cas_z[:, chosen]
            inverse_z[t, at, j, :] = cas_z[chosen, :]
            kappa_z[t, at] = kappa(depth)[chosen]
    forward_z = halves(forward_z.reshape(parts * depth, tests * lanes))
    inverse_z = halves(inverse_z.reshape(tests * lanes, parts * depth))
    deep = kappa_z.astype(np.float32)
    across = np.repeat(kappa(ny)[:, None], lanes, axis=1).astype(np.float32)
    cas_y = cas(ny)

    chunks = 2 if (ny // 2) % 48 == 0 else 1
    size = ny // chunks
    other_core = [(i, i ^ 1) for i in range(tests)]
    coded = parts > 1 and length % 4 == 0 and size % 16 == 0
    groups, fars, tables = [], [], []
    for c in range(chunks):
        mine, other = misfit(meta, sums, fields, w, h, ends, forward_z, c * size, size, parts, tests)
        if fars:
            other, fars[-1] = lax.optimization_barrier((other, fars[-1]))
        other = lax.ppermute(other, "test", other_core)
        hops = [[(i, (i + 2 * k) % tests) for i in range(tests)] for k in range(1, chips)]
        if coded:
            total, far = join(mine, other, length, width, width // 4)
            fars += [lax.ppermute(far[k], "test", hop) for k, hop in enumerate(hops)]
            far, *sums = lax.optimization_barrier((far, *sums))
        else:
            summed = mine + other
            total = summed[0]
            for k, hop in enumerate(hops, 1):
                total = total + lax.ppermute(summed[k], "test", hop)
        groups.append(total)
        tables += halves(cas_y[:, c * size : (c + 1) * size])

    local, state, packed = solve(
        meta, across, deep, groups, fars, tables, length, parts, width, width // 4
    )
    if spaces <= 8:
        wide = 0.61**rows > 1e-4
        gathered = [packed]
        for k, turn in enumerate(turns, 1):
            near = wide or k in (1, spaces - 1)
            gathered.append(lax.ppermute(packed if near else packed.astype(BF16), "space", turn))
    else:
        gathered = jnp.take(lax.all_gather(packed, "space"), (rank - jnp.arange(spaces)) % spaces, axis=0)
        gathered = [gathered[k] for k in range(spaces)]
    kept = width // 2 if coded and (ny // tests) % 8 == 0 else 0
    pieces = finish(
        meta, across, deep, local, state, gathered, halves(cas_y), parts, width, kept, tests, 1.0 / (ny * depth)
    )
    if kept:
        arrived = [pieces[0]]
        for k in range(1, tests):
            hop, which = divmod(k, 2)
            turn = [(i, 2 * ((i // 2 + hop) % chips) + (i % 2 + which) % 2) for i in range(tests)]
            arrived.append(lax.ppermute(pieces[k], "test", turn))
        result = depth_coded(meta, arrived, inverse_z, tests, parts, depth, width, kept, length)
    else:
        pieces = pieces[0].reshape(tests, length * (ny // tests), lanes)
        pieces = lax.all_to_all(pieces, "test", split_axis=0, concat_axis=0, tiled=True)
        result = depth_cells(pieces, inverse_z, parts, depth)
    return result.reshape(rows, ny // tests, depth)


def solution(mesh):
    placed = (
        P(("groups", "space"), None, None),
        P("test", ("groups", "space"), None, None),
        P("test", ("groups", "space"), None, None),
        P("test", "groups"),
        P("test", "groups", None),
        P(("groups", "test")),
    )
    return jax.shard_map(
        on_device,
        mesh=mesh,
        in_specs=placed,
        out_specs=P(("groups", "space"), "test", None),
        check_vma=False,
    )
```
